512 devices in a mesh: blk: 16 (over y, x_hi), rep: 32 (over x_lo, z, core).
Axes of the slice: x: 4 (x_hi: 2, x_lo: 2; x = x_hi * 2 + x_lo), y: 8, z: 8, core: 2. Of those that a mesh axis runs over, the one named last changes fastest.
Arguments:
- features: bfloat16 [131072, 2048], P(('rep', 'blk'))
- head_weight: bfloat16 [2048, 512], replicated, may hold values from -0.125 to 0.125
- partner: int32 [131072], P(('rep', 'blk')), may hold values from 0 to 4095, as said below
Outputs:
- update: float32 [2048, 512], P('blk')
The draws below stay inside these ranges and needn't reach their ends.
Inputs may be any that keep to these rules, and one draw needn't show every extreme that they name: partner pairs the images of each replica group: partner[partner[i]] = i and partner[i] != i, indices counted from the group's first image.
All inputs are finite; a program needn't handle non-finite values.
Results may differ from the reference program's by a relative error of at most 0.004.
Values may be sent and summed in bfloat16 or wider, within the bound.
No kernel may reach another device: no remote copies, remote signals or barrier semaphores. Data moves between devices by JAX's collectives and lax.ppermute only.
A program may use at most 64 MiB of HBM per device.

```python
import jax
import jax.numpy as jnp
from jax import lax

C = 2048
D = 512
GROUP = 4096
IMAGES = 131072
N_REP = 32


def pair_up(leading, trailing):
    return jnp.zeros((GROUP,), jnp.int32).at[leading].set(trailing).at[trailing].set(leading)


def pair_layout(key):
    group_keys = jax.random.split(key, N_REP)
    orders = jax.vmap(lambda sub_key: jax.random.permutation(sub_key, GROUP))(group_keys)
    return jax.vmap(pair_up)(orders[:, 0::2], orders[:, 1::2])


def draw_partner(key, part):
    layout = pair_layout(key)
    return layout.reshape(-1).astype(jnp.int32)


def draw_features(key, part):
    layout = pair_layout(key)
    key = jax.random.fold_in(key, 5)
    key_base, key_noise, key_cols, key_matrix_rows = jax.random.split(key, 4)
    within = jnp.arange(GROUP, dtype=jnp.int32)
    anchor = (jnp.minimum(within[None, :], layout) + GROUP * jnp.arange(N_REP, dtype=jnp.int32)[:, None]).reshape(-1)
    base = jax.random.normal(key_base, (IMAGES, C), jnp.float32)
    noise = jax.random.normal(key_noise, (IMAGES, C), jnp.float32)
    mixed = 0.6 * base[anchor] + 0.8 * noise
    column_scale = 10.0 ** (jnp.arange(C, dtype=jnp.float32) / C - 0.5)
    column_scale = column_scale * jnp.exp(jax.random.uniform(key_cols, (C,), jnp.float32, -0.35, 0.35))
    row_scale = jnp.exp(jax.random.uniform(key_matrix_rows, (IMAGES, 1), jnp.float32, -1.15, 1.15))
    return (mixed * column_scale[None, :] * row_scale).astype(jnp.bfloat16)


def bell_draw(rng, shape, deviation, most, kind=jnp.bfloat16):
    return jnp.clip(deviation * jax.random.normal(rng, shape, jnp.float32), -most, most).astype(kind)


def setup_inputs(seed: int = 0) -> dict:
    keys = jax.random.split(jax.random.key(seed), 4)
    features = draw_features(jax.random.fold_in(keys[3], 71), 0)
    head_weight = bell_draw(keys[1], (C, D), C ** -0.5, 0.125)
    partner = draw_partner(jax.random.fold_in(keys[3], 71), 0)
    return {"features": features, "head_weight": head_weight, "partner": partner}


softness_factor = 0.05

def group_gradient(features, head_weight, partner):
    hidden = jnp.dot(features, head_weight, preferred_element_type=jnp.float32)
    row_norm = jnp.sqrt(lax.optimization_barrier(jnp.sum(hidden * hidden, axis=1, keepdims=True)) + 1e-05)
    unit = hidden / row_norm
    unit_rows_halfprec = unit.astype(jnp.bfloat16)
    logit_scores = lax.dot_general(unit_rows_halfprec, unit_rows_halfprec, (((1,), (1,)), ((), ())), preferred_element_type=jnp.float32) / softness_factor
    row_length_total = logit_scores.shape[0]
    indices = jnp.arange(row_length_total, dtype=jnp.int32)
    self_mask = indices[:, None] == indices[None, :]
    log_sum = jnp.log(lax.optimization_barrier(jnp.sum(jnp.where(self_mask, 0.0, jnp.exp(logit_scores)), axis=1)))
    target = (indices[None, :] == partner[:, None]).astype(jnp.float32)
    row_weight = (jnp.where(self_mask, 0.0, jnp.exp(logit_scores - log_sum[:, None])) - target).astype(jnp.bfloat16)
    column_weight = (jnp.where(self_mask, 0.0, jnp.exp(logit_scores - log_sum[None, :])) - target).astype(jnp.bfloat16)
    unit_gradient_rows = (jnp.dot(row_weight, unit_rows_halfprec, preferred_element_type=jnp.float32) + jnp.dot(column_weight, unit_rows_halfprec, preferred_element_type=jnp.float32)) / softness_factor
    along = lax.optimization_barrier(jnp.sum(unit * unit_gradient_rows, axis=1, keepdims=True))
    grad_hidden = ((unit_gradient_rows - unit * along) / row_norm).astype(jnp.bfloat16)
    return lax.dot_general(features, grad_hidden, (((0,), (0,)), ((), ())), preferred_element_type=jnp.float32)

def reference(features, head_weight, partner):
    grouped = features.reshape(N_REP, GROUP, C)
    pairs = partner.reshape(N_REP, GROUP)

    def accumulate(running, items):
        return (running + group_gradient(items[0], head_weight, items[1]), None)
    gradient, unused = lax.scan(accumulate, jnp.zeros((C, D), jnp.float32), (grouped, pairs))
    mean_square = jnp.mean(gradient * gradient)
    return gradient / jnp.sqrt(mean_square + 1e-06)
```

```python
import jax
import jax.numpy as jnp
from jax import lax
from jax.experimental import pallas as pl
from jax.experimental.pallas import tpu as pltpu
from jax.sharding import PartitionSpec as P

softness_factor = 0.05
EXP2_SCALE = 1.4426950408889634 / softness_factor
BOTH = ("blk", "rep")
Y, XH, XL, Z, CORE = 8, 2, 2, 8, 2


def device_of(y, xh, xl, z, core):
    return (y * XH + xh) * (XL * Z * CORE) + (xl * Z + z) * CORE + core


PLACES = [
    (y, xh, xl, z, core)
    for y in range(Y)
    for xh in range(XH)
    for xl in range(XL)
    for z in range(Z)
    for core in range(CORE)
]
TO_HOST = [(device_of(y, h, l, z, c), device_of(y, c, l, z, h)) for y, h, l, z, c in PLACES]
TO_SIBLING = [(device_of(y, h, l, z, c), device_of(y, c, l, z, 1 - h)) for y, h, l, z, c in PLACES]
OTHER_CORE = [(r, r ^ 1) for r in range(XL * Z * CORE)]


def along_y(step):
    return [(b, ((b // XH + step) % Y) * XH + b % XH) for b in range(Y * XH)]


def contrast_kernel(*refs):
    core_ref, column_ref, side_ref = refs[:3]
    pieces = refs[3:-6]
    keep_ref, send_ref, units, per_lane, per_column, inverse = refs[-6:]
    wide = units.shape[1]
    blocks = units.shape[0]
    row = 0
    for piece in pieces:
        rows = piece.shape[0]
        block, start = divmod(row, wide)
        units[block, start : start + rows, :] = piece[...]
        row += rows
    per_lane[...] = jnp.zeros_like(per_lane)
    per_column[...] = jnp.zeros_like(per_column)

    def exponentials(left, right):
        scores = lax.dot_general(
            left, right, (((1,), (1,)), ((), ())), preferred_element_type=jnp.float32
        )
        return jnp.exp2(scores * EXP2_SCALE)

    def over_rows(values):
        return values.reshape(values.shape[0] // 8, 8, values.shape[1]).sum(0)

    def one_block(i, unused):
        left = units[i]
        values = exponentials(left, left)
        rows = lax.broadcasted_iota(jnp.int32, values.shape, 0)
        columns = lax.broadcasted_iota(jnp.int32, values.shape, 1)
        per_column[i] += over_rows(jnp.where(rows == columns, 0.0, values))

        def one_pair(j, unused):
            values = exponentials(left, units[j])
            per_column[j] += over_rows(values)
            per_lane[i] += sum(values[:, k : k + 128] for k in range(0, wide, 128))
            return unused

        return lax.fori_loop(i + 1, blocks, one_pair, unused)

    lax.fori_loop(0, blocks, one_block, 0)

    def invert(i, unused):
        total = per_column[i].sum(0, keepdims=True) + per_lane[i].T.sum(0, keepdims=True)
        inverse[i] = 1.0 / total
        return unused

    lax.fori_loop(0, blocks, invert, 0)

    own = units[0, :256, :]
    inverse_own = jnp.broadcast_to(inverse[0][:, :256], (128, 256)).T[:, :1]
    partner = side_ref[:, 0:1]
    row_ids = lax.broadcasted_iota(jnp.int32, (256, wide), 0)
    column_ids = lax.broadcasted_iota(jnp.int32, (256, wide), 1)

    def weigh(j, total):
        right = units[j]
        values = exponentials(own, right) * (inverse_own + inverse[j])
        values = jnp.where(row_ids == column_ids + j * wide, 0.0, values)
        values = jnp.where(column_ref[j] == partner, values - 2.0, values)
        return total + jnp.dot(
            values.astype(jnp.bfloat16), right, preferred_element_type=jnp.float32
        )

    grad_unit = lax.fori_loop(0, blocks, weigh, jnp.zeros(own.shape, jnp.float32))
    grad_unit = grad_unit * (1.0 / softness_factor)
    unit = own.astype(jnp.float32)
    along = jnp.sum(unit * grad_unit, axis=1, keepdims=True)
    grad_hidden = ((grad_unit - unit * along) * side_ref[:, 1:2]).astype(jnp.bfloat16)
    first, second = grad_hidden[:, :256], grad_hidden[:, 256:]
    low = core_ref[0] == 0
    keep_ref[...] = jnp.where(low, first, second)
    send_ref[...] = jnp.where(low, second, first)


def contrast(core, column_index, side, pieces):
    rows, width = pieces[0].shape
    half = jax.ShapeDtypeStruct((rows, width // 2), jnp.bfloat16)
    vmem = pl.BlockSpec(memory_space=pltpu.VMEM)
    return pl.pallas_call(
        contrast_kernel,
        out_shape=(half, half),
        in_specs=[pl.BlockSpec(memory_space=pltpu.SMEM)] + [vmem] * (2 + len(pieces)),
        out_specs=(vmem, vmem),
        scratch_shapes=[
            pltpu.VMEM((8, 512, width), jnp.bfloat16),
            pltpu.VMEM((8, 512, 128), jnp.float32),
            pltpu.VMEM((8, 8, 512), jnp.float32),
            pltpu.VMEM((8, 1, 512), jnp.float32),
        ],
        compiler_params=pltpu.CompilerParams(vmem_limit_bytes=40 * 1024 * 1024),
        cost_estimate=pl.CostEstimate(
            flops=14_000_000_000, bytes_accessed=5_000_000, transcendentals=10_000_000
        ),
        name="contrast",
    )(core, column_index, side, *pieces)


def on_device(features, head_weight, partner):
    rows = features.shape[0]
    channels, width = head_weight.shape
    y = lax.axis_index("blk") // XH
    core = lax.axis_index("rep") % CORE

    hidden = jnp.dot(features, head_weight, preferred_element_type=jnp.float32)
    row_norm = jnp.sqrt(jnp.sum(hidden * hidden, axis=1, keepdims=True) + 1e-05)
    unit = (hidden / row_norm).astype(jnp.bfloat16)
    side = jnp.stack([partner.astype(jnp.float32), 1.0 / row_norm[:, 0]])

    own = lax.ppermute(unit, BOTH, TO_HOST)
    up, down = along_y(1), along_y(-1)
    from_below, from_above = own, own
    near, places = [], []
    for distance in range(1, 4):
        from_below = lax.ppermute(from_below, "blk", up)
        from_above = lax.ppermute(from_above, "blk", down)
        near.append(jnp.concatenate([from_below, from_above]))
        places.append(((y - distance) % Y, (y + distance) % Y))
    half = rows // 2
    near.append(
        jnp.concatenate(
            [
                lax.ppermute(from_below[:half], "blk", up),
                lax.ppermute(from_above[half:], "blk", down),
            ]
        )
    )
    places.append(((y + Y // 2) % Y,))

    pieces = [own, lax.ppermute(own, "rep", OTHER_CORE)]
    starts = [(y * 2 + core) * rows, (y * 2 + 1 - core) * rows]
    for block, where in zip(near, places):
        pieces += [block, lax.ppermute(block, "rep", OTHER_CORE)]
        starts += [(w * 2 + core) * rows for w in where]
        starts += [(w * 2 + 1 - core) * rows for w in where]
    column_index = (
        jnp.stack(starts)[:, None] + jnp.arange(rows, dtype=jnp.int32)[None, :]
    ).astype(jnp.float32).reshape(8, 1, 512)

    later, own_again = lax.optimization_barrier((features, own))
    rows_here = lax.ppermute(later, BOTH, TO_HOST)
    rows_beside = lax.ppermute(later, BOTH, TO_SIBLING)
    side_here = lax.ppermute(side, BOTH, TO_HOST)

    kept, sent = contrast(core.reshape(1).astype(jnp.int32), column_index, side_here.T, pieces)
    beside = lax.ppermute(sent, "rep", OTHER_CORE)

    def contract(left, right):
        return lax.dot_general(
            left, right, (((0,), (0,)), ((), ())), preferred_element_type=jnp.float32
        )

    partial = (contract(rows_here, kept) + contract(rows_beside, beside)).astype(jnp.bfloat16)
    tiles = partial.reshape(channels // 8, 8, 2, 128).transpose(0, 2, 1, 3).reshape(512, 8, 128)
    received = lax.all_to_all(tiles, BOTH, 0, 0)
    fragment = received.reshape(256, 2, 8, 128).astype(jnp.float32).sum(0)
    spread = lax.all_to_all(jnp.broadcast_to(fragment[None], (32, 2, 8, 128)), "rep", 0, 0)
    gradient = spread.reshape(16, 2, 2, 8, 128).transpose(0, 3, 2, 1, 4).reshape(128, width)
    squares = jnp.sum(gradient * gradient)
    squares = lax.all_to_all(jnp.broadcast_to(squares, (16, 128)), "blk", 0, 0)
    total = jnp.sum(squares[:, 0])
    return gradient * lax.rsqrt(total / (channels * width) + 1e-06)


def solution(mesh):
    return jax.shard_map(
        on_device,
        mesh=mesh,
        in_specs=(P(("rep", "blk"), None), P(), P(("rep", "blk"))),
        out_specs=P("blk", None),
        check_vma=False,
    )
```

```python
import itertools

import jax
import jax.numpy as jnp
from jax import lax
from jax.experimental import pallas as pl
from jax.experimental.pallas import tpu as pltpu
from jax.sharding import Mesh
from jax.sharding import PartitionSpec as P

softness_factor = 0.05
EXP2_SCALE = 1.4426950408889634 / softness_factor
Y = 8
BITS = ("y2", "y1", "y0", "xh", "xl", "z2", "z1", "z0", "c")
YBITS = BITS[:3]
OTHER_CORE = [(0, 1), (1, 0)]


def moves(other_core):
    pairs = []
    for place in itertools.product((0, 1), repeat=len(BITS)):
        target = list(place)
        target[3], target[8] = place[8], place[3] ^ other_core
        index = [sum(bit << (8 - k) for k, bit in enumerate(bits)) for bits in (place, target)]
        pairs.append(tuple(index))
    return pairs


TO_HOST, TO_SIBLING = moves(0), moves(1)


def along_y(step):
    return [(k, (k + step) % Y) for k in range(Y)]


def exponentials(left, right):
    scores = lax.dot_general(
        left, right, (((1,), (1,)), ((), ())), preferred_element_type=jnp.float32
    )
    return jnp.exp2(scores * EXP2_SCALE)


def over_rows(values):
    return values.reshape(values.shape[0] // 8, 8, values.shape[1]).sum(0)


def over_lane_groups(values):
    return sum(values[:, k : k + 128] for k in range(0, values.shape[1], 128))


def same_block_kernel(mine_ref, sums_ref, per_lane, per_column):
    blocks, wide = per_lane.shape[0], per_lane.shape[1]
    per_lane[...] = jnp.zeros_like(per_lane)
    per_column[...] = jnp.zeros_like(per_column)
    for i in range(blocks):
        left = mine_ref[i * wide : (i + 1) * wide, :]
        values = exponentials(left, left)
        rows = lax.broadcasted_iota(jnp.int32, values.shape, 0)
        columns = lax.broadcasted_iota(jnp.int32, values.shape, 1)
        per_column[i] += over_rows(jnp.where(rows == columns, 0.0, values))
        for j in range(i + 1, blocks):
            values = exponentials(left, mine_ref[j * wide : (j + 1) * wide, :])
            per_column[j] += over_rows(values)
            per_lane[i] += over_lane_groups(values)
    for i in range(blocks):
        sums_ref[i] = per_column[i].sum(0, keepdims=True) + per_lane[i].T.sum(0, keepdims=True)


def cross_block_kernel(core_ref, mine_ref, sibling_ref, same_ref, sums_ref, units, per_lane, per_column):
    core = core_ref[0]
    blocks, wide = per_column.shape[0], per_column.shape[2]
    for k in range(blocks):
        units[blocks * core + k] = mine_ref[k * wide : (k + 1) * wide, :]
        units[blocks * (1 - core) + k] = sibling_ref[k * wide : (k + 1) * wide, :]
    per_lane[...] = jnp.zeros_like(per_lane)
    per_column[...] = jnp.zeros_like(per_column)
    for i in range(blocks // 2):
        left = units[blocks // 2 * core + i]
        for j in range(blocks):
            values = exponentials(left, units[blocks + j])
            per_column[j] += over_rows(values)
            per_lane[i] += over_lane_groups(values)
    for k in range(blocks):
        sums_ref[k] = jnp.zeros_like(sums_ref[k])
        sums_ref[blocks + k] = per_column[k].sum(0, keepdims=True)
    for i in range(blocks // 2):
        sums_ref[blocks // 2 * core + i] = per_lane[i].T.sum(0, keepdims=True)
    for k in range(blocks):
        sums_ref[blocks * core + k] += same_ref[k]


def weight_kernel(
    core_ref, start_ref, side_ref, sums_ref, mine_ref, sibling_ref, keep_ref, send_ref, total
):
    core = core_ref[0]
    wide = sums_ref.shape[2]
    blocks = sums_ref.shape[0] // 2
    rows = side_ref.shape[0]
    own = mine_ref[:rows, :]
    mine_sums = sums_ref[blocks * core][:, :rows]
    inverse_own = 1.0 / jnp.broadcast_to(mine_sums, (128, rows)).T[:, :1]
    partner = side_ref[:, 0:1].astype(jnp.int32)
    lanes = lax.broadcasted_iota(jnp.int32, (1, wide), 1)
    for part, ref in enumerate((mine_ref, sibling_ref)):
        for k in range(blocks):
            which = core if part == 0 else 1 - core
            right = ref[k * wide : (k + 1) * wide, :]
            inverse = 1.0 / sums_ref[blocks * which + k]
            values = exponentials(own, right) * (inverse_own + inverse)
            if part == 0 and k == 0:
                row_ids = lax.broadcasted_iota(jnp.int32, values.shape, 0)
                column_ids = lax.broadcasted_iota(jnp.int32, values.shape, 1)
                values = jnp.where(row_ids == column_ids, 0.0, values)
            first = start_ref[part * blocks * 2 + 2 * k]
            second = start_ref[part * blocks * 2 + 2 * k + 1]
            columns = lanes + jnp.where(lanes < rows, first, second - rows)
            values = jnp.where(columns == partner, values - 2.0, values)
            product = jnp.dot(
                values.astype(jnp.bfloat16), right, preferred_element_type=jnp.float32
            )
            if part == 0 and k == 0:
                total[...] = product
            else:
                total[...] += product
    grad_unit = total[...] * (1.0 / softness_factor)
    unit = own.astype(jnp.float32)
    along = jnp.sum(unit * grad_unit, axis=1, keepdims=True)
    grad_hidden = ((grad_unit - unit * along) * side_ref[:, 1:2]).astype(jnp.bfloat16)
    middle = grad_hidden.shape[1] // 2
    first, second = grad_hidden[:, :middle], grad_hidden[:, middle:]
    keep_ref[...] = jnp.where(core == 0, first, second)
    send_ref[...] = jnp.where(core == 0, second, first)


VMEM = pl.BlockSpec(memory_space=pltpu.VMEM)
SMEM = pl.BlockSpec(memory_space=pltpu.SMEM)


def kernel_call(body, outputs, in_specs, scratch, flops, name):
    return pl.pallas_call(
        body,
        out_shape=outputs,
        in_specs=in_specs,
        out_specs=jax.tree.map(lambda unused: VMEM, outputs),
        scratch_shapes=scratch,
        compiler_params=pltpu.CompilerParams(vmem_limit_bytes=40 * 1024 * 1024),
        cost_estimate=pl.CostEstimate(
            flops=flops, bytes_accessed=2_000_000, transcendentals=100_000
        ),
        name=name,
    )


def on_device(features, head_weight, partner):
    rows = features.shape[0]
    channels, width = head_weight.shape
    y = lax.axis_index("y2") * 4 + lax.axis_index("y1") * 2 + lax.axis_index("y0")
    core = lax.axis_index("c")
    core_scalar = core.reshape(1).astype(jnp.int32)

    hidden = jnp.dot(features, head_weight, preferred_element_type=jnp.float32)
    row_norm = jnp.sqrt(jnp.sum(hidden * hidden, axis=1, keepdims=True) + 1e-05)
    unit = (hidden / row_norm).astype(jnp.bfloat16)
    side = jnp.stack([partner.astype(jnp.float32), 1.0 / row_norm[:, 0]])

    own = lax.ppermute(unit, BITS, TO_HOST)
    side_here = lax.ppermute(side, BITS, TO_HOST)
    up, down = along_y(1), along_y(-1)
    from_below, from_above = own, own
    pieces, places = [own], [y]
    sends = []
    for distance in range(1, 4):
        from_below = lax.ppermute(from_below, YBITS, up)
        from_above = lax.ppermute(from_above, YBITS, down)
        pieces += [from_below, from_above]
        places += [(y - distance) % Y, (y + distance) % Y]
        if distance < 3:
            later, unused = lax.optimization_barrier((features, from_below))
            sends.append(lax.ppermute(later, BITS, (TO_HOST, TO_SIBLING)[distance - 1]))
    half = rows // 2
    pieces += [
        lax.ppermute(from_below[:half], YBITS, up),
        lax.ppermute(from_above[half:], YBITS, down),
    ]
    places.append((y + Y // 2) % Y)
    mine = jnp.concatenate(pieces)
    rows_here, rows_beside = sends
    places = jnp.stack(places)
    starts = jnp.concatenate([places * 2 + core, places * 2 + 1 - core]).astype(jnp.int32) * rows

    sibling = lax.ppermute(mine, "c", OTHER_CORE)
    lanes = pltpu.VMEM((4, 512, 128), jnp.float32)
    columns = pltpu.VMEM((4, 8, 512), jnp.float32)
    same = kernel_call(
        same_block_kernel,
        jax.ShapeDtypeStruct((4, 1, 512), jnp.float32),
        [VMEM],
        [lanes, columns],
        3_000_000_000,
        "same_parity_sums",
    )(mine)
    sums = kernel_call(
        cross_block_kernel,
        jax.ShapeDtypeStruct((8, 1, 512), jnp.float32),
        [SMEM, VMEM, VMEM, VMEM],
        [pltpu.VMEM((8, 512, width), jnp.bfloat16), lanes, columns],
        2_000_000_000,
        "cross_parity_sums",
    )(core_scalar, mine, sibling, same)
    sums = lax.psum(sums, "c")
    piece = jax.ShapeDtypeStruct((rows, width // 2), jnp.bfloat16)
    kept, sent = kernel_call(
        weight_kernel,
        (piece, piece),
        [SMEM, SMEM, VMEM, VMEM, VMEM, VMEM],
        [pltpu.VMEM((rows, width), jnp.float32)],
        2_000_000_000,
        "weights",
    )(core_scalar, starts, side_here.T, sums, mine, sibling)
    beside = lax.ppermute(sent, "c", OTHER_CORE)

    def contract(left, right):
        return lax.dot_general(
            left, right, (((0,), (0,)), ((), ())), preferred_element_type=jnp.float32
        )

    partial = (contract(rows_here, kept) + contract(rows_beside, beside)).astype(jnp.bfloat16)
    tiles = partial.reshape(4, 2, 2, 2, 4, 2, 8, 256)
    tiles = tiles.transpose(1, 3, 5, 0, 2, 4, 6, 7).reshape(8, 32 * 8, 256)
    received = lax.all_to_all(tiles, ("y0", "xl", "z0"), 0, 0)
    near_sum = received.astype(jnp.float32).sum(0).reshape(32, 8, 256)
    received = lax.all_to_all(near_sum, ("y2", "y1", "xh", "z2", "z1"), 0, 0)
    fragment = received.sum(0)
    spread = lax.all_to_all(
        jnp.broadcast_to(fragment[None], (32, 8, 256)), ("xl", "z2", "z1", "z0", "c"), 0, 0
    )
    gradient = spread.reshape(16, 2, 8, 256).transpose(0, 2, 1, 3).reshape(128, width)
    squares = jnp.sum(gradient * gradient)
    squares = lax.all_to_all(
        jnp.broadcast_to(squares, (16, 128)), ("y2", "y1", "y0", "xh"), 0, 0
    )
    total = jnp.sum(squares[:, 0])
    return gradient * lax.rsqrt(total / (channels * width) + 1e-06)


def solution(mesh):
    bits = Mesh(mesh.devices.reshape((2,) * len(BITS)), BITS)
    images = P(("xl", "z2", "z1", "z0", "c", "y2", "y1", "y0", "xh"))
    return jax.shard_map(
        on_device,
        mesh=bits,
        in_specs=(P(*images, None), P(), images),
        out_specs=P(("y2", "y1", "y0", "xh"), None),
        check_vma=False,
    )
```

```python
import itertools

import jax
import jax.numpy as jnp
from jax import lax
from jax.experimental import pallas as pl
from jax.experimental.pallas import tpu as pltpu
from jax.sharding import Mesh
from jax.sharding import PartitionSpec as P

softness_factor = 0.05
EXP2_SCALE = 1.4426950408889634 / softness_factor
Y = 8
BITS = ("y2", "y1", "y0", "xh", "xl", "z2", "z1", "z0", "c")
YBITS = BITS[:3]
OTHER_CORE = [(0, 1), (1, 0)]


def moves(other_core):
    pairs = []
    for place in itertools.product((0, 1), repeat=len(BITS)):
        target = list(place)
        xh, xl, core = place[3], place[4], place[8]
        target[3], target[4], target[8] = core ^ xl, 1 - xl, xh ^ other_core
        index = [sum(bit << (8 - k) for k, bit in enumerate(bits)) for bits in (place, target)]
        pairs.append(tuple(index))
    return pairs


TO_HOST, TO_SIBLING = moves(0), moves(1)


ROUND = [(2 * y + c, 2 * ((y + (1, -1)[c]) % Y) + c) for y in range(Y) for c in range(2)]


def exponentials(left, right):
    scores = lax.dot_general(
        left, right, (((1,), (1,)), ((), ())), preferred_element_type=jnp.float32
    )
    return jnp.exp2(scores * EXP2_SCALE)


def over_rows(values):
    return values.reshape(values.shape[0] // 8, 8, values.shape[1]).sum(0)


def over_lane_groups(values):
    return sum(values[:, k : k + 128] for k in range(0, values.shape[1], 128))


def same_block_kernel(mine_ref, sums_ref, per_lane, per_column):
    blocks, wide = per_lane.shape[0], per_lane.shape[1]
    per_lane[...] = jnp.zeros_like(per_lane)
    per_column[...] = jnp.zeros_like(per_column)
    for i in range(blocks):
        left = mine_ref[i * wide : (i + 1) * wide, :]
        values = exponentials(left, left)
        rows = lax.broadcasted_iota(jnp.int32, values.shape, 0)
        columns = lax.broadcasted_iota(jnp.int32, values.shape, 1)
        per_column[i] += over_rows(jnp.where(rows == columns, 0.0, values))
        for j in range(i + 1, blocks):
            values = exponentials(left, mine_ref[j * wide : (j + 1) * wide, :])
            per_column[j] += over_rows(values)
            per_lane[i] += over_lane_groups(values)
    for i in range(blocks):
        sums_ref[i] = per_column[i].sum(0, keepdims=True) + per_lane[i].T.sum(0, keepdims=True)


def cross_block_kernel(core_ref, mine_ref, sibling_ref, same_ref, sums_ref, per_lane, per_column):
    core = core_ref[0]
    blocks, wide = per_column.shape[0], per_column.shape[2]
    half = blocks // 2
    per_lane[...] = jnp.zeros_like(per_lane)
    per_column[...] = jnp.zeros_like(per_column)

    def pairs(left_ref, first, right_ref):
        for i in range(half):
            left = left_ref[(first + i) * wide : (first + i + 1) * wide, :]
            for j in range(blocks):
                values = exponentials(left, right_ref[j * wide : (j + 1) * wide, :])
                per_column[j] += over_rows(values)
                per_lane[i] += over_lane_groups(values)
        for k in range(blocks):
            sums_ref[k] = jnp.zeros_like(sums_ref[k])
            sums_ref[blocks + k] = per_column[k].sum(0, keepdims=True)
        for i in range(half):
            sums_ref[first + i] = per_lane[i].T.sum(0, keepdims=True)

    @pl.when(core == 0)
    def _():
        pairs(mine_ref, 0, sibling_ref)

    @pl.when(core == 1)
    def _():
        pairs(sibling_ref, half, mine_ref)

    for k in range(blocks):
        sums_ref[blocks * core + k] += same_ref[k]


def weight_kernel(
    core_ref, start_ref, side_ref, sums_ref, mine_ref, sibling_ref, keep_ref, send_ref, total
):
    core = core_ref[0]
    wide = sums_ref.shape[2]
    blocks = sums_ref.shape[0] // 2
    rows = side_ref.shape[0]
    own = mine_ref[:rows, :]
    mine_sums = sums_ref[blocks * core][:, :rows]
    inverse_own = 1.0 / jnp.broadcast_to(mine_sums, (128, rows)).T[:, :1]
    partner = side_ref[:, 0:1].astype(jnp.int32)
    lanes = lax.broadcasted_iota(jnp.int32, (1, wide), 1)
    for part, ref in enumerate((mine_ref, sibling_ref)):
        for k in range(blocks):
            which = core if part == 0 else 1 - core
            right = ref[k * wide : (k + 1) * wide, :]
            inverse = 1.0 / sums_ref[blocks * which + k]
            values = exponentials(own, right) * (inverse_own + inverse)
            if part == 0 and k == 0:
                row_ids = lax.broadcasted_iota(jnp.int32, values.shape, 0)
                column_ids = lax.broadcasted_iota(jnp.int32, values.shape, 1)
                values = jnp.where(row_ids == column_ids, 0.0, values)
            first = start_ref[part * blocks * 2 + 2 * k]
            second = start_ref[part * blocks * 2 + 2 * k + 1]
            columns = lanes + jnp.where(lanes < rows, first, second - rows)
            values = jnp.where(columns == partner, values - 2.0, values)
            product = jnp.dot(
                values.astype(jnp.bfloat16), right, preferred_element_type=jnp.float32
            )
            if part == 0 and k == 0:
                total[...] = product
            else:
                total[...] += product
    grad_unit = total[...] * (1.0 / softness_factor)
    unit = own.astype(jnp.float32)
    along = jnp.sum(unit * grad_unit, axis=1, keepdims=True)
    grad_hidden = ((grad_unit - unit * along) * side_ref[:, 1:2]).astype(jnp.bfloat16)
    middle = grad_hidden.shape[1] // 2
    first, second = grad_hidden[:, :middle], grad_hidden[:, middle:]
    keep_ref[...] = jnp.where(core == 0, first, second)
    send_ref[...] = jnp.where(core == 0, second, first)


VMEM = pl.BlockSpec(memory_space=pltpu.VMEM)
SMEM = pl.BlockSpec(memory_space=pltpu.SMEM)


def kernel_call(body, outputs, in_specs, scratch, flops, name):
    return pl.pallas_call(
        body,
        out_shape=outputs,
        in_specs=in_specs,
        out_specs=jax.tree.map(lambda unused: VMEM, outputs),
        scratch_shapes=scratch,
        compiler_params=pltpu.CompilerParams(vmem_limit_bytes=40 * 1024 * 1024),
        cost_estimate=pl.CostEstimate(
            flops=flops, bytes_accessed=2_000_000, transcendentals=100_000
        ),
        name=name,
    )


def on_device(features, head_weight, partner):
    rows = features.shape[0]
    channels, width = head_weight.shape
    y = lax.axis_index("y2") * 4 + lax.axis_index("y1") * 2 + lax.axis_index("y0")
    core = lax.axis_index("c")
    core_scalar = core.reshape(1).astype(jnp.int32)

    hidden = jnp.dot(features, head_weight, preferred_element_type=jnp.float32)
    row_norm = jnp.sqrt(jnp.sum(hidden * hidden, axis=1, keepdims=True) + 1e-05)
    unit = (hidden / row_norm).astype(jnp.bfloat16)
    side = jnp.stack([partner.astype(jnp.float32), 1.0 / row_norm[:, 0]])

    own = lax.ppermute(unit, BITS, TO_HOST)
    side_here = lax.ppermute(side, BITS, TO_HOST)
    sign = jnp.where(core == 0, -1, 1)
    same_core = own
    other_core = lax.ppermute(own, "c", OTHER_CORE)
    pieces, places = [own], [y * 2 + core]
    sends = []
    for distance in range(1, 5):
        place = (y + sign * distance) % Y * 2
        same_core = lax.ppermute(same_core, (*YBITS, "c"), ROUND)
        pieces.append(same_core)
        places.append(place + core)
        if distance == 4:
            break
        other_core = lax.ppermute(other_core, (*YBITS, "c"), ROUND)
        pieces.append(other_core)
        places.append(place + 1 - core)
        if distance < 3:
            later, unused = lax.optimization_barrier((features, same_core))
            sends.append(lax.ppermute(later, BITS, (TO_HOST, TO_SIBLING)[distance - 1]))
    sign, core_there = -sign, 1 - core
    places.append(y * 2 + core_there)
    for distance in range(1, 5):
        place = (y + sign * distance) % Y * 2
        places += [place + core_there, place + 1 - core_there][: 1 if distance == 4 else 2]
    mine = jnp.concatenate(pieces)
    starts = jnp.stack(places).astype(jnp.int32) * rows
    rows_here, rows_beside = sends

    sibling = lax.ppermute(mine, "c", OTHER_CORE)
    lanes = pltpu.VMEM((4, 512, 128), jnp.float32)
    columns = pltpu.VMEM((4, 8, 512), jnp.float32)
    same = kernel_call(
        same_block_kernel,
        jax.ShapeDtypeStruct((4, 1, 512), jnp.float32),
        [VMEM],
        [lanes, columns],
        3_000_000_000,
        "same_parity_sums",
    )(mine)
    sums = kernel_call(
        cross_block_kernel,
        jax.ShapeDtypeStruct((8, 1, 512), jnp.float32),
        [SMEM, VMEM, VMEM, VMEM],
        [lanes, columns],
        2_000_000_000,
        "cross_parity_sums",
    )(core_scalar, mine, sibling, same)
    sums = lax.psum(sums, "c")
    piece = jax.ShapeDtypeStruct((rows, width // 2), jnp.bfloat16)
    kept, sent = kernel_call(
        weight_kernel,
        (piece, piece),
        [SMEM, SMEM, VMEM, VMEM, VMEM, VMEM],
        [pltpu.VMEM((rows, width), jnp.float32)],
        2_000_000_000,
        "weights",
    )(core_scalar, starts, side_here.T, sums, mine, sibling)
    beside = lax.ppermute(sent, "c", OTHER_CORE)

    def contract(left, right):
        return lax.dot_general(
            left, right, (((0,), (0,)), ((), ())), preferred_element_type=jnp.float32
        )

    partial = (contract(rows_here, kept) + contract(rows_beside, beside)).astype(jnp.bfloat16)
    tiles = partial.reshape(4, 2, 2, 2, 4, 2, 8, 256)
    tiles = tiles.transpose(1, 2, 3, 5, 0, 4, 6, 7).reshape(16, 16 * 8, 256)
    received = lax.all_to_all(tiles, ("y0", "xh", "xl", "z0"), 0, 0)
    near_sum = received.astype(jnp.float32).sum(0).reshape(4, 4 * 8, 256)
    along_y_sum = lax.all_to_all(near_sum, ("y2", "y1"), 0, 0).sum(0).reshape(4, 8, 256)
    fragment = lax.all_to_all(along_y_sum, ("z2", "z1"), 0, 0).sum(0).astype(jnp.bfloat16)
    spread = lax.all_to_all(
        jnp.broadcast_to(fragment[None], (32, 8, 256)), ("xl", "z2", "z1", "z0", "c"), 0, 0
    )
    gradient = spread.reshape(16, 2, 8, 256).transpose(0, 2, 1, 3).reshape(128, width)
    gradient = gradient.astype(jnp.float32)
    squares = jnp.sum(gradient * gradient)
    squares = lax.all_to_all(
        jnp.broadcast_to(squares, (16, 128)), ("y2", "y1", "y0", "xh"), 0, 0
    )
    total = jnp.sum(squares[:, 0])
    return gradient * lax.rsqrt(total / (channels * width) + 1e-06)


def solution(mesh):
    bits = Mesh(mesh.devices.reshape((2,) * len(BITS)), BITS)
    images = P(("xl", "z2", "z1", "z0", "c", "y2", "y1", "y0", "xh"))
    return jax.shard_map(
        on_device,
        mesh=bits,
        in_specs=(P(*images, None), P(), images),
        out_specs=P(("y2", "y1", "y0", "xh"), None),
        check_vma=False,
    )
```

```python
import itertools

import jax
import jax.numpy as jnp
from jax import lax
from jax.experimental import pallas as pl
from jax.experimental.pallas import tpu as pltpu
from jax.sharding import Mesh
from jax.sharding import PartitionSpec as P

softness_factor = 0.05
EXP2_SCALE = 1.4426950408889634 / softness_factor
Y = 8
BITS = ("y2", "y1", "y0", "xh", "xl", "z2", "z1", "z0", "c")
YBITS = BITS[:3]
OTHER_CORE = [(0, 1), (1, 0)]


def moves(other_core, step):
    pairs = []
    for y, xh, xl, z, core in itertools.product(range(Y), range(2), range(2), range(8), range(2)):
        there = xh ^ other_core
        y_there = (y + step * (1, -1)[there]) % Y
        pairs.append((place(y, xh, xl, z, core), place(y_there, core ^ xl, 1 - xl, z, there)))
    return pairs


def place(y, xh, xl, z, core):
    return (((y * 2 + xh) * 2 + xl) * 8 + z) * 2 + core


TO_HOST, TO_SIBLING = moves(0, 0), moves(1, 0)
TO_NEXT_SAME, TO_NEXT_OTHER = moves(0, 1), moves(1, 1)
ROUND = [(2 * y + c, 2 * ((y + (1, -1)[c]) % Y) + c) for y in range(Y) for c in range(2)]


def exponentials(left, right):
    scores = lax.dot_general(
        left, right, (((1,), (1,)), ((), ())), preferred_element_type=jnp.float32
    )
    return jnp.exp2(scores * EXP2_SCALE)


def over_rows(values):
    return values.reshape(values.shape[0] // 8, 8, values.shape[1]).sum(0)


def over_lane_groups(values):
    return sum(values[:, k : k + 128] for k in range(0, values.shape[1], 128))


def same_block_kernel(mine_ref, sums_ref, per_lane, per_column):
    blocks, wide = per_lane.shape[0], per_lane.shape[1]
    per_lane[...] = jnp.zeros_like(per_lane)
    per_column[...] = jnp.zeros_like(per_column)
    for i in range(blocks):
        left = mine_ref[i * wide : (i + 1) * wide, :]
        values = exponentials(left, left)
        rows = lax.broadcasted_iota(jnp.int32, values.shape, 0)
        columns = lax.broadcasted_iota(jnp.int32, values.shape, 1)
        per_column[i] += over_rows(jnp.where(rows == columns, 0.0, values))
        for j in range(i + 1, blocks):
            values = exponentials(left, mine_ref[j * wide : (j + 1) * wide, :])
            per_column[j] += over_rows(values)
            per_lane[i] += over_lane_groups(values)
    for i in range(blocks):
        sums_ref[i] = per_column[i].sum(0, keepdims=True) + per_lane[i].T.sum(0, keepdims=True)


def cross_block_kernel(core_ref, mine_ref, sibling_ref, same_ref, sums_ref, per_lane, per_column):
    core = core_ref[0]
    blocks, wide = per_column.shape[0], per_column.shape[2]
    half = blocks // 2
    per_lane[...] = jnp.zeros_like(per_lane)
    per_column[...] = jnp.zeros_like(per_column)

    def pairs(left_ref, first, right_ref):
        for i in range(half):
            left = left_ref[(first + i) * wide : (first + i + 1) * wide, :]
            for j in range(blocks):
                values = exponentials(left, right_ref[j * wide : (j + 1) * wide, :])
                per_column[j] += over_rows(values)
                per_lane[i] += over_lane_groups(values)
        for k in range(blocks):
            sums_ref[k] = jnp.zeros_like(sums_ref[k])
            sums_ref[blocks + k] = per_column[k].sum(0, keepdims=True)
        for i in range(half):
            sums_ref[first + i] = per_lane[i].T.sum(0, keepdims=True)

    @pl.when(core == 0)
    def _():
        pairs(mine_ref, 0, sibling_ref)

    @pl.when(core == 1)
    def _():
        pairs(sibling_ref, half, mine_ref)

    for k in range(blocks):
        sums_ref[blocks * core + k] += same_ref[k]


def weight_kernel(
    core_ref, start_ref, side_ref, sums_ref, mine_ref, sibling_ref, keep_ref, send_ref, total
):
    core = core_ref[0]
    wide = sums_ref.shape[2]
    blocks = sums_ref.shape[0] // 2
    rows = side_ref.shape[0]
    own = mine_ref[:rows, :]
    mine_sums = sums_ref[blocks * core][:, :rows]
    inverse_own = 1.0 / jnp.broadcast_to(mine_sums, (128, rows)).T[:, :1]
    partner = side_ref[:, 0:1].astype(jnp.int32)
    lanes = lax.broadcasted_iota(jnp.int32, (1, wide), 1)
    for part, ref in enumerate((mine_ref, sibling_ref)):
        for k in range(blocks):
            which = core if part == 0 else 1 - core
            right = ref[k * wide : (k + 1) * wide, :]
            inverse = 1.0 / sums_ref[blocks * which + k]
            values = exponentials(own, right) * (inverse_own + inverse)
            if part == 0 and k == 0:
                row_ids = lax.broadcasted_iota(jnp.int32, values.shape, 0)
                column_ids = lax.broadcasted_iota(jnp.int32, values.shape, 1)
                values = jnp.where(row_ids == column_ids, 0.0, values)
            first = start_ref[part * blocks * 2 + 2 * k]
            second = start_ref[part * blocks * 2 + 2 * k + 1]
            columns = lanes + jnp.where(lanes < rows, first, second - rows)
            values = jnp.where(columns == partner, values - 2.0, values)
            product = jnp.dot(
                values.astype(jnp.bfloat16), right, preferred_element_type=jnp.float32
            )
            if part == 0 and k == 0:
                total[...] = product
            else:
                total[...] += product
    grad_unit = total[...] * (1.0 / softness_factor)
    unit = own.astype(jnp.float32)
    along = jnp.sum(unit * grad_unit, axis=1, keepdims=True)
    grad_hidden = ((grad_unit - unit * along) * side_ref[:, 1:2]).astype(jnp.bfloat16)
    middle = grad_hidden.shape[1] // 2
    first, second = grad_hidden[:, :middle], grad_hidden[:, middle:]
    keep_ref[...] = jnp.where(core == 0, first, second)
    send_ref[...] = jnp.where(core == 0, second, first)


VMEM = pl.BlockSpec(memory_space=pltpu.VMEM)
SMEM = pl.BlockSpec(memory_space=pltpu.SMEM)


def kernel_call(body, outputs, in_specs, scratch, flops, name):
    return pl.pallas_call(
        body,
        out_shape=outputs,
        in_specs=in_specs,
        out_specs=jax.tree.map(lambda unused: VMEM, outputs),
        scratch_shapes=scratch,
        compiler_params=pltpu.CompilerParams(vmem_limit_bytes=40 * 1024 * 1024),
        cost_estimate=pl.CostEstimate(
            flops=flops, bytes_accessed=2_000_000, transcendentals=100_000
        ),
        name=name,
    )


def on_device(features, head_weight, partner):
    rows = features.shape[0]
    channels, width = head_weight.shape
    y = lax.axis_index("y2") * 4 + lax.axis_index("y1") * 2 + lax.axis_index("y0")
    core = lax.axis_index("c")
    core_scalar = core.reshape(1).astype(jnp.int32)

    hidden = jnp.dot(features, head_weight, preferred_element_type=jnp.float32)
    row_norm = jnp.sqrt(jnp.sum(hidden * hidden, axis=1, keepdims=True) + 1e-05)
    unit = (hidden / row_norm).astype(jnp.bfloat16)
    side = jnp.stack([partner.astype(jnp.float32), 1.0 / row_norm[:, 0]])

    sign = jnp.where(core == 0, -1, 1)
    same_core = lax.ppermute(unit, BITS, TO_NEXT_SAME)
    other_core = lax.ppermute(unit, BITS, TO_NEXT_OTHER)
    own = lax.ppermute(unit, BITS, TO_HOST)
    side_here = lax.ppermute(side, BITS, TO_HOST)
    later, unused = lax.optimization_barrier((features, same_core))
    rows_here = lax.ppermute(later, BITS, TO_HOST)
    later, unused = lax.optimization_barrier((features, other_core))
    rows_beside = lax.ppermute(later, BITS, TO_SIBLING)
    pieces, places = [own], [y * 2 + core]
    for distance in range(1, 5):
        place_there = (y + sign * distance) % Y * 2
        if distance == 3:
            same_core, side_here = lax.optimization_barrier((same_core, side_here))
        if distance == 4:
            same_core, rows_here = lax.optimization_barrier((same_core, rows_here))
        if distance > 1:
            same_core = lax.ppermute(same_core, (*YBITS, "c"), ROUND)
        if distance == 4:
            same_core, rows_beside = lax.optimization_barrier((same_core, rows_beside))
        pieces.append(same_core)
        places.append(place_there + core)
        if distance == 4:
            break
        if distance > 1:
            other_core = lax.ppermute(other_core, (*YBITS, "c"), ROUND)
        pieces.append(other_core)
        places.append(place_there + 1 - core)
    sign, core_there = -sign, 1 - core
    places.append(y * 2 + core_there)
    for distance in range(1, 5):
        place_there = (y + sign * distance) % Y * 2
        there = [place_there + core_there, place_there + 1 - core_there]
        places += there[: 1 if distance == 4 else 2]
    mine = jnp.concatenate(pieces)
    starts = jnp.stack(places).astype(jnp.int32) * rows

    sibling = lax.ppermute(mine, "c", OTHER_CORE)
    lanes = pltpu.VMEM((4, 512, 128), jnp.float32)
    columns = pltpu.VMEM((4, 8, 512), jnp.float32)
    same = kernel_call(
        same_block_kernel,
        jax.ShapeDtypeStruct((4, 1, 512), jnp.float32),
        [VMEM],
        [lanes, columns],
        3_000_000_000,
        "same_parity_sums",
    )(mine)
    sums = kernel_call(
        cross_block_kernel,
        jax.ShapeDtypeStruct((8, 1, 512), jnp.float32),
        [SMEM, VMEM, VMEM, VMEM],
        [lanes, columns],
        2_000_000_000,
        "cross_parity_sums",
    )(core_scalar, mine, sibling, same)
    sums = lax.psum(sums, "c")
    piece = jax.ShapeDtypeStruct((rows, width // 2), jnp.bfloat16)
    kept, sent = kernel_call(
        weight_kernel,
        (piece, piece),
        [SMEM, SMEM, VMEM, VMEM, VMEM, VMEM],
        [pltpu.VMEM((rows, width), jnp.float32)],
        2_000_000_000,
        "weights",
    )(core_scalar, starts, side_here.T, sums, mine, sibling)
    beside = lax.ppermute(sent, "c", OTHER_CORE)

    def contract(left, right):
        return lax.dot_general(
            left, right, (((0,), (0,)), ((), ())), preferred_element_type=jnp.float32
        )

    partial = (contract(rows_here, kept) + contract(rows_beside, beside)).astype(jnp.bfloat16)
    tiles = partial.reshape(4, 2, 2, 2, 2, 2, 2, 8, 256)
    tiles = tiles.transpose(1, 2, 3, 6, 0, 5, 4, 7, 8).reshape(16, 16 * 8, 256)
    received = lax.all_to_all(tiles, ("y0", "xh", "xl", "z0"), 0, 0)
    near_sum = received.astype(jnp.float32).sum(0).reshape(8, 2 * 8, 256)
    part = lax.all_to_all(near_sum, ("y2", "y1", "z1"), 0, 0).sum(0).astype(jnp.bfloat16)
    spread = lax.all_to_all(
        jnp.broadcast_to(part[None], (32, 2 * 8, 256)), ("xl", "z2", "z1", "z0", "c"), 0, 0
    )
    spread = spread.reshape(2, 2, 4, 2, 2, 8, 256).astype(jnp.float32)
    gradient = (spread[:, 0] + spread[:, 1]).transpose(0, 3, 1, 4, 2, 5).reshape(128, width)
    squares = jnp.sum(gradient * gradient)
    squares = lax.all_to_all(
        jnp.broadcast_to(squares, (16, 128)), ("y2", "y1", "y0", "xh"), 0, 0
    )
    total = jnp.sum(squares[:, 0])
    return gradient * lax.rsqrt(total / (channels * width) + 1e-06)


def solution(mesh):
    bits = Mesh(mesh.devices.reshape((2,) * len(BITS)), BITS)
    images = P(("xl", "z2", "z1", "z0", "c", "y2", "y1", "y0", "xh"))
    return jax.shard_map(
        on_device,
        mesh=bits,
        in_specs=(P(*images, None), P(), images),
        out_specs=P(("y2", "y1", "y0", "xh"), None),
        check_vma=False,
    )
```

```python
import itertools

import jax
import jax.numpy as jnp
from jax import lax
from jax.experimental import pallas as pl
from jax.experimental.pallas import tpu as pltpu
from jax.sharding import Mesh
from jax.sharding import PartitionSpec as P

softness_factor = 0.05
EXP2_SCALE = 1.4426950408889634 / softness_factor
Y = 8
BITS = ("y2", "y1", "y0", "xh", "xl", "z2", "z1", "z0", "c")
YBITS = BITS[:3]
OTHER_CORE = [(0, 1), (1, 0)]


def moves(other_core, step):
    pairs = []
    for y, xh, xl, z, core in itertools.product(range(Y), range(2), range(2), range(8), range(2)):
        there = xh ^ other_core
        y_there = (y + step * (1, -1)[there]) % Y
        pairs.append((place(y, xh, xl, z, core), place(y_there, core ^ xl, 1 - xl, z, there)))
    return pairs


def place(y, xh, xl, z, core):
    return (((y * 2 + xh) * 2 + xl) * 8 + z) * 2 + core


TO_HOST, TO_SIBLING = moves(0, 0), moves(1, 0)
TO_NEXT_SAME, TO_NEXT_OTHER = moves(0, 1), moves(1, 1)
ROUND = [(2 * y + c, 2 * ((y + (1, -1)[c]) % Y) + c) for y in range(Y) for c in range(2)]


def exponentials(left, right):
    scores = lax.dot_general(
        left, right, (((1,), (1,)), ((), ())), preferred_element_type=jnp.float32
    )
    return jnp.exp2(scores * EXP2_SCALE)


def over_rows(values):
    return values.reshape(values.shape[0] // 8, 8, values.shape[1]).sum(0)


def over_lane_groups(values):
    return sum(values[:, k : k + 128] for k in range(0, values.shape[1], 128))


def same_block_kernel(mine_ref, sums_ref, per_lane, per_column):
    blocks, wide = per_lane.shape[0], per_lane.shape[1]
    per_lane[...] = jnp.zeros_like(per_lane)
    per_column[...] = jnp.zeros_like(per_column)
    for i in range(blocks):
        left = mine_ref[i * wide : (i + 1) * wide, :]
        values = exponentials(left, left)
        rows = lax.broadcasted_iota(jnp.int32, values.shape, 0)
        columns = lax.broadcasted_iota(jnp.int32, values.shape, 1)
        per_column[i] += over_rows(jnp.where(rows == columns, 0.0, values))
        for j in range(i + 1, blocks):
            values = exponentials(left, mine_ref[j * wide : (j + 1) * wide, :])
            per_column[j] += over_rows(values)
            per_lane[i] += over_lane_groups(values)
    for i in range(blocks):
        sums_ref[i] = per_column[i].sum(0, keepdims=True) + per_lane[i].T.sum(0, keepdims=True)


def cross_block_kernel(core_ref, mine_ref, sibling_ref, same_ref, sums_ref, per_lane, per_column):
    core = core_ref[0]
    blocks, wide = per_column.shape[0], per_column.shape[2]
    half = blocks // 2
    per_lane[...] = jnp.zeros_like(per_lane)
    per_column[...] = jnp.zeros_like(per_column)

    def pairs(left_ref, first, right_ref):
        for i in range(half):
            left = left_ref[(first + i) * wide : (first + i + 1) * wide, :]
            for j in range(blocks):
                values = exponentials(left, right_ref[j * wide : (j + 1) * wide, :])
                per_column[j] += over_rows(values)
                per_lane[i] += over_lane_groups(values)
        for k in range(blocks):
            sums_ref[k] = jnp.zeros_like(sums_ref[k])
            sums_ref[blocks + k] = per_column[k].sum(0, keepdims=True)
        for i in range(half):
            sums_ref[first + i] = per_lane[i].T.sum(0, keepdims=True)

    @pl.when(core == 0)
    def _():
        pairs(mine_ref, 0, sibling_ref)

    @pl.when(core == 1)
    def _():
        pairs(sibling_ref, half, mine_ref)

    for k in range(blocks):
        sums_ref[blocks * core + k] += same_ref[k]


def weight_kernel(
    core_ref, start_ref, side_ref, sums_ref, mine_ref, sibling_ref, keep_ref, send_ref, total
):
    core = core_ref[0]
    wide = sums_ref.shape[2]
    blocks = sums_ref.shape[0] // 2
    rows = side_ref.shape[0]
    own = mine_ref[:rows, :]
    mine_sums = sums_ref[blocks * core][:, :rows]
    inverse_own = 1.0 / jnp.broadcast_to(mine_sums, (128, rows)).T[:, :1]
    partner = side_ref[:, 0:1].astype(jnp.int32)
    lanes = lax.broadcasted_iota(jnp.int32, (1, wide), 1)
    for part, ref in enumerate((mine_ref, sibling_ref)):
        for k in range(blocks):
            which = core if part == 0 else 1 - core
            right = ref[k * wide : (k + 1) * wide, :]
            inverse = 1.0 / sums_ref[blocks * which + k]
            values = exponentials(own, right) * (inverse_own + inverse)
            if part == 0 and k == 0:
                row_ids = lax.broadcasted_iota(jnp.int32, values.shape, 0)
                column_ids = lax.broadcasted_iota(jnp.int32, values.shape, 1)
                values = jnp.where(row_ids == column_ids, 0.0, values)
            first = start_ref[part * blocks * 2 + 2 * k]
            second = start_ref[part * blocks * 2 + 2 * k + 1]
            columns = lanes + jnp.where(lanes < rows, first, second - rows)
            values = jnp.where(columns == partner, values - 2.0, values)
            product = jnp.dot(
                values.astype(jnp.bfloat16), right, preferred_element_type=jnp.float32
            )
            if part == 0 and k == 0:
                total[...] = product
            else:
                total[...] += product
    grad_unit = total[...] * (1.0 / softness_factor)
    unit = own.astype(jnp.float32)
    along = jnp.sum(unit * grad_unit, axis=1, keepdims=True)
    grad_hidden = ((grad_unit - unit * along) * side_ref[:, 1:2]).astype(jnp.bfloat16)
    middle = grad_hidden.shape[1] // 2
    first, second = grad_hidden[:, :middle], grad_hidden[:, middle:]
    keep_ref[...] = jnp.where(core == 0, first, second)
    send_ref[...] = jnp.where(core == 0, second, first)


VMEM = pl.BlockSpec(memory_space=pltpu.VMEM)
SMEM = pl.BlockSpec(memory_space=pltpu.SMEM)


def kernel_call(body, outputs, in_specs, scratch, flops, name):
    return pl.pallas_call(
        body,
        out_shape=outputs,
        in_specs=in_specs,
        out_specs=jax.tree.map(lambda unused: VMEM, outputs),
        scratch_shapes=scratch,
        compiler_params=pltpu.CompilerParams(vmem_limit_bytes=40 * 1024 * 1024),
        cost_estimate=pl.CostEstimate(
            flops=flops, bytes_accessed=2_000_000, transcendentals=100_000
        ),
        name=name,
    )


def on_device(features, head_weight, partner):
    rows = features.shape[0]
    channels, width = head_weight.shape
    y = lax.axis_index("y2") * 4 + lax.axis_index("y1") * 2 + lax.axis_index("y0")
    core = lax.axis_index("c")
    core_scalar = core.reshape(1).astype(jnp.int32)

    hidden = jnp.dot(features, head_weight, preferred_element_type=jnp.float32)
    row_norm = jnp.sqrt(jnp.sum(hidden * hidden, axis=1, keepdims=True) + 1e-05)
    unit = (hidden / row_norm).astype(jnp.bfloat16)
    side = jnp.stack([partner.astype(jnp.float32), 1.0 / row_norm[:, 0]])

    sign = jnp.where(core == 0, -1, 1)
    same_core = lax.ppermute(unit, BITS, TO_NEXT_SAME)
    other_core = lax.ppermute(unit, BITS, TO_NEXT_OTHER)
    own = lax.ppermute(unit, BITS, TO_HOST)
    side_here = lax.ppermute(side, BITS, TO_HOST)
    pieces, places = [own], [y * 2 + core]
    for distance in range(1, 5):
        place_there = (y + sign * distance) % Y * 2
        if distance > 1:
            same_core = lax.ppermute(same_core, (*YBITS, "c"), ROUND)
        if distance == 4:
            same_core, side_here = lax.optimization_barrier((same_core, side_here))
        pieces.append(same_core)
        places.append(place_there + core)
        if distance == 4:
            break
        if distance == 3:
            later, unused = lax.optimization_barrier((features, same_core))
            rows_here = lax.ppermute(later, BITS, TO_HOST)
            rows_beside = lax.ppermute(later, BITS, TO_SIBLING)
        if distance > 1:
            other_core = lax.ppermute(other_core, (*YBITS, "c"), ROUND)
        pieces.append(other_core)
        places.append(place_there + 1 - core)
    sign, core_there = -sign, 1 - core
    places.append(y * 2 + core_there)
    for distance in range(1, 5):
        place_there = (y + sign * distance) % Y * 2
        there = [place_there + core_there, place_there + 1 - core_there]
        places += there[: 1 if distance == 4 else 2]
    mine = jnp.concatenate(pieces)
    starts = jnp.stack(places).astype(jnp.int32) * rows

    sibling = lax.ppermute(mine, "c", OTHER_CORE)
    lanes = pltpu.VMEM((4, 512, 128), jnp.float32)
    columns = pltpu.VMEM((4, 8, 512), jnp.float32)
    same = kernel_call(
        same_block_kernel,
        jax.ShapeDtypeStruct((4, 1, 512), jnp.float32),
        [VMEM],
        [lanes, columns],
        3_000_000_000,
        "same_parity_sums",
    )(mine)
    sums = kernel_call(
        cross_block_kernel,
        jax.ShapeDtypeStruct((8, 1, 512), jnp.float32),
        [SMEM, VMEM, VMEM, VMEM],
        [lanes, columns],
        2_000_000_000,
        "cross_parity_sums",
    )(core_scalar, mine, sibling, same)
    sums = lax.psum(sums, "c")
    piece = jax.ShapeDtypeStruct((rows, width // 2), jnp.bfloat16)
    kept, sent = kernel_call(
        weight_kernel,
        (piece, piece),
        [SMEM, SMEM, VMEM, VMEM, VMEM, VMEM],
        [pltpu.VMEM((rows, width), jnp.float32)],
        2_000_000_000,
        "weights",
    )(core_scalar, starts, side_here.T, sums, mine, sibling)
    beside = lax.ppermute(sent, "c", OTHER_CORE)

    def contract(left, right):
        return lax.dot_general(
            left, right, (((0,), (0,)), ((), ())), preferred_element_type=jnp.float32
        )

    partial = (contract(rows_here, kept) + contract(rows_beside, beside)).astype(jnp.bfloat16)
    tiles = partial.reshape(channels // 8, 8, 2, 128).transpose(0, 2, 1, 3).reshape(512, 8, 128)
    received = lax.all_to_all(tiles, BITS, 0, 0).reshape(256, 2, 8, 128)
    fragment = received.astype(jnp.float32).sum(0).astype(jnp.bfloat16)
    spread = lax.all_to_all(jnp.broadcast_to(fragment[None], (32, 2, 8, 128)), BITS[4:], 0, 0)
    gradient = spread.reshape(16, 2, 2, 8, 128).transpose(0, 3, 2, 1, 4).reshape(128, width)
    gradient = gradient.astype(jnp.float32)
    squares = jnp.sum(gradient * gradient)
    squares = lax.all_to_all(
        jnp.broadcast_to(squares, (16, 128)), ("y2", "y1", "y0", "xh"), 0, 0
    )
    total = jnp.sum(squares[:, 0])
    return gradient * lax.rsqrt(total / (channels * width) + 1e-06)


def solution(mesh):
    bits = Mesh(mesh.devices.reshape((2,) * len(BITS)), BITS)
    images = P(("xl", "z2", "z1", "z0", "c", "y2", "y1", "y0", "xh"))
    return jax.shard_map(
        on_device,
        mesh=bits,
        in_specs=(P(*images, None), P(), images),
        out_specs=P(("y2", "y1", "y0", "xh"), None),
        check_vma=False,
    )
```

```python
import itertools

import jax
import jax.numpy as jnp
from jax import lax
from jax.experimental import pallas as pl
from jax.experimental.pallas import tpu as pltpu
from jax.sharding import Mesh
from jax.sharding import PartitionSpec as P

softness_factor = 0.05
EXP2_SCALE = 1.4426950408889634 / softness_factor
Y = 8
BITS = ("y2", "y1", "y0", "xh", "xl", "z2", "z1", "z0", "c")
YBITS = BITS[:3]
OTHER_CORE = [(0, 1), (1, 0)]


def moves(other_core, step):
    pairs = []
    for y, xh, xl, z, core in itertools.product(range(Y), range(2), range(2), range(8), range(2)):
        there = xh ^ other_core
        y_there = (y + step * (1, -1)[there]) % Y
        pairs.append((place(y, xh, xl, z, core), place(y_there, core ^ xl, 1 - xl, z, there)))
    return pairs


def place(y, xh, xl, z, core):
    return (((y * 2 + xh) * 2 + xl) * 8 + z) * 2 + core


TO_HOST, TO_SIBLING = moves(0, 0), moves(1, 0)
TO_NEXT_SAME, TO_NEXT_OTHER = moves(0, 1), moves(1, 1)
ROUND = [(2 * y + c, 2 * ((y + (1, -1)[c]) % Y) + c) for y in range(Y) for c in range(2)]


def exponentials(left, right):
    scores = lax.dot_general(
        left, right, (((1,), (1,)), ((), ())), preferred_element_type=jnp.float32
    )
    return jnp.exp2(scores * EXP2_SCALE)


def over_rows(values):
    return values.reshape(values.shape[0] // 8, 8, values.shape[1]).sum(0)


def over_lane_groups(values):
    return sum(values[:, k : k + 128] for k in range(0, values.shape[1], 128))


def same_block_kernel(mine_ref, sums_ref, per_lane, per_column):
    blocks, wide = per_lane.shape[0], per_lane.shape[1]
    per_lane[...] = jnp.zeros_like(per_lane)
    per_column[...] = jnp.zeros_like(per_column)
    for i in range(blocks):
        left = mine_ref[i * wide : (i + 1) * wide, :]
        values = exponentials(left, left)
        rows = lax.broadcasted_iota(jnp.int32, values.shape, 0)
        columns = lax.broadcasted_iota(jnp.int32, values.shape, 1)
        per_column[i] += over_rows(jnp.where(rows == columns, 0.0, values))
        for j in range(i + 1, blocks):
            values = exponentials(left, mine_ref[j * wide : (j + 1) * wide, :])
            per_column[j] += over_rows(values)
            per_lane[i] += over_lane_groups(values)
    for i in range(blocks):
        sums_ref[i] = per_column[i].sum(0, keepdims=True) + per_lane[i].T.sum(0, keepdims=True)


def cross_block_kernel(core_ref, mine_ref, sibling_ref, same_ref, sums_ref, per_lane, per_column):
    core = core_ref[0]
    blocks, wide = per_column.shape[0], per_column.shape[2]
    half = blocks // 2
    per_lane[...] = jnp.zeros_like(per_lane)
    per_column[...] = jnp.zeros_like(per_column)

    def pairs(left_ref, first, right_ref):
        for i in range(half):
            left = left_ref[(first + i) * wide : (first + i + 1) * wide, :]
            for j in range(blocks):
                values = exponentials(left, right_ref[j * wide : (j + 1) * wide, :])
                per_column[j] += over_rows(values)
                per_lane[i] += over_lane_groups(values)
        for k in range(blocks):
            sums_ref[k] = jnp.zeros_like(sums_ref[k])
            sums_ref[blocks + k] = per_column[k].sum(0, keepdims=True)
        for i in range(half):
            sums_ref[first + i] = per_lane[i].T.sum(0, keepdims=True)

    @pl.when(core == 0)
    def _():
        pairs(mine_ref, 0, sibling_ref)

    @pl.when(core == 1)
    def _():
        pairs(sibling_ref, half, mine_ref)

    for k in range(blocks):
        sums_ref[blocks * core + k] += same_ref[k]


def weight_kernel(
    core_ref, start_ref, side_ref, sums_ref, mine_ref, sibling_ref, keep_ref, send_ref, total
):
    core = core_ref[0]
    wide = sums_ref.shape[2]
    blocks = sums_ref.shape[0] // 2
    rows = side_ref.shape[0]
    own = mine_ref[:rows, :]
    mine_sums = sums_ref[blocks * core][:, :rows]
    inverse_own = 1.0 / jnp.broadcast_to(mine_sums, (128, rows)).T[:, :1]
    partner = side_ref[:, 0:1].astype(jnp.int32)
    lanes = lax.broadcasted_iota(jnp.int32, (1, wide), 1)
    for part, ref in enumerate((mine_ref, sibling_ref)):
        for k in range(blocks):
            which = core if part == 0 else 1 - core
            right = ref[k * wide : (k + 1) * wide, :]
            inverse = 1.0 / sums_ref[blocks * which + k]
            values = exponentials(own, right) * (inverse_own + inverse)
            if part == 0 and k == 0:
                row_ids = lax.broadcasted_iota(jnp.int32, values.shape, 0)
                column_ids = lax.broadcasted_iota(jnp.int32, values.shape, 1)
                values = jnp.where(row_ids == column_ids, 0.0, values)
            first = start_ref[part * blocks * 2 + 2 * k]
            second = start_ref[part * blocks * 2 + 2 * k + 1]
            columns = lanes + jnp.where(lanes < rows, first, second - rows)
            values = jnp.where(columns == partner, values - 2.0, values)
            product = jnp.dot(
                values.astype(jnp.bfloat16), right, preferred_element_type=jnp.float32
            )
            if part == 0 and k == 0:
                total[...] = product
            else:
                total[...] += product
    grad_unit = total[...] * (1.0 / softness_factor)
    unit = own.astype(jnp.float32)
    along = jnp.sum(unit * grad_unit, axis=1, keepdims=True)
    grad_hidden = ((grad_unit - unit * along) * side_ref[:, 1:2]).astype(jnp.bfloat16)
    middle = grad_hidden.shape[1] // 2
    first, second = grad_hidden[:, :middle], grad_hidden[:, middle:]
    keep_ref[...] = jnp.where(core == 0, first, second)
    send_ref[...] = jnp.where(core == 0, second, first)


VMEM = pl.BlockSpec(memory_space=pltpu.VMEM)
SMEM = pl.BlockSpec(memory_space=pltpu.SMEM)


def kernel_call(body, outputs, in_specs, scratch, flops, name):
    return pl.pallas_call(
        body,
        out_shape=outputs,
        in_specs=in_specs,
        out_specs=jax.tree.map(lambda unused: VMEM, outputs),
        scratch_shapes=scratch,
        compiler_params=pltpu.CompilerParams(vmem_limit_bytes=40 * 1024 * 1024),
        cost_estimate=pl.CostEstimate(
            flops=flops, bytes_accessed=2_000_000, transcendentals=100_000
        ),
        name=name,
    )


def on_device(features, head_weight, partner):
    rows = features.shape[0]
    channels, width = head_weight.shape
    y = lax.axis_index("y2") * 4 + lax.axis_index("y1") * 2 + lax.axis_index("y0")
    core = lax.axis_index("c")
    core_scalar = core.reshape(1).astype(jnp.int32)

    hidden = jnp.dot(features, head_weight, preferred_element_type=jnp.float32)
    row_norm = jnp.sqrt(jnp.sum(hidden * hidden, axis=1, keepdims=True) + 1e-05)
    unit = (hidden / row_norm).astype(jnp.bfloat16)
    side = jnp.stack([partner.astype(jnp.float32), 1.0 / row_norm[:, 0]])

    sign = jnp.where(core == 0, -1, 1)
    same_core = lax.ppermute(unit, BITS, TO_NEXT_SAME)
    other_core = lax.ppermute(unit, BITS, TO_NEXT_OTHER)
    own = lax.ppermute(unit, BITS, TO_HOST)
    side_here = lax.ppermute(side, BITS, TO_HOST)
    pieces, places = [own], [y * 2 + core]
    for distance in range(1, 5):
        place_there = (y + sign * distance) % Y * 2
        if distance > 1:
            same_core = lax.ppermute(same_core, (*YBITS, "c"), ROUND)
        if distance == 4:
            same_core, side_here = lax.optimization_barrier((same_core, side_here))
        pieces.append(same_core)
        places.append(place_there + core)
        if distance == 4:
            break
        if distance == 3:
            later, unused = lax.optimization_barrier((features, same_core))
            rows_here = lax.ppermute(later, BITS, TO_HOST)
            rows_beside = lax.ppermute(later, BITS, TO_SIBLING)
        if distance > 1:
            other_core = lax.ppermute(other_core, (*YBITS, "c"), ROUND)
        pieces.append(other_core)
        places.append(place_there + 1 - core)
    sign, core_there = -sign, 1 - core
    places.append(y * 2 + core_there)
    for distance in range(1, 5):
        place_there = (y + sign * distance) % Y * 2
        there = [place_there + core_there, place_there + 1 - core_there]
        places += there[: 1 if distance == 4 else 2]
    mine = jnp.concatenate(pieces)
    starts = jnp.stack(places).astype(jnp.int32) * rows

    sibling = lax.ppermute(mine, "c", OTHER_CORE)
    lanes = pltpu.VMEM((4, 512, 128), jnp.float32)
    columns = pltpu.VMEM((4, 8, 512), jnp.float32)
    same = kernel_call(
        same_block_kernel,
        jax.ShapeDtypeStruct((4, 1, 512), jnp.float32),
        [VMEM],
        [lanes, columns],
        3_000_000_000,
        "same_parity_sums",
    )(mine)
    sums = kernel_call(
        cross_block_kernel,
        jax.ShapeDtypeStruct((8, 1, 512), jnp.float32),
        [SMEM, VMEM, VMEM, VMEM],
        [lanes, columns],
        2_000_000_000,
        "cross_parity_sums",
    )(core_scalar, mine, sibling, same)
    sums = lax.psum(sums, "c")
    piece = jax.ShapeDtypeStruct((rows, width // 2), jnp.bfloat16)
    kept, sent = kernel_call(
        weight_kernel,
        (piece, piece),
        [SMEM, SMEM, VMEM, VMEM, VMEM, VMEM],
        [pltpu.VMEM((rows, width), jnp.float32)],
        2_000_000_000,
        "weights",
    )(core_scalar, starts, side_here.T, sums, mine, sibling)
    beside = lax.ppermute(sent, "c", OTHER_CORE)

    def contract(left, right):
        return lax.dot_general(
            left, right, (((0,), (0,)), ((), ())), preferred_element_type=jnp.float32
        )

    partial = (contract(rows_here, kept) + contract(rows_beside, beside)).astype(jnp.bfloat16)
    tiles = partial.reshape(4, 2, 2, 2, 4, 2, 8, 256)
    tiles = tiles.transpose(1, 3, 5, 0, 2, 4, 6, 7).reshape(8, 32 * 8, 256)
    received = lax.all_to_all(tiles, ("y0", "xl", "z0"), 0, 0)
    near_sum = received.astype(jnp.float32).sum(0).astype(jnp.bfloat16).reshape(32, 8, 256)
    received = lax.all_to_all(near_sum, ("y2", "y1", "xh", "z2", "z1"), 0, 0)
    fragment = received.astype(jnp.float32).sum(0).astype(jnp.bfloat16)
    spread = lax.all_to_all(jnp.broadcast_to(fragment[None], (32, 8, 256)), BITS[4:], 0, 0)
    gradient = spread.reshape(16, 2, 8, 256).transpose(0, 2, 1, 3).reshape(128, width)
    gradient = gradient.astype(jnp.float32)
    squares = jnp.sum(gradient * gradient)
    squares = lax.all_to_all(
        jnp.broadcast_to(squares, (16, 128)), ("y2", "y1", "y0", "xh"), 0, 0
    )
    total = jnp.sum(squares[:, 0])
    return gradient * lax.rsqrt(total / (channels * width) + 1e-06)


def solution(mesh):
    bits = Mesh(mesh.devices.reshape((2,) * len(BITS)), BITS)
    images = P(("xl", "z2", "z1", "z0", "c", "y2", "y1", "y0", "xh"))
    return jax.shard_map(
        on_device,
        mesh=bits,
        in_specs=(P(*images, None), P(), images),
        out_specs=P(("y2", "y1", "y0", "xh"), None),
        check_vma=False,
    )
```

```python
import itertools

import jax
import jax.numpy as jnp
from jax import lax
from jax.experimental import pallas as pl
from jax.experimental.pallas import tpu as pltpu
from jax.sharding import Mesh
from jax.sharding import PartitionSpec as P

softness_factor = 0.05
EXP2_SCALE = 1.4426950408889634 / softness_factor
Y = 8
BITS = ("y2", "y1", "y0", "xh", "xl", "z2", "z1", "z0", "c")
YBITS = BITS[:3]
OTHER_CORE = [(0, 1), (1, 0)]


def moves(other_core, step):
    pairs = []
    for y, xh, xl, z, core in itertools.product(range(Y), range(2), range(2), range(8), range(2)):
        there = xh ^ other_core
        y_there = (y + step * (1, -1)[there]) % Y
        pairs.append((place(y, xh, xl, z, core), place(y_there, core ^ xl, 1 - xl, z, there)))
    return pairs


def place(y, xh, xl, z, core):
    return (((y * 2 + xh) * 2 + xl) * 8 + z) * 2 + core


TO_HOST, TO_SIBLING = moves(0, 0), moves(1, 0)
TO_NEXT_SAME, TO_NEXT_OTHER = moves(0, 1), moves(1, 1)
ROUND = [(2 * y + c, 2 * ((y + (1, -1)[c]) % Y) + c) for y in range(Y) for c in range(2)]


def exponentials(left, right):
    scores = lax.dot_general(
        left, right, (((1,), (1,)), ((), ())), preferred_element_type=jnp.float32
    )
    return jnp.exp2(scores * EXP2_SCALE)


def over_rows(values):
    return values.reshape(values.shape[0] // 8, 8, values.shape[1]).sum(0)


def over_lane_groups(values):
    return sum(values[:, k : k + 128] for k in range(0, values.shape[1], 128))


def row_totals(per_lane):
    ones = jnp.ones((8, per_lane.shape[1]), jnp.float32)
    totals = lax.dot_general(
        ones,
        per_lane,
        (((1,), (1,)), ((), ())),
        precision=lax.Precision.HIGHEST,
        preferred_element_type=jnp.float32,
    )
    return totals[0:1, :]


def without_self(values):
    rows = lax.broadcasted_iota(jnp.int32, values.shape, 0)
    columns = lax.broadcasted_iota(jnp.int32, values.shape, 1)
    return jnp.where(rows == columns, 0.0, values)


def early_sums_kernel(*refs):
    pieces, (sums_ref, per_lane, per_column) = refs[:-3], refs[-3:]
    rows = per_lane.shape[1]
    per_lane[...] = jnp.zeros_like(per_lane)
    for i, piece in enumerate(pieces):
        left = piece[...]
        own = over_rows(without_self(exponentials(left, left)))
        per_column[i] = own if i == 0 else per_column[i] + own
        for j in range(i + 1, len(pieces)):
            values = exponentials(left, pieces[j][...])
            column = over_rows(values)
            per_column[j] = column if i == 0 else per_column[j] + column
            per_lane[i] += over_lane_groups(values)
    for i in range(len(pieces)):
        total = per_column[i].sum(0, keepdims=True) + row_totals(per_lane[i])
        sums_ref[i // 2, :, i % 2 * rows : (i % 2 + 1) * rows] = total


def late_sums_kernel(mine_ref, early_ref, sums_ref):
    blocks, wide = sums_ref.shape[0], sums_ref.shape[2]
    last = mine_ref[(blocks - 1) * wide :, :]
    column = over_rows(without_self(exponentials(last, last)))
    for i in range(blocks - 1):
        values = exponentials(mine_ref[i * wide : (i + 1) * wide, :], last)
        column += over_rows(values)
        sums_ref[i] = early_ref[i] + row_totals(over_lane_groups(values))
    sums_ref[blocks - 1] = column.sum(0, keepdims=True)


def cross_block_kernel(core_ref, mine_ref, sibling_ref, same_ref, sums_ref, per_lane, per_column):
    core = core_ref[0]
    blocks, wide = per_column.shape[0], per_column.shape[2]
    half = blocks // 2
    per_lane[...] = jnp.zeros_like(per_lane)
    per_column[...] = jnp.zeros_like(per_column)

    def pairs(left_ref, first, right_ref):
        for i in range(half):
            left = left_ref[(first + i) * wide : (first + i + 1) * wide, :]
            for j in range(blocks):
                values = exponentials(left, right_ref[j * wide : (j + 1) * wide, :])
                per_column[j] += over_rows(values)
                per_lane[i] += over_lane_groups(values)
        for k in range(blocks):
            sums_ref[k] = jnp.zeros_like(sums_ref[k])
            sums_ref[blocks + k] = per_column[k].sum(0, keepdims=True)
        for i in range(half):
            sums_ref[first + i] = row_totals(per_lane[i])

    @pl.when(core == 0)
    def _():
        pairs(mine_ref, 0, sibling_ref)

    @pl.when(core == 1)
    def _():
        pairs(sibling_ref, half, mine_ref)

    for k in range(blocks):
        sums_ref[blocks * core + k] += same_ref[k]


def weight_kernel(
    core_ref, start_ref, side_ref, sums_ref, mine_ref, sibling_ref, keep_ref, send_ref, weights
):
    core = core_ref[0]
    wide = sums_ref.shape[2]
    blocks = sums_ref.shape[0] // 2
    rows = side_ref.shape[0]
    own = mine_ref[:rows, :]
    mine_sums = sums_ref[blocks * core][:, :rows]
    inverse_own = 1.0 / jnp.broadcast_to(mine_sums, (128, rows)).T[:, :1]
    partner = side_ref[:, 0:1].astype(jnp.int32)
    lanes = lax.broadcasted_iota(jnp.int32, (1, wide), 1)
    for part, ref in enumerate((mine_ref, sibling_ref)):
        for k in range(blocks):
            which = core if part == 0 else 1 - core
            right = ref[k * wide : (k + 1) * wide, :]
            inverse = 1.0 / sums_ref[blocks * which + k]
            values = exponentials(own, right)
            if part == 0 and k == 0:
                values = without_self(values)
            first = start_ref[part * blocks * 2 + 2 * k]
            second = start_ref[part * blocks * 2 + 2 * k + 1]
            columns = lanes + jnp.where(lanes < rows, first, second - rows)
            target = jnp.where(columns == partner, 1.0, 0.0)
            place_here = slice(k * wide, (k + 1) * wide)
            weights[part, :rows, place_here] = (values * inverse_own - target).astype(jnp.bfloat16)
            weights[part, rows:, place_here] = (values * inverse - target).astype(jnp.bfloat16)
    total = jnp.dot(weights[0], mine_ref[...], preferred_element_type=jnp.float32)
    total += jnp.dot(weights[1], sibling_ref[...], preferred_element_type=jnp.float32)
    grad_unit = (total[:rows] + total[rows:]) * (1.0 / softness_factor)
    unit = own.astype(jnp.float32)
    along = jnp.sum(unit * grad_unit, axis=1, keepdims=True)
    grad_hidden = ((grad_unit - unit * along) * side_ref[:, 1:2]).astype(jnp.bfloat16)
    middle = grad_hidden.shape[1] // 2
    first, second = grad_hidden[:, :middle], grad_hidden[:, middle:]
    keep_ref[...] = jnp.where(core == 0, first, second)
    send_ref[...] = jnp.where(core == 0, second, first)


VMEM = pl.BlockSpec(memory_space=pltpu.VMEM)
SMEM = pl.BlockSpec(memory_space=pltpu.SMEM)


def kernel_call(body, outputs, in_specs, scratch, flops, name):
    return pl.pallas_call(
        body,
        out_shape=outputs,
        in_specs=in_specs,
        out_specs=jax.tree.map(lambda unused: VMEM, outputs),
        scratch_shapes=scratch,
        compiler_params=pltpu.CompilerParams(vmem_limit_bytes=40 * 1024 * 1024),
        cost_estimate=pl.CostEstimate(
            flops=flops, bytes_accessed=2_000_000, transcendentals=100_000
        ),
        name=name,
    )


def on_device(features, head_weight, partner):
    rows = features.shape[0]
    channels, width = head_weight.shape
    y = lax.axis_index("y2") * 4 + lax.axis_index("y1") * 2 + lax.axis_index("y0")
    core = lax.axis_index("c")
    core_scalar = core.reshape(1).astype(jnp.int32)

    hidden = jnp.dot(features, head_weight, preferred_element_type=jnp.float32)
    row_norm = jnp.sqrt(jnp.sum(hidden * hidden, axis=1, keepdims=True) + 1e-05)
    unit = (hidden / row_norm).astype(jnp.bfloat16)
    side = jnp.stack([partner.astype(jnp.float32), 1.0 / row_norm[:, 0]])

    sign = jnp.where(core == 0, -1, 1)
    same_core = lax.ppermute(unit, BITS, TO_NEXT_SAME)
    other_core = lax.ppermute(unit, BITS, TO_NEXT_OTHER)
    own = lax.ppermute(unit, BITS, TO_HOST)
    side_here = lax.ppermute(side, BITS, TO_HOST)
    pieces, places = [own], [y * 2 + core]
    for distance in range(1, 5):
        place_there = (y + sign * distance) % Y * 2
        if distance > 1:
            same_core = lax.ppermute(same_core, (*YBITS, "c"), ROUND)
        if distance == 4:
            early = kernel_call(
                early_sums_kernel,
                jax.ShapeDtypeStruct((3, 1, 512), jnp.float32),
                [VMEM] * 6,
                [pltpu.VMEM((6, rows, 128), jnp.float32), pltpu.VMEM((6, 8, rows), jnp.float32)],
                2_000_000_000,
                "early_sums",
            )(*pieces[:6])
            same_core, side_here, early = lax.optimization_barrier((same_core, side_here, early))
        pieces.append(same_core)
        places.append(place_there + core)
        if distance == 4:
            break
        if distance == 3:
            later, unused = lax.optimization_barrier((features, same_core))
            rows_here = lax.ppermute(later, BITS, TO_HOST)
            rows_beside = lax.ppermute(later, BITS, TO_SIBLING)
        if distance > 1:
            other_core = lax.ppermute(other_core, (*YBITS, "c"), ROUND)
        pieces.append(other_core)
        places.append(place_there + 1 - core)
    sign, core_there = -sign, 1 - core
    places.append(y * 2 + core_there)
    for distance in range(1, 5):
        place_there = (y + sign * distance) % Y * 2
        there = [place_there + core_there, place_there + 1 - core_there]
        places += there[: 1 if distance == 4 else 2]
    mine = jnp.concatenate(pieces)
    starts = jnp.stack(places).astype(jnp.int32) * rows

    sibling = lax.ppermute(mine, "c", OTHER_CORE)
    lanes = pltpu.VMEM((4, 512, 128), jnp.float32)
    columns = pltpu.VMEM((4, 8, 512), jnp.float32)
    same = kernel_call(
        late_sums_kernel,
        jax.ShapeDtypeStruct((4, 1, 512), jnp.float32),
        [VMEM, VMEM],
        [],
        1_000_000_000,
        "late_sums",
    )(mine, early)
    sums = kernel_call(
        cross_block_kernel,
        jax.ShapeDtypeStruct((8, 1, 512), jnp.float32),
        [SMEM, VMEM, VMEM, VMEM],
        [lanes, columns],
        2_000_000_000,
        "cross_parity_sums",
    )(core_scalar, mine, sibling, same)
    sums = lax.psum(sums, "c")
    piece = jax.ShapeDtypeStruct((rows, width // 2), jnp.bfloat16)
    kept, sent = kernel_call(
        weight_kernel,
        (piece, piece),
        [SMEM, SMEM, VMEM, VMEM, VMEM, VMEM],
        [pltpu.VMEM((2, 2 * rows, 8 * rows), jnp.bfloat16)],
        2_000_000_000,
        "weights",
    )(core_scalar, starts, side_here.T, sums, mine, sibling)
    beside = lax.ppermute(sent, "c", OTHER_CORE)

    def contract(left, right):
        return lax.dot_general(
            left, right, (((0,), (0,)), ((), ())), preferred_element_type=jnp.float32
        )

    partial = (contract(rows_here, kept) + contract(rows_beside, beside)).astype(jnp.bfloat16)
    tiles = partial.reshape(4, 2, 2, 2, 4, 2, 8, 256)
    tiles = tiles.transpose(5, 3, 1, 2, 4, 0, 6, 7).reshape(16, 16 * 8, 256)
    received = lax.all_to_all(tiles, ("z0", "xl", "y0", "xh"), 0, 0)
    near_sum = received.astype(jnp.float32).sum(0).astype(jnp.bfloat16).reshape(16, 8, 256)
    received = lax.all_to_all(near_sum, ("z2", "z1", "y2", "y1"), 0, 0)
    fragment = received.astype(jnp.float32).sum(0).astype(jnp.bfloat16)
    spread = lax.all_to_all(
        jnp.broadcast_to(fragment[None], (32, 8, 256)), ("c", "xl", "z2", "z1", "z0"), 0, 0
    )
    gradient = spread.reshape(2, 16, 8, 256).transpose(1, 2, 0, 3).reshape(128, width)
    gradient = gradient.astype(jnp.float32)
    squares = jnp.sum(gradient * gradient)
    squares = lax.all_to_all(
        jnp.broadcast_to(squares, (16, 128)), ("y2", "y1", "y0", "xh"), 0, 0
    )
    total = jnp.sum(squares[:, 0])
    return gradient * lax.rsqrt(total / (channels * width) + 1e-06)


def solution(mesh):
    bits = Mesh(mesh.devices.reshape((2,) * len(BITS)), BITS)
    images = P(("xl", "z2", "z1", "z0", "c", "y2", "y1", "y0", "xh"))
    return jax.shard_map(
        on_device,
        mesh=bits,
        in_specs=(P(*images, None), P(), images),
        out_specs=P(("y2", "y1", "y0", "xh"), None),
        check_vma=False,
    )
```

```python
import itertools

import jax
import jax.numpy as jnp
from jax import lax
from jax.experimental import pallas as pl
from jax.experimental.pallas import tpu as pltpu
from jax.sharding import Mesh
from jax.sharding import PartitionSpec as P

softness_factor = 0.05
EXP2_SCALE = 1.4426950408889634 / softness_factor
Y = 8
BITS = ("y2", "y1", "y0", "xh", "xl", "z2", "z1", "z0", "c")
YBITS = BITS[:3]
OTHER_CORE = [(0, 1), (1, 0)]


def moves(other_core, step):
    pairs = []
    for y, xh, xl, z, core in itertools.product(range(Y), range(2), range(2), range(8), range(2)):
        there = xh ^ other_core
        y_there = (y + step * (1, -1)[there]) % Y
        pairs.append((place(y, xh, xl, z, core), place(y_there, core ^ xl, 1 - xl, z, there)))
    return pairs


def place(y, xh, xl, z, core):
    return (((y * 2 + xh) * 2 + xl) * 8 + z) * 2 + core


TO_HOST, TO_SIBLING = moves(0, 0), moves(1, 0)
TO_NEXT_SAME, TO_NEXT_OTHER = moves(0, 1), moves(1, 1)
ROUND = [(2 * y + c, 2 * ((y + (1, -1)[c]) % Y) + c) for y in range(Y) for c in range(2)]


def exponentials(left, right):
    scores = lax.dot_general(
        left, right, (((1,), (1,)), ((), ())), preferred_element_type=jnp.float32
    )
    return jnp.exp2(scores * EXP2_SCALE)


def over_rows(values):
    return values.reshape(values.shape[0] // 8, 8, values.shape[1]).sum(0)


def over_lane_groups(values):
    return sum(values[:, k : k + 128] for k in range(0, values.shape[1], 128))


def row_totals(per_lane):
    ones = jnp.ones((8, per_lane.shape[1]), jnp.float32)
    totals = lax.dot_general(
        ones,
        per_lane,
        (((1,), (1,)), ((), ())),
        precision=lax.Precision.HIGHEST,
        preferred_element_type=jnp.float32,
    )
    return totals[0:1, :]


def without_self(values):
    rows = lax.broadcasted_iota(jnp.int32, values.shape, 0)
    columns = lax.broadcasted_iota(jnp.int32, values.shape, 1)
    return jnp.where(rows == columns, 0.0, values)


def early_sums_kernel(*refs):
    pieces, (sums_ref, per_lane, per_column) = refs[:-3], refs[-3:]
    rows = per_lane.shape[1]
    per_lane[...] = jnp.zeros_like(per_lane)
    for i, piece in enumerate(pieces):
        left = piece[...]
        own = over_rows(without_self(exponentials(left, left)))
        per_column[i] = own if i == 0 else per_column[i] + own
        for j in range(i + 1, len(pieces)):
            values = exponentials(left, pieces[j][...])
            column = over_rows(values)
            per_column[j] = column if i == 0 else per_column[j] + column
            per_lane[i] += over_lane_groups(values)
    for i in range(len(pieces)):
        total = per_column[i].sum(0, keepdims=True) + row_totals(per_lane[i])
        sums_ref[i // 2, :, i % 2 * rows : (i % 2 + 1) * rows] = total


def block_copies(source, target, semaphores, order, first):
    rows = target.shape[0] // len(order)
    copies = {}
    for position, k in enumerate(order):
        part = pl.ds(k * rows, rows)
        copies[k] = pltpu.make_async_copy(
            source.at[part], target.at[part], semaphores.at[first + position]
        )
        copies[k].start()
    return copies


def pair_sums_kernel(
    core_ref, mine_hbm, sibling_hbm, early_ref, sums_ref, mine, sibling, per_lane, per_column, semaphores
):
    core = core_ref[0]
    blocks, wide = per_column.shape[0], per_column.shape[2]
    half = blocks // 2
    mine_copies = block_copies(mine_hbm, mine, semaphores, (3, 0, 1, 2), 0)
    sibling_copies = block_copies(sibling_hbm, sibling, semaphores, (2, 3, 0, 1), blocks)
    per_lane[...] = jnp.zeros_like(per_lane)
    per_column[...] = jnp.zeros_like(per_column)

    def block(ref, k):
        return ref[k * wide : (k + 1) * wide, :]

    mine_copies[blocks - 1].wait()
    last = block(mine, blocks - 1)
    column = over_rows(without_self(exponentials(last, last)))
    same = []
    for i in range(blocks - 1):
        mine_copies[i].wait()
        values = exponentials(block(mine, i), last)
        column += over_rows(values)
        same.append(early_ref[i] + row_totals(over_lane_groups(values)))
    same.append(column.sum(0, keepdims=True))

    def pairs(left_ref, first, right_ref, columns):
        for i in range(half):
            left = block(left_ref, first + i)
            for j in columns:
                values = exponentials(left, block(right_ref, j))
                per_column[j] += over_rows(values)
                per_lane[i] += over_lane_groups(values)

    sibling_copies[2].wait()
    sibling_copies[3].wait()

    @pl.when(core == 0)
    def _():
        pairs(mine, 0, sibling, (2, 3))

    @pl.when(core == 1)
    def _():
        pairs(sibling, half, mine, (0, 1))

    sibling_copies[0].wait()
    sibling_copies[1].wait()

    @pl.when(core == 0)
    def _():
        pairs(mine, 0, sibling, (0, 1))

    @pl.when(core == 1)
    def _():
        pairs(sibling, half, mine, (2, 3))

    for k in range(blocks):
        sums_ref[k] = jnp.zeros_like(sums_ref[k])
        sums_ref[blocks + k] = per_column[k].sum(0, keepdims=True)
    for i in range(half):
        sums_ref[half * core + i] = row_totals(per_lane[i])
    for k in range(blocks):
        sums_ref[blocks * core + k] += same[k]


def weight_kernel(
    core_ref,
    start_ref,
    side_ref,
    sums_ref,
    mine_hbm,
    sibling_hbm,
    keep_ref,
    send_ref,
    mine_ref,
    sibling_ref,
    weights,
    semaphores,
):
    core = core_ref[0]
    wide = sums_ref.shape[2]
    blocks = sums_ref.shape[0] // 2
    rows = side_ref.shape[0]
    copies = (
        block_copies(mine_hbm, mine_ref, semaphores, range(blocks), 0),
        block_copies(sibling_hbm, sibling_ref, semaphores, range(blocks), blocks),
    )
    copies[0][0].wait()
    own = mine_ref[:rows, :]
    mine_sums = sums_ref[blocks * core][:, :rows]
    inverse_own = 1.0 / jnp.broadcast_to(mine_sums, (128, rows)).T[:, :1]
    partner = side_ref[:, 0:1].astype(jnp.int32)
    lanes = lax.broadcasted_iota(jnp.int32, (1, wide), 1)
    for part, ref in enumerate((mine_ref, sibling_ref)):
        for k in range(blocks):
            which = core if part == 0 else 1 - core
            if part > 0 or k > 0:
                copies[part][k].wait()
            right = ref[k * wide : (k + 1) * wide, :]
            inverse = 1.0 / sums_ref[blocks * which + k]
            values = exponentials(own, right)
            if part == 0 and k == 0:
                values = without_self(values)
            first = start_ref[part * blocks * 2 + 2 * k]
            second = start_ref[part * blocks * 2 + 2 * k + 1]
            columns = lanes + jnp.where(lanes < rows, first, second - rows)
            target = jnp.where(columns == partner, 1.0, 0.0)
            place_here = slice(k * wide, (k + 1) * wide)
            weights[part, :rows, place_here] = (values * inverse_own - target).astype(jnp.bfloat16)
            weights[part, rows:, place_here] = (values * inverse - target).astype(jnp.bfloat16)
    total = jnp.dot(weights[0], mine_ref[...], preferred_element_type=jnp.float32)
    total += jnp.dot(weights[1], sibling_ref[...], preferred_element_type=jnp.float32)
    grad_unit = (total[:rows] + total[rows:]) * (1.0 / softness_factor)
    unit = own.astype(jnp.float32)
    along = jnp.sum(unit * grad_unit, axis=1, keepdims=True)
    grad_hidden = ((grad_unit - unit * along) * side_ref[:, 1:2]).astype(jnp.bfloat16)
    middle = grad_hidden.shape[1] // 2
    first, second = grad_hidden[:, :middle], grad_hidden[:, middle:]
    keep_ref[...] = jnp.where(core == 0, first, second)
    send_ref[...] = jnp.where(core == 0, second, first)


VMEM = pl.BlockSpec(memory_space=pltpu.VMEM)
SMEM = pl.BlockSpec(memory_space=pltpu.SMEM)
ANYWHERE = pl.BlockSpec(memory_space=pl.ANY)


def kernel_call(body, outputs, in_specs, scratch, flops, name):
    return pl.pallas_call(
        body,
        out_shape=outputs,
        in_specs=in_specs,
        out_specs=jax.tree.map(lambda unused: VMEM, outputs),
        scratch_shapes=scratch,
        compiler_params=pltpu.CompilerParams(vmem_limit_bytes=24 * 1024 * 1024),
        cost_estimate=pl.CostEstimate(
            flops=flops, bytes_accessed=2_000_000, transcendentals=100_000
        ),
        name=name,
    )


def on_device(features, head_weight, partner):
    rows = features.shape[0]
    channels, width = head_weight.shape
    y = lax.axis_index("y2") * 4 + lax.axis_index("y1") * 2 + lax.axis_index("y0")
    core = lax.axis_index("c")
    core_scalar = core.reshape(1).astype(jnp.int32)

    hidden = jnp.dot(features, head_weight, preferred_element_type=jnp.float32)
    row_norm = jnp.sqrt(jnp.sum(hidden * hidden, axis=1, keepdims=True) + 1e-05)
    unit = (hidden / row_norm).astype(jnp.bfloat16)
    side = jnp.stack([partner.astype(jnp.float32), 1.0 / row_norm[:, 0]])

    sign = jnp.where(core == 0, -1, 1)
    same_core = lax.ppermute(unit, BITS, TO_NEXT_SAME)
    other_core = lax.ppermute(unit, BITS, TO_NEXT_OTHER)
    own = lax.ppermute(unit, BITS, TO_HOST)
    side_here = lax.ppermute(side, BITS, TO_HOST)
    pieces, places = [own], [y * 2 + core]
    for distance in range(1, 5):
        place_there = (y + sign * distance) % Y * 2
        if distance > 1:
            same_core = lax.ppermute(same_core, (*YBITS, "c"), ROUND)
        if distance == 4:
            early = kernel_call(
                early_sums_kernel,
                jax.ShapeDtypeStruct((3, 1, 512), jnp.float32),
                [VMEM] * 6,
                [pltpu.VMEM((6, rows, 128), jnp.float32), pltpu.VMEM((6, 8, rows), jnp.float32)],
                2_000_000_000,
                "early_sums",
            )(*pieces[:6])
            same_core, side_here, early = lax.optimization_barrier((same_core, side_here, early))
        pieces.append(same_core)
        places.append(place_there + core)
        if distance == 4:
            break
        if distance == 3:
            later, unused = lax.optimization_barrier((features, same_core))
            rows_here = lax.ppermute(later, BITS, TO_HOST)
            rows_beside = lax.ppermute(later, BITS, TO_SIBLING)
        if distance > 1:
            other_core = lax.ppermute(other_core, (*YBITS, "c"), ROUND)
        pieces.append(other_core)
        places.append(place_there + 1 - core)
    sign, core_there = -sign, 1 - core
    places.append(y * 2 + core_there)
    for distance in range(1, 5):
        place_there = (y + sign * distance) % Y * 2
        there = [place_there + core_there, place_there + 1 - core_there]
        places += there[: 1 if distance == 4 else 2]
    mine = jnp.concatenate(pieces)
    starts = jnp.stack(places).astype(jnp.int32) * rows

    sibling = lax.ppermute(mine, "c", OTHER_CORE)
    held = [pltpu.VMEM(mine.shape, jnp.bfloat16)] * 2
    semaphores = pltpu.SemaphoreType.DMA((8,))
    sums = kernel_call(
        pair_sums_kernel,
        jax.ShapeDtypeStruct((8, 1, 512), jnp.float32),
        [SMEM, ANYWHERE, ANYWHERE, VMEM],
        held
        + [
            pltpu.VMEM((2, 512, 128), jnp.float32),
            pltpu.VMEM((4, 8, 512), jnp.float32),
            semaphores,
        ],
        3_000_000_000,
        "pair_sums",
    )(core_scalar, mine, sibling, early)
    sums = lax.psum(sums, "c")
    piece = jax.ShapeDtypeStruct((rows, width // 2), jnp.bfloat16)
    kept, sent = kernel_call(
        weight_kernel,
        (piece, piece),
        [SMEM, SMEM, VMEM, VMEM, ANYWHERE, ANYWHERE],
        held + [pltpu.VMEM((2, 2 * rows, 8 * rows), jnp.bfloat16), semaphores],
        2_000_000_000,
        "weights",
    )(core_scalar, starts, side_here.T, sums, mine, sibling)
    beside = lax.ppermute(sent, "c", OTHER_CORE)

    def contract(left, right):
        return lax.dot_general(
            left, right, (((0,), (0,)), ((), ())), preferred_element_type=jnp.float32
        )

    partial = (contract(rows_here, kept) + contract(rows_beside, beside)).astype(jnp.bfloat16)
    tiles = partial.reshape(4, 2, 2, 2, 4, 2, 8, 256)
    tiles = tiles.transpose(5, 3, 1, 2, 4, 0, 6, 7).reshape(16, 16 * 8, 256)
    received = lax.all_to_all(tiles, ("z0", "xl", "y0", "xh"), 0, 0)
    near_sum = received.astype(jnp.float32).sum(0).astype(jnp.bfloat16).reshape(16, 8, 256)
    received = lax.all_to_all(near_sum, ("z2", "z1", "y2", "y1"), 0, 0)
    fragment = received.astype(jnp.float32).sum(0).astype(jnp.bfloat16)
    spread = lax.all_to_all(
        jnp.broadcast_to(fragment[None], (32, 8, 256)), ("c", "xl", "z2", "z1", "z0"), 0, 0
    )
    gradient = spread.reshape(2, 16, 8, 256).transpose(1, 2, 0, 3).reshape(128, width)
    gradient = gradient.astype(jnp.float32)
    squares = jnp.sum(gradient * gradient)
    squares = lax.all_to_all(
        jnp.broadcast_to(squares, (16, 128)), ("y2", "y1", "y0", "xh"), 0, 0
    )
    total = jnp.sum(squares[:, 0])
    return gradient * lax.rsqrt(total / (channels * width) + 1e-06)


def solution(mesh):
    bits = Mesh(mesh.devices.reshape((2,) * len(BITS)), BITS)
    images = P(("xl", "z2", "z1", "z0", "c", "y2", "y1", "y0", "xh"))
    return jax.shard_map(
        on_device,
        mesh=bits,
        in_specs=(P(*images, None), P(), images),
        out_specs=P(("y2", "y1", "y0", "xh"), None),
        check_vma=False,
    )
```

```python
import itertools

import jax
import jax.numpy as jnp
from jax import lax
from jax.experimental import pallas as pl
from jax.experimental.pallas import tpu as pltpu
from jax.sharding import Mesh
from jax.sharding import PartitionSpec as P

softness_factor = 0.05
EXP2_SCALE = 1.4426950408889634 / softness_factor
Y = 8
BITS = ("y2", "y1", "y0", "xh", "xl", "z2", "z1", "z0", "c")
YBITS = BITS[:3]
OTHER_CORE = [(0, 1), (1, 0)]


def moves(other_core, step):
    pairs = []
    for y, xh, xl, z, core in itertools.product(range(Y), range(2), range(2), range(8), range(2)):
        there = xh ^ other_core
        y_there = (y + step * (1, -1)[there]) % Y
        pairs.append((place(y, xh, xl, z, core), place(y_there, core ^ xl, 1 - xl, z, there)))
    return pairs


def place(y, xh, xl, z, core):
    return (((y * 2 + xh) * 2 + xl) * 8 + z) * 2 + core


TO_HOST, TO_SIBLING = moves(0, 0), moves(1, 0)
TO_NEXT_SAME, TO_NEXT_OTHER = moves(0, 1), moves(1, 1)
ROUND = [(2 * y + c, 2 * ((y + (1, -1)[c]) % Y) + c) for y in range(Y) for c in range(2)]


def exponentials(left, right):
    scores = lax.dot_general(
        left, right, (((1,), (1,)), ((), ())), preferred_element_type=jnp.float32
    )
    return jnp.exp2(scores * EXP2_SCALE)


def over_rows(values):
    return values.reshape(values.shape[0] // 8, 8, values.shape[1]).sum(0)


def over_lane_groups(values):
    return sum(values[:, k : k + 128] for k in range(0, values.shape[1], 128))


def row_totals(per_lane):
    ones = jnp.ones((8, per_lane.shape[1]), jnp.float32)
    totals = lax.dot_general(
        ones,
        per_lane,
        (((1,), (1,)), ((), ())),
        precision=lax.Precision.HIGHEST,
        preferred_element_type=jnp.float32,
    )
    return totals[0:1, :]


def without_self(values):
    rows = lax.broadcasted_iota(jnp.int32, values.shape, 0)
    columns = lax.broadcasted_iota(jnp.int32, values.shape, 1)
    return jnp.where(rows == columns, 0.0, values)


def early_sums_kernel(*refs):
    pieces, (sums_ref, per_lane, per_column) = refs[:-3], refs[-3:]
    rows = per_lane.shape[1]
    per_lane[...] = jnp.zeros_like(per_lane)
    for i, piece in enumerate(pieces):
        left = piece[...]
        own = over_rows(without_self(exponentials(left, left)))
        per_column[i] = own if i == 0 else per_column[i] + own
        for j in range(i + 1, len(pieces)):
            values = exponentials(left, pieces[j][...])
            column = over_rows(values)
            per_column[j] = column if i == 0 else per_column[j] + column
            per_lane[i] += over_lane_groups(values)
    for i in range(len(pieces)):
        total = per_column[i].sum(0, keepdims=True) + row_totals(per_lane[i])
        sums_ref[i // 2, :, i % 2 * rows : (i % 2 + 1) * rows] = total


def block_copies(source, target, semaphores, order, first):
    rows = target.shape[0] // len(order)
    copies = {}
    for position, k in enumerate(order):
        part = pl.ds(k * rows, rows)
        copies[k] = pltpu.make_async_copy(
            source.at[part], target.at[part], semaphores.at[first + position]
        )
        copies[k].start()
    return copies


def pair_sums_kernel(
    core_ref, mine_hbm, sibling_hbm, early_ref, sums_ref, mine, sibling, per_lane, per_column, semaphores
):
    core = core_ref[0]
    blocks, wide = per_column.shape[0], per_column.shape[2]
    half = blocks // 2
    mine_copies = block_copies(mine_hbm, mine, semaphores, (3, 0, 1, 2), 0)
    sibling_copies = block_copies(sibling_hbm, sibling, semaphores, (2, 3, 0, 1), blocks)
    per_lane[...] = jnp.zeros_like(per_lane)
    per_column[...] = jnp.zeros_like(per_column)

    def block(ref, k):
        return ref[k * wide : (k + 1) * wide, :]

    mine_copies[blocks - 1].wait()
    last = block(mine, blocks - 1)
    column = over_rows(without_self(exponentials(last, last)))
    same = []
    for i in range(blocks - 1):
        mine_copies[i].wait()
        values = exponentials(block(mine, i), last)
        column += over_rows(values)
        same.append(early_ref[i] + row_totals(over_lane_groups(values)))
    same.append(column.sum(0, keepdims=True))

    def pairs(left_ref, first, right_ref, columns):
        for i in range(half):
            left = block(left_ref, first + i)
            for j in columns:
                values = exponentials(left, block(right_ref, j))
                per_column[j] += over_rows(values)
                per_lane[i] += over_lane_groups(values)

    sibling_copies[2].wait()
    sibling_copies[3].wait()

    @pl.when(core == 0)
    def _():
        pairs(mine, 0, sibling, (2, 3))

    @pl.when(core == 1)
    def _():
        pairs(sibling, half, mine, (0, 1))

    sibling_copies[0].wait()
    sibling_copies[1].wait()

    @pl.when(core == 0)
    def _():
        pairs(mine, 0, sibling, (0, 1))

    @pl.when(core == 1)
    def _():
        pairs(sibling, half, mine, (2, 3))

    for k in range(blocks):
        sums_ref[k] = jnp.zeros_like(sums_ref[k])
        sums_ref[blocks + k] = per_column[k].sum(0, keepdims=True)
    for i in range(half):
        sums_ref[half * core + i] = row_totals(per_lane[i])
    for k in range(blocks):
        sums_ref[blocks * core + k] += same[k]


def weight_kernel(
    core_ref,
    start_ref,
    side_ref,
    sums_ref,
    mine_ref,
    sibling_ref,
    keep_ref,
    send_ref,
    weights,
):
    core = core_ref[0]
    wide = sums_ref.shape[2]
    blocks = sums_ref.shape[0] // 2
    rows = side_ref.shape[0]
    own = mine_ref[:rows, :]
    mine_sums = sums_ref[blocks * core][:, :rows]
    inverse_own = 1.0 / jnp.broadcast_to(mine_sums, (128, rows)).T[:, :1]
    partner = side_ref[:, 0:1].astype(jnp.int32)
    lanes = lax.broadcasted_iota(jnp.int32, (1, wide), 1)
    for part, ref in enumerate((mine_ref, sibling_ref)):
        for k in range(blocks):
            which = core if part == 0 else 1 - core
            right = ref[k * wide : (k + 1) * wide, :]
            inverse = 1.0 / sums_ref[blocks * which + k]
            values = exponentials(own, right)
            if part == 0 and k == 0:
                values = without_self(values)
            first = start_ref[part * blocks * 2 + 2 * k]
            second = start_ref[part * blocks * 2 + 2 * k + 1]
            columns = lanes + jnp.where(lanes < rows, first, second - rows)
            target = jnp.where(columns == partner, 1.0, 0.0)
            place_here = slice(k * wide, (k + 1) * wide)
            weights[part, :rows, place_here] = (values * inverse_own - target).astype(jnp.bfloat16)
            weights[part, rows:, place_here] = (values * inverse - target).astype(jnp.bfloat16)
    total = jnp.dot(weights[0], mine_ref[...], preferred_element_type=jnp.float32)
    total += jnp.dot(weights[1], sibling_ref[...], preferred_element_type=jnp.float32)
    grad_unit = (total[:rows] + total[rows:]) * (1.0 / softness_factor)
    unit = own.astype(jnp.float32)
    along = jnp.sum(unit * grad_unit, axis=1, keepdims=True)
    grad_hidden = ((grad_unit - unit * along) * side_ref[:, 1:2]).astype(jnp.bfloat16)
    middle = grad_hidden.shape[1] // 2
    first, second = grad_hidden[:, :middle], grad_hidden[:, middle:]
    keep_ref[...] = jnp.where(core == 0, first, second)
    send_ref[...] = jnp.where(core == 0, second, first)


def unit_kernel(features_ref, weight_ref, unit_ref, inverse_ref, hidden):
    step = pl.program_id(0)
    product = jnp.dot(features_ref[...], weight_ref[...], preferred_element_type=jnp.float32)

    @pl.when(step == 0)
    def _():
        hidden[...] = product

    @pl.when(step > 0)
    def _():
        hidden[...] += product

    @pl.when(step == pl.num_programs(0) - 1)
    def _():
        squares = hidden[...] * hidden[...]
        inverse = 1.0 / jnp.sqrt(jnp.sum(squares, axis=1, keepdims=True) + 1e-05)
        unit_ref[...] = (hidden[...] * inverse).astype(jnp.bfloat16)
        inverse_ref[...] = 1.0 / jnp.sqrt(row_totals(over_lane_groups(squares)) + 1e-05)


def units(features, head_weight):
    rows, channels = features.shape
    width = head_weight.shape[1]
    deep = channels // 4
    return pl.pallas_call(
        unit_kernel,
        grid=(4,),
        out_shape=(
            jax.ShapeDtypeStruct((rows, width), jnp.bfloat16),
            jax.ShapeDtypeStruct((1, rows), jnp.float32),
        ),
        in_specs=[
            pl.BlockSpec((rows, deep), lambda k: (0, k)),
            pl.BlockSpec((deep, width), lambda k: (k, 0)),
        ],
        out_specs=(
            pl.BlockSpec((rows, width), lambda k: (0, 0)),
            pl.BlockSpec((1, rows), lambda k: (0, 0)),
        ),
        scratch_shapes=[pltpu.VMEM((rows, width), jnp.float32)],
        compiler_params=pltpu.CompilerParams(vmem_limit_bytes=60 * 1024 * 1024),
        cost_estimate=pl.CostEstimate(
            flops=2 * rows * channels * width, bytes_accessed=3_000_000, transcendentals=0
        ),
        name="units",
    )(features, head_weight)


def squares_kernel(spread_ref, squares_ref):
    values = spread_ref[...].astype(jnp.float32)
    squares_ref[...] = jnp.full(squares_ref.shape, jnp.sum(values * values), jnp.float32)


def scale_kernel(spread_ref, squares_ref, update_ref):
    total = jnp.sum(squares_ref[...], axis=0, keepdims=True)
    entries = 16 * update_ref.shape[0] * update_ref.shape[1]
    scale = 1.0 / jnp.sqrt(total * (1.0 / entries) + 1e-06)
    for core in range(2):
        for row in range(16):
            for half in range(2):
                column = 256 * half + 128 * core
                tile = spread_ref[16 * core + row, half].astype(jnp.float32)
                update_ref[8 * row : 8 * row + 8, column : column + 128] = tile * scale


VMEM = pl.BlockSpec(memory_space=pltpu.VMEM)
SMEM = pl.BlockSpec(memory_space=pltpu.SMEM)
ANYWHERE = pl.BlockSpec(memory_space=pl.ANY)


def kernel_call(body, outputs, in_specs, scratch, flops, name):
    return pl.pallas_call(
        body,
        out_shape=outputs,
        in_specs=in_specs,
        out_specs=jax.tree.map(lambda unused: VMEM, outputs),
        scratch_shapes=scratch,
        compiler_params=pltpu.CompilerParams(vmem_limit_bytes=24 * 1024 * 1024),
        cost_estimate=pl.CostEstimate(
            flops=flops, bytes_accessed=2_000_000, transcendentals=100_000
        ),
        name=name,
    )


def on_device(features, head_weight, partner):
    rows = features.shape[0]
    channels, width = head_weight.shape
    y = lax.axis_index("y2") * 4 + lax.axis_index("y1") * 2 + lax.axis_index("y0")
    core = lax.axis_index("c")
    core_scalar = core.reshape(1).astype(jnp.int32)

    unit, inverse_norm = units(features, head_weight)
    side = jnp.concatenate([partner.astype(jnp.float32)[None], inverse_norm])

    sign = jnp.where(core == 0, -1, 1)
    same_core = lax.ppermute(unit, BITS, TO_NEXT_SAME)
    other_core = lax.ppermute(unit, BITS, TO_NEXT_OTHER)
    own = lax.ppermute(unit, BITS, TO_HOST)
    side_here = lax.ppermute(side, BITS, TO_HOST)
    pieces, places = [own], [y * 2 + core]
    for distance in range(1, 5):
        place_there = (y + sign * distance) % Y * 2
        if distance > 1:
            same_core = lax.ppermute(same_core, (*YBITS, "c"), ROUND)
        if distance == 4:
            early = kernel_call(
                early_sums_kernel,
                jax.ShapeDtypeStruct((3, 1, 512), jnp.float32),
                [VMEM] * 6,
                [pltpu.VMEM((6, rows, 128), jnp.float32), pltpu.VMEM((6, 8, rows), jnp.float32)],
                2_000_000_000,
                "early_sums",
            )(*pieces[:6])
            same_core, side_here, early = lax.optimization_barrier((same_core, side_here, early))
        pieces.append(same_core)
        places.append(place_there + core)
        if distance == 4:
            break
        if distance == 3:
            later, unused = lax.optimization_barrier((features, same_core))
            rows_here = lax.ppermute(later, BITS, TO_HOST)
            rows_beside = lax.ppermute(later, BITS, TO_SIBLING)
        if distance > 1:
            other_core = lax.ppermute(other_core, (*YBITS, "c"), ROUND)
        pieces.append(other_core)
        places.append(place_there + 1 - core)
    sign, core_there = -sign, 1 - core
    places.append(y * 2 + core_there)
    for distance in range(1, 5):
        place_there = (y + sign * distance) % Y * 2
        there = [place_there + core_there, place_there + 1 - core_there]
        places += there[: 1 if distance == 4 else 2]
    mine = jnp.concatenate(pieces)
    starts = jnp.stack(places).astype(jnp.int32) * rows

    sibling = lax.ppermute(mine, "c", OTHER_CORE)
    held = [pltpu.VMEM(mine.shape, jnp.bfloat16)] * 2
    semaphores = pltpu.SemaphoreType.DMA((8,))
    sums = kernel_call(
        pair_sums_kernel,
        jax.ShapeDtypeStruct((8, 1, 512), jnp.float32),
        [SMEM, ANYWHERE, ANYWHERE, VMEM],
        held
        + [
            pltpu.VMEM((2, 512, 128), jnp.float32),
            pltpu.VMEM((4, 8, 512), jnp.float32),
            semaphores,
        ],
        3_000_000_000,
        "pair_sums",
    )(core_scalar, mine, sibling, early)
    sums = lax.psum(sums, "c")
    piece = jax.ShapeDtypeStruct((rows, width // 2), jnp.bfloat16)
    kept, sent = kernel_call(
        weight_kernel,
        (piece, piece),
        [SMEM, SMEM, VMEM, VMEM, VMEM, VMEM],
        [pltpu.VMEM((2, 2 * rows, 8 * rows), jnp.bfloat16)],
        2_000_000_000,
        "weights",
    )(core_scalar, starts, side_here.T, sums, mine, sibling)
    beside = lax.ppermute(sent, "c", OTHER_CORE)

    def contract(left, right):
        return lax.dot_general(
            left, right, (((0,), (0,)), ((), ())), preferred_element_type=jnp.float32
        )

    partial = (contract(rows_here, kept) + contract(rows_beside, beside)).astype(jnp.bfloat16)
    tiles = partial.reshape(*(2,) * 8, 8, 2, 128)
    tiles = tiles.transpose(9, 7, 6, 5, 4, 3, 2, 1, 0, 8, 10).reshape(512, 8, 128)
    received = lax.all_to_all(tiles, BITS[::-1], 0, 0).reshape(2, 256, 8, 128)
    fragment = received.astype(jnp.float32).sum(1).astype(jnp.bfloat16)
    spread = lax.all_to_all(
        jnp.broadcast_to(fragment[None], (32, 2, 8, 128)), ("c", "xl", "z2", "z1", "z0"), 0, 0
    )
    squares = kernel_call(
        squares_kernel, jax.ShapeDtypeStruct((16, 128), jnp.float32), [VMEM], [], 100_000, "squares"
    )(spread)
    squares = lax.all_to_all(squares, ("y2", "y1", "y0", "xh"), 0, 0)
    return kernel_call(
        scale_kernel,
        jax.ShapeDtypeStruct((channels // 16, width), jnp.float32),
        [VMEM, VMEM],
        [],
        100_000,
        "scale",
    )(spread, squares)


def solution(mesh):
    bits = Mesh(mesh.devices.reshape((2,) * len(BITS)), BITS)
    images = P(("xl", "z2", "z1", "z0", "c", "y2", "y1", "y0", "xh"))
    return jax.shard_map(
        on_device,
        mesh=bits,
        in_specs=(P(*images, None), P(), images),
        out_specs=P(("y2", "y1", "y0", "xh"), None),
        check_vma=False,
    )
```

```python
import itertools

import jax
import jax.numpy as jnp
from jax import lax
from jax.experimental import pallas as pl
from jax.experimental.pallas import tpu as pltpu
from jax.sharding import Mesh
from jax.sharding import PartitionSpec as P

softness_factor = 0.05
EXP2_SCALE = 1.4426950408889634 / softness_factor
Y = 8
BITS = ("y2", "y1", "y0", "xh", "xl", "z2", "z1", "z0", "c")
YBITS = BITS[:3]
OTHER_CORE = [(0, 1), (1, 0)]


def moves(other_core, step):
    pairs = []
    for y, xh, xl, z, core in itertools.product(range(Y), range(2), range(2), range(8), range(2)):
        there = xh ^ other_core
        y_there = (y + step * (1, -1)[there]) % Y
        pairs.append((place(y, xh, xl, z, core), place(y_there, core ^ xl, 1 - xl, z, there)))
    return pairs


def place(y, xh, xl, z, core):
    return (((y * 2 + xh) * 2 + xl) * 8 + z) * 2 + core


TO_HOST, TO_SIBLING = moves(0, 0), moves(1, 0)
TO_NEXT_SAME, TO_NEXT_OTHER = moves(0, 1), moves(1, 1)
ROUND = [(2 * y + c, 2 * ((y + (1, -1)[c]) % Y) + c) for y in range(Y) for c in range(2)]


def exponentials(left, right):
    scores = lax.dot_general(
        left, right, (((1,), (1,)), ((), ())), preferred_element_type=jnp.float32
    )
    return jnp.exp2(scores * EXP2_SCALE)


def over_rows(values):
    return values.reshape(values.shape[0] // 8, 8, values.shape[1]).sum(0)


def over_lane_groups(values):
    return sum(values[:, k : k + 128] for k in range(0, values.shape[1], 128))


def row_totals(per_lane):
    ones = jnp.ones((8, per_lane.shape[1]), jnp.float32)
    totals = lax.dot_general(
        ones,
        per_lane,
        (((1,), (1,)), ((), ())),
        precision=lax.Precision.HIGHEST,
        preferred_element_type=jnp.float32,
    )
    return totals[0:1, :]


def without_self(values):
    rows = lax.broadcasted_iota(jnp.int32, values.shape, 0)
    columns = lax.broadcasted_iota(jnp.int32, values.shape, 1)
    return jnp.where(rows == columns, 0.0, values)


def early_sums_kernel(*refs):
    pieces, (sums_ref, per_lane, per_column) = refs[:-3], refs[-3:]
    rows = per_lane.shape[1]
    per_lane[...] = jnp.zeros_like(per_lane)
    for i, piece in enumerate(pieces):
        left = piece[...]
        own = over_rows(without_self(exponentials(left, left)))
        per_column[i] = own if i == 0 else per_column[i] + own
        for j in range(i + 1, len(pieces)):
            values = exponentials(left, pieces[j][...])
            column = over_rows(values)
            per_column[j] = column if i == 0 else per_column[j] + column
            per_lane[i] += over_lane_groups(values)
    for i in range(len(pieces)):
        total = per_column[i].sum(0, keepdims=True) + row_totals(per_lane[i])
        sums_ref[i // 2, :, i % 2 * rows : (i % 2 + 1) * rows] = total


def block_copies(source, target, semaphores, order, first):
    rows = target.shape[0] // len(order)
    copies = {}
    for position, k in enumerate(order):
        part = pl.ds(k * rows, rows)
        copies[k] = pltpu.make_async_copy(
            source.at[part], target.at[part], semaphores.at[first + position]
        )
        copies[k].start()
    return copies


def pair_sums_kernel(
    core_ref, mine_hbm, sibling_hbm, early_ref, sums_ref, mine, sibling, per_lane, per_column, semaphores
):
    core = core_ref[0]
    blocks, wide = per_column.shape[0], per_column.shape[2]
    half = blocks // 2
    mine_copies = block_copies(mine_hbm, mine, semaphores, (3, 0, 1, 2), 0)
    sibling_copies = block_copies(sibling_hbm, sibling, semaphores, (2, 3, 0, 1), blocks)
    per_lane[...] = jnp.zeros_like(per_lane)
    per_column[...] = jnp.zeros_like(per_column)

    def block(ref, k):
        return ref[k * wide : (k + 1) * wide, :]

    mine_copies[blocks - 1].wait()
    last = block(mine, blocks - 1)
    column = over_rows(without_self(exponentials(last, last)))
    same = []
    for i in range(blocks - 1):
        mine_copies[i].wait()
        values = exponentials(block(mine, i), last)
        column += over_rows(values)
        same.append(early_ref[i] + row_totals(over_lane_groups(values)))
    same.append(column.sum(0, keepdims=True))

    def pairs(left_ref, first, right_ref, columns):
        for i in range(half):
            left = block(left_ref, first + i)
            for j in columns:
                values = exponentials(left, block(right_ref, j))
                per_column[j] += over_rows(values)
                per_lane[i] += over_lane_groups(values)

    sibling_copies[2].wait()
    sibling_copies[3].wait()

    @pl.when(core == 0)
    def _():
        pairs(mine, 0, sibling, (2, 3))

    @pl.when(core == 1)
    def _():
        pairs(sibling, half, mine, (0, 1))

    sibling_copies[0].wait()
    sibling_copies[1].wait()

    @pl.when(core == 0)
    def _():
        pairs(mine, 0, sibling, (0, 1))

    @pl.when(core == 1)
    def _():
        pairs(sibling, half, mine, (2, 3))

    for k in range(blocks):
        sums_ref[k] = jnp.zeros_like(sums_ref[k])
        sums_ref[blocks + k] = per_column[k].sum(0, keepdims=True)
    for i in range(half):
        sums_ref[half * core + i] = row_totals(per_lane[i])
    for k in range(blocks):
        sums_ref[blocks * core + k] += same[k]


def weight_kernel(
    core_ref,
    start_ref,
    side_ref,
    sums_ref,
    mine_ref,
    sibling_ref,
    keep_ref,
    send_ref,
    weights,
):
    core = core_ref[0]
    wide = sums_ref.shape[2]
    blocks = sums_ref.shape[0] // 2
    rows = side_ref.shape[0]
    own = mine_ref[:rows, :]
    mine_sums = sums_ref[blocks * core][:, :rows]
    inverse_own = 1.0 / jnp.broadcast_to(mine_sums, (128, rows)).T[:, :1]
    partner = side_ref[:, 0:1].astype(jnp.int32)
    lanes = lax.broadcasted_iota(jnp.int32, (1, wide), 1)
    for part, ref in enumerate((mine_ref, sibling_ref)):
        for k in range(blocks):
            which = core if part == 0 else 1 - core
            right = ref[k * wide : (k + 1) * wide, :]
            inverse = 1.0 / sums_ref[blocks * which + k]
            values = exponentials(own, right)
            if part == 0 and k == 0:
                values = without_self(values)
            first = start_ref[part * blocks * 2 + 2 * k]
            second = start_ref[part * blocks * 2 + 2 * k + 1]
            columns = lanes + jnp.where(lanes < rows, first, second - rows)
            target = jnp.where(columns == partner, 1.0, 0.0)
            place_here = slice(k * wide, (k + 1) * wide)
            weights[part, :rows, place_here] = (values * inverse_own - target).astype(jnp.bfloat16)
            weights[part, rows:, place_here] = (values * inverse - target).astype(jnp.bfloat16)
    total = jnp.dot(weights[0], mine_ref[...], preferred_element_type=jnp.float32)
    total += jnp.dot(weights[1], sibling_ref[...], preferred_element_type=jnp.float32)
    grad_unit = (total[:rows] + total[rows:]) * (1.0 / softness_factor)
    unit = own.astype(jnp.float32)
    along = jnp.sum(unit * grad_unit, axis=1, keepdims=True)
    grad_hidden = ((grad_unit - unit * along) * side_ref[:, 1:2]).astype(jnp.bfloat16)
    middle = grad_hidden.shape[1] // 2
    first, second = grad_hidden[:, :middle], grad_hidden[:, middle:]
    keep_ref[...] = jnp.where(core == 0, first, second)
    send_ref[...] = jnp.where(core == 0, second, first)


def squares_kernel(spread_ref, squares_ref):
    values = spread_ref[...].astype(jnp.float32)
    squares_ref[...] = jnp.full(squares_ref.shape, jnp.sum(values * values), jnp.float32)


def scale_kernel(spread_ref, squares_ref, update_ref):
    total = jnp.sum(squares_ref[...], axis=0, keepdims=True)
    entries = 16 * update_ref.shape[0] * update_ref.shape[1]
    scale = 1.0 / jnp.sqrt(total * (1.0 / entries) + 1e-06)
    scale = jnp.concatenate([scale, scale], axis=1)
    for core in range(2):
        for row in range(16):
            tile = spread_ref[16 * core + row].astype(jnp.float32)
            update_ref[8 * row : 8 * row + 8, 256 * core : 256 * core + 256] = tile * scale


VMEM = pl.BlockSpec(memory_space=pltpu.VMEM)
SMEM = pl.BlockSpec(memory_space=pltpu.SMEM)
ANYWHERE = pl.BlockSpec(memory_space=pl.ANY)


def kernel_call(body, outputs, in_specs, scratch, flops, name):
    return pl.pallas_call(
        body,
        out_shape=outputs,
        in_specs=in_specs,
        out_specs=jax.tree.map(lambda unused: VMEM, outputs),
        scratch_shapes=scratch,
        compiler_params=pltpu.CompilerParams(vmem_limit_bytes=24 * 1024 * 1024),
        cost_estimate=pl.CostEstimate(
            flops=flops, bytes_accessed=2_000_000, transcendentals=100_000
        ),
        name=name,
    )


def on_device(features, head_weight, partner):
    rows = features.shape[0]
    channels, width = head_weight.shape
    y = lax.axis_index("y2") * 4 + lax.axis_index("y1") * 2 + lax.axis_index("y0")
    core = lax.axis_index("c")
    core_scalar = core.reshape(1).astype(jnp.int32)

    hidden = jnp.dot(features, head_weight, preferred_element_type=jnp.float32)
    row_norm = jnp.sqrt(jnp.sum(hidden * hidden, axis=1, keepdims=True) + 1e-05)
    unit = (hidden / row_norm).astype(jnp.bfloat16)
    side = jnp.stack([partner.astype(jnp.float32), 1.0 / row_norm[:, 0]])

    sign = jnp.where(core == 0, -1, 1)
    same_core = lax.ppermute(unit, BITS, TO_NEXT_SAME)
    other_core = lax.ppermute(unit, BITS, TO_NEXT_OTHER)
    own = lax.ppermute(unit, BITS, TO_HOST)
    side_here = lax.ppermute(side, BITS, TO_HOST)
    pieces, places = [own], [y * 2 + core]
    for distance in range(1, 5):
        place_there = (y + sign * distance) % Y * 2
        if distance > 1:
            same_core = lax.ppermute(same_core, (*YBITS, "c"), ROUND)
        if distance == 4:
            early = kernel_call(
                early_sums_kernel,
                jax.ShapeDtypeStruct((3, 1, 512), jnp.float32),
                [VMEM] * 6,
                [pltpu.VMEM((6, rows, 128), jnp.float32), pltpu.VMEM((6, 8, rows), jnp.float32)],
                2_000_000_000,
                "early_sums",
            )(*pieces[:6])
            same_core, side_here, early = lax.optimization_barrier((same_core, side_here, early))
        pieces.append(same_core)
        places.append(place_there + core)
        if distance == 4:
            break
        if distance == 3:
            later, unused = lax.optimization_barrier((features, same_core))
            rows_here = lax.ppermute(later, BITS, TO_HOST)
            rows_beside = lax.ppermute(later, BITS, TO_SIBLING)
        if distance > 1:
            other_core = lax.ppermute(other_core, (*YBITS, "c"), ROUND)
        pieces.append(other_core)
        places.append(place_there + 1 - core)
    sign, core_there = -sign, 1 - core
    places.append(y * 2 + core_there)
    for distance in range(1, 5):
        place_there = (y + sign * distance) % Y * 2
        there = [place_there + core_there, place_there + 1 - core_there]
        places += there[: 1 if distance == 4 else 2]
    mine = jnp.concatenate(pieces)
    starts = jnp.stack(places).astype(jnp.int32) * rows

    sibling = lax.ppermute(mine, "c", OTHER_CORE)
    held = [pltpu.VMEM(mine.shape, jnp.bfloat16)] * 2
    semaphores = pltpu.SemaphoreType.DMA((8,))
    sums = kernel_call(
        pair_sums_kernel,
        jax.ShapeDtypeStruct((8, 1, 512), jnp.float32),
        [SMEM, ANYWHERE, ANYWHERE, VMEM],
        held
        + [
            pltpu.VMEM((2, 512, 128), jnp.float32),
            pltpu.VMEM((4, 8, 512), jnp.float32),
            semaphores,
        ],
        3_000_000_000,
        "pair_sums",
    )(core_scalar, mine, sibling, early)
    sums = lax.psum(sums, "c")
    piece = jax.ShapeDtypeStruct((rows, width // 2), jnp.bfloat16)
    kept, sent = kernel_call(
        weight_kernel,
        (piece, piece),
        [SMEM, SMEM, VMEM, VMEM, VMEM, VMEM],
        [pltpu.VMEM((2, 2 * rows, 8 * rows), jnp.bfloat16)],
        2_000_000_000,
        "weights",
    )(core_scalar, starts, side_here.T, sums, mine, sibling)
    beside = lax.ppermute(sent, "c", OTHER_CORE)

    def contract(left, right):
        return lax.dot_general(
            left, right, (((0,), (0,)), ((), ())), preferred_element_type=jnp.float32
        )

    partial = (contract(rows_here, kept) + contract(rows_beside, beside)).astype(jnp.bfloat16)
    tiles = partial.reshape(4, 2, 2, 2, 4, 2, 8, 256)
    tiles = tiles.transpose(5, 3, 1, 2, 4, 0, 6, 7).reshape(16, 16 * 8, 256)
    received = lax.all_to_all(tiles, ("z0", "xl", "y0", "xh"), 0, 0)
    near_sum = received.astype(jnp.float32).sum(0).astype(jnp.bfloat16).reshape(16, 8, 256)
    received = lax.all_to_all(near_sum, ("z2", "z1", "y2", "y1"), 0, 0)
    fragment = received.astype(jnp.float32).sum(0).astype(jnp.bfloat16)
    spread = lax.all_to_all(
        jnp.broadcast_to(fragment[None], (32, 8, 256)), ("c", "xl", "z2", "z1", "z0"), 0, 0
    )
    squares = kernel_call(
        squares_kernel, jax.ShapeDtypeStruct((16, 128), jnp.float32), [VMEM], [], 100_000, "squares"
    )(spread)
    squares = lax.all_to_all(squares, ("y2", "y1", "y0", "xh"), 0, 0)
    return kernel_call(
        scale_kernel,
        jax.ShapeDtypeStruct((channels // 16, width), jnp.float32),
        [VMEM, VMEM],
        [],
        100_000,
        "scale",
    )(spread, squares)


def solution(mesh):
    bits = Mesh(mesh.devices.reshape((2,) * len(BITS)), BITS)
    images = P(("xl", "z2", "z1", "z0", "c", "y2", "y1", "y0", "xh"))
    return jax.shard_map(
        on_device,
        mesh=bits,
        in_specs=(P(*images, None), P(), images),
        out_specs=P(("y2", "y1", "y0", "xh"), None),
        check_vma=False,
    )
```

```python
import itertools

import jax
import jax.numpy as jnp
from jax import lax
from jax.experimental import pallas as pl
from jax.experimental.pallas import tpu as pltpu
from jax.sharding import Mesh
from jax.sharding import PartitionSpec as P

softness_factor = 0.05
EXP2_SCALE = 1.4426950408889634 / softness_factor
Y = 8
BITS = ("y2", "y1", "y0", "xh", "xl", "z2", "z1", "z0", "c")
YBITS = BITS[:3]
OTHER_CORE = [(0, 1), (1, 0)]


def moves(other_core, step):
    pairs = []
    for y, xh, xl, z, core in itertools.product(range(Y), range(2), range(2), range(8), range(2)):
        there = xh ^ other_core
        y_there = (y + step * (1, -1)[there]) % Y
        pairs.append((place(y, xh, xl, z, core), place(y_there, core ^ xl, 1 - xl, z, there)))
    return pairs


def place(y, xh, xl, z, core):
    return (((y * 2 + xh) * 2 + xl) * 8 + z) * 2 + core


TO_HOST, TO_SIBLING = moves(0, 0), moves(1, 0)
TO_NEXT_SAME, TO_NEXT_OTHER = moves(0, 1), moves(1, 1)
ROUND = [(2 * y + c, 2 * ((y + (1, -1)[c]) % Y) + c) for y in range(Y) for c in range(2)]


def exponentials(left, right):
    scores = lax.dot_general(
        left, right, (((1,), (1,)), ((), ())), preferred_element_type=jnp.float32
    )
    return jnp.exp2(scores * EXP2_SCALE)


def over_rows(values):
    return values.reshape(values.shape[0] // 8, 8, values.shape[1]).sum(0)


def over_lane_groups(values):
    return sum(values[:, k : k + 128] for k in range(0, values.shape[1], 128))


def row_totals(per_lane):
    ones = jnp.ones((8, per_lane.shape[1]), jnp.float32)
    totals = lax.dot_general(
        ones,
        per_lane,
        (((1,), (1,)), ((), ())),
        precision=lax.Precision.HIGHEST,
        preferred_element_type=jnp.float32,
    )
    return totals[0:1, :]


def without_self(values):
    rows = lax.broadcasted_iota(jnp.int32, values.shape, 0)
    columns = lax.broadcasted_iota(jnp.int32, values.shape, 1)
    return jnp.where(rows == columns, 0.0, values)


def early_sums_kernel(*refs):
    pieces, (sums_ref, per_lane, per_column) = refs[:-3], refs[-3:]
    rows = per_lane.shape[1]
    per_lane[...] = jnp.zeros_like(per_lane)
    for i, piece in enumerate(pieces):
        left = piece[...]
        own = over_rows(without_self(exponentials(left, left)))
        per_column[i] = own if i == 0 else per_column[i] + own
        for j in range(i + 1, len(pieces)):
            values = exponentials(left, pieces[j][...])
            column = over_rows(values)
            per_column[j] = column if i == 0 else per_column[j] + column
            per_lane[i] += over_lane_groups(values)
    for i in range(len(pieces)):
        total = per_column[i].sum(0, keepdims=True) + row_totals(per_lane[i])
        sums_ref[i // 2, :, i % 2 * rows : (i % 2 + 1) * rows] = total


def block_copies(source, target, semaphores, order, first):
    rows = target.shape[0] // len(order)
    copies = {}
    for position, k in enumerate(order):
        part = pl.ds(k * rows, rows)
        copies[k] = pltpu.make_async_copy(
            source.at[part], target.at[part], semaphores.at[first + position]
        )
        copies[k].start()
    return copies


def pair_sums_kernel(
    core_ref, mine_hbm, sibling_hbm, early_ref, sums_ref, mine, sibling, per_lane, per_column, semaphores
):
    core = core_ref[0]
    blocks, wide = per_column.shape[0], per_column.shape[2]
    half = blocks // 2
    mine_copies = block_copies(mine_hbm, mine, semaphores, (3, 0, 1, 2), 0)
    sibling_copies = block_copies(sibling_hbm, sibling, semaphores, (2, 3, 0, 1), blocks)
    per_lane[...] = jnp.zeros_like(per_lane)
    per_column[...] = jnp.zeros_like(per_column)

    def block(ref, k):
        return ref[k * wide : (k + 1) * wide, :]

    mine_copies[blocks - 1].wait()
    last = block(mine, blocks - 1)
    column = over_rows(without_self(exponentials(last, last)))
    same = []
    for i in range(blocks - 1):
        mine_copies[i].wait()
        values = exponentials(block(mine, i), last)
        column += over_rows(values)
        same.append(early_ref[i] + row_totals(over_lane_groups(values)))
    same.append(column.sum(0, keepdims=True))

    def pairs(left_ref, first, right_ref, columns):
        for i in range(half):
            left = block(left_ref, first + i)
            for j in columns:
                values = exponentials(left, block(right_ref, j))
                per_column[j] += over_rows(values)
                per_lane[i] += over_lane_groups(values)

    sibling_copies[2].wait()
    sibling_copies[3].wait()

    @pl.when(core == 0)
    def _():
        pairs(mine, 0, sibling, (2, 3))

    @pl.when(core == 1)
    def _():
        pairs(sibling, half, mine, (0, 1))

    sibling_copies[0].wait()
    sibling_copies[1].wait()

    @pl.when(core == 0)
    def _():
        pairs(mine, 0, sibling, (0, 1))

    @pl.when(core == 1)
    def _():
        pairs(sibling, half, mine, (2, 3))

    for k in range(blocks):
        sums_ref[k] = jnp.zeros_like(sums_ref[k])
        sums_ref[blocks + k] = per_column[k].sum(0, keepdims=True)
    for i in range(half):
        sums_ref[half * core + i] = row_totals(per_lane[i])
    for k in range(blocks):
        sums_ref[blocks * core + k] += same[k]


def weight_kernel(
    core_ref,
    start_ref,
    side_ref,
    sums_ref,
    mine_ref,
    sibling_ref,
    keep_ref,
    send_ref,
    weights,
):
    core = core_ref[0]
    wide = sums_ref.shape[2]
    blocks = sums_ref.shape[0] // 2
    rows = side_ref.shape[0]
    own = mine_ref[:rows, :]
    mine_sums = sums_ref[blocks * core][:, :rows]
    inverse_own = 1.0 / jnp.broadcast_to(mine_sums, (128, rows)).T[:, :1]
    partner = side_ref[:, 0:1].astype(jnp.int32)
    lanes = lax.broadcasted_iota(jnp.int32, (1, wide), 1)
    for part, ref in enumerate((mine_ref, sibling_ref)):
        for k in range(blocks):
            which = core if part == 0 else 1 - core
            right = ref[k * wide : (k + 1) * wide, :]
            inverse = 1.0 / sums_ref[blocks * which + k]
            values = exponentials(own, right)
            if part == 0 and k == 0:
                values = without_self(values)
            first = start_ref[part * blocks * 2 + 2 * k]
            second = start_ref[part * blocks * 2 + 2 * k + 1]
            columns = lanes + jnp.where(lanes < rows, first, second - rows)
            target = jnp.where(columns == partner, 1.0, 0.0)
            place_here = slice(k * wide, (k + 1) * wide)
            weights[part, :rows, place_here] = (values * inverse_own - target).astype(jnp.bfloat16)
            weights[part, rows:, place_here] = (values * inverse - target).astype(jnp.bfloat16)
    total = jnp.dot(weights[0], mine_ref[...], preferred_element_type=jnp.float32)
    total += jnp.dot(weights[1], sibling_ref[...], preferred_element_type=jnp.float32)
    grad_unit = (total[:rows] + total[rows:]) * (1.0 / softness_factor)
    unit = own.astype(jnp.float32)
    along = jnp.sum(unit * grad_unit, axis=1, keepdims=True)
    grad_hidden = ((grad_unit - unit * along) * side_ref[:, 1:2]).astype(jnp.bfloat16)
    middle = grad_hidden.shape[1] // 2
    first, second = grad_hidden[:, :middle], grad_hidden[:, middle:]
    keep_ref[...] = jnp.where(core == 0, first, second)
    send_ref[...] = jnp.where(core == 0, second, first)


def squares_kernel(spread_ref, squares_ref):
    values = spread_ref[...].astype(jnp.float32)
    squares_ref[...] = jnp.full(squares_ref.shape, jnp.sum(values * values), jnp.float32)


def scale_kernel(spread_ref, squares_ref, update_ref):
    total = jnp.sum(squares_ref[...], axis=0, keepdims=True)
    entries = 16 * update_ref.shape[0] * update_ref.shape[1]
    scale = 1.0 / jnp.sqrt(total * (1.0 / entries) + 1e-06)
    scale = jnp.concatenate([scale, scale], axis=1)
    for core in range(2):
        for row in range(16):
            tile = spread_ref[16 * core + row].astype(jnp.float32)
            update_ref[8 * row : 8 * row + 8, 256 * core : 256 * core + 256] = tile * scale


VMEM = pl.BlockSpec(memory_space=pltpu.VMEM)
SMEM = pl.BlockSpec(memory_space=pltpu.SMEM)
ANYWHERE = pl.BlockSpec(memory_space=pl.ANY)


def kernel_call(body, outputs, in_specs, scratch, flops, name):
    return pl.pallas_call(
        body,
        out_shape=outputs,
        in_specs=in_specs,
        out_specs=jax.tree.map(lambda unused: VMEM, outputs),
        scratch_shapes=scratch,
        compiler_params=pltpu.CompilerParams(vmem_limit_bytes=24 * 1024 * 1024),
        cost_estimate=pl.CostEstimate(
            flops=flops, bytes_accessed=2_000_000, transcendentals=100_000
        ),
        name=name,
    )


def on_device(features, head_weight, partner):
    rows = features.shape[0]
    channels, width = head_weight.shape
    y = lax.axis_index("y2") * 4 + lax.axis_index("y1") * 2 + lax.axis_index("y0")
    core = lax.axis_index("c")
    core_scalar = core.reshape(1).astype(jnp.int32)

    hidden = jnp.dot(features, head_weight, preferred_element_type=jnp.float32)
    row_norm = jnp.sqrt(jnp.sum(hidden * hidden, axis=1, keepdims=True) + 1e-05)
    unit = (hidden / row_norm).astype(jnp.bfloat16)
    side = jnp.stack([partner.astype(jnp.float32), 1.0 / row_norm[:, 0]])

    sign = jnp.where(core == 0, -1, 1)
    same_core = lax.ppermute(unit, BITS, TO_NEXT_SAME)
    other_core = lax.ppermute(unit, BITS, TO_NEXT_OTHER)
    own = lax.ppermute(unit, BITS, TO_HOST)
    side_here = lax.ppermute(side, BITS, TO_HOST)
    pieces, places = [own], [y * 2 + core]
    for distance in range(1, 5):
        place_there = (y + sign * distance) % Y * 2
        if distance > 1:
            same_core = lax.ppermute(same_core, (*YBITS, "c"), ROUND)
        if distance == 4:
            early = kernel_call(
                early_sums_kernel,
                jax.ShapeDtypeStruct((3, 1, 512), jnp.float32),
                [VMEM] * 6,
                [pltpu.VMEM((6, rows, 128), jnp.float32), pltpu.VMEM((6, 8, rows), jnp.float32)],
                2_000_000_000,
                "early_sums",
            )(*pieces[:6])
            same_core, side_here, early = lax.optimization_barrier((same_core, side_here, early))
        pieces.append(same_core)
        places.append(place_there + core)
        if distance == 4:
            break
        if distance == 3:
            later, unused = lax.optimization_barrier((features, same_core))
            rows_here = lax.ppermute(later, BITS, TO_HOST)
            rows_beside = lax.ppermute(later, BITS, TO_SIBLING)
        if distance > 1:
            other_core = lax.ppermute(other_core, (*YBITS, "c"), ROUND)
        pieces.append(other_core)
        places.append(place_there + 1 - core)
    sign, core_there = -sign, 1 - core
    places.append(y * 2 + core_there)
    for distance in range(1, 5):
        place_there = (y + sign * distance) % Y * 2
        there = [place_there + core_there, place_there + 1 - core_there]
        places += there[: 1 if distance == 4 else 2]
    mine = jnp.concatenate(pieces)
    starts = jnp.stack(places).astype(jnp.int32) * rows

    sibling = lax.ppermute(mine, "c", OTHER_CORE)
    held = [pltpu.VMEM(mine.shape, jnp.bfloat16)] * 2
    semaphores = pltpu.SemaphoreType.DMA((8,))
    sums = kernel_call(
        pair_sums_kernel,
        jax.ShapeDtypeStruct((8, 1, 512), jnp.float32),
        [SMEM, ANYWHERE, ANYWHERE, VMEM],
        held
        + [
            pltpu.VMEM((2, 512, 128), jnp.float32),
            pltpu.VMEM((4, 8, 512), jnp.float32),
            semaphores,
        ],
        3_000_000_000,
        "pair_sums",
    )(core_scalar, mine, sibling, early)
    sums = lax.psum(sums, "c")
    piece = jax.ShapeDtypeStruct((rows, width // 2), jnp.bfloat16)
    kept, sent = kernel_call(
        weight_kernel,
        (piece, piece),
        [SMEM, SMEM, VMEM, VMEM, VMEM, VMEM],
        [pltpu.VMEM((2, 2 * rows, 8 * rows), jnp.bfloat16)],
        2_000_000_000,
        "weights",
    )(core_scalar, starts, side_here.T, sums, mine, sibling)
    beside = lax.ppermute(sent, "c", OTHER_CORE)

    def contract(left, right):
        return lax.dot_general(
            left, right, (((0,), (0,)), ((), ())), preferred_element_type=jnp.float32
        )

    partial = (contract(rows_here, kept) + contract(rows_beside, beside)).astype(jnp.bfloat16)
    tiles = partial.reshape(4, 2, 2, 2, 4, 2, 8, 256)
    tiles = tiles.transpose(5, 3, 1, 2, 0, 4, 6, 7).reshape(16, 16 * 8, 256)
    received = lax.all_to_all(tiles, ("z0", "xl", "y0", "xh"), 0, 0)
    near_sum = received.astype(jnp.float32).sum(0).astype(jnp.bfloat16).reshape(16, 8, 256)
    received = lax.all_to_all(near_sum, ("y2", "y1", "z2", "z1"), 0, 0)
    fragment = received.astype(jnp.float32).sum(0).astype(jnp.bfloat16)
    spread = lax.all_to_all(
        jnp.broadcast_to(fragment[None], (32, 8, 256)), ("c", "xl", "z2", "z1", "z0"), 0, 0
    )
    squares = kernel_call(
        squares_kernel, jax.ShapeDtypeStruct((16, 128), jnp.float32), [VMEM], [], 100_000, "squares"
    )(spread)
    squares = lax.all_to_all(squares, ("y2", "y1", "y0", "xh"), 0, 0)
    return kernel_call(
        scale_kernel,
        jax.ShapeDtypeStruct((channels // 16, width), jnp.float32),
        [VMEM, VMEM],
        [],
        100_000,
        "scale",
    )(spread, squares)


def solution(mesh):
    bits = Mesh(mesh.devices.reshape((2,) * len(BITS)), BITS)
    images = P(("xl", "z2", "z1", "z0", "c", "y2", "y1", "y0", "xh"))
    return jax.shard_map(
        on_device,
        mesh=bits,
        in_specs=(P(*images, None), P(), images),
        out_specs=P(("y2", "y1", "y0", "xh"), None),
        check_vma=False,
    )
```

```python
import itertools

import jax
import jax.numpy as jnp
from jax import lax
from jax.experimental import pallas as pl
from jax.experimental.pallas import tpu as pltpu
from jax.sharding import Mesh
from jax.sharding import PartitionSpec as P

softness_factor = 0.05
EXP2_SCALE = 1.4426950408889634 / softness_factor
Y = 8
BITS = ("y2", "y1", "y0", "xh", "xl", "z2", "z1", "z0", "c")
YBITS = BITS[:3]
OTHER_CORE = [(0, 1), (1, 0)]


def moves(other_core, step):
    pairs = []
    for y, xh, xl, z, core in itertools.product(range(Y), range(2), range(2), range(8), range(2)):
        there = xh ^ other_core
        y_there = (y + step * (1, -1)[there]) % Y
        pairs.append((place(y, xh, xl, z, core), place(y_there, core ^ xl, 1 - xl, z, there)))
    return pairs


def place(y, xh, xl, z, core):
    return (((y * 2 + xh) * 2 + xl) * 8 + z) * 2 + core


TO_HOST, TO_SIBLING = moves(0, 0), moves(1, 0)
TO_NEXT_SAME, TO_NEXT_OTHER = moves(0, 1), moves(1, 1)
ROUND = [(2 * y + c, 2 * ((y + (1, -1)[c]) % Y) + c) for y in range(Y) for c in range(2)]


def exponentials(left, right):
    scores = lax.dot_general(
        left, right, (((1,), (1,)), ((), ())), preferred_element_type=jnp.float32
    )
    return jnp.exp2(scores * EXP2_SCALE)


def over_rows(values):
    return values.reshape(values.shape[0] // 8, 8, values.shape[1]).sum(0)


def over_lane_groups(values):
    return sum(values[:, k : k + 128] for k in range(0, values.shape[1], 128))


def row_totals(per_lane):
    ones = jnp.ones((8, per_lane.shape[1]), jnp.float32)
    totals = lax.dot_general(
        ones,
        per_lane,
        (((1,), (1,)), ((), ())),
        precision=lax.Precision.HIGHEST,
        preferred_element_type=jnp.float32,
    )
    return totals[0:1, :]


def without_self(values):
    rows = lax.broadcasted_iota(jnp.int32, values.shape, 0)
    columns = lax.broadcasted_iota(jnp.int32, values.shape, 1)
    return jnp.where(rows == columns, 0.0, values)


def early_sums_kernel(*refs):
    pieces, (sums_ref, per_lane, per_column) = refs[:-3], refs[-3:]
    rows = per_lane.shape[1]
    per_lane[...] = jnp.zeros_like(per_lane)
    for i, piece in enumerate(pieces):
        left = piece[...]
        own = over_rows(without_self(exponentials(left, left)))
        per_column[i] = own if i == 0 else per_column[i] + own
        for j in range(i + 1, len(pieces)):
            values = exponentials(left, pieces[j][...])
            column = over_rows(values)
            per_column[j] = column if i == 0 else per_column[j] + column
            per_lane[i] += over_lane_groups(values)
    for i in range(len(pieces)):
        total = per_column[i].sum(0, keepdims=True) + row_totals(per_lane[i])
        sums_ref[i // 2, :, i % 2 * rows : (i % 2 + 1) * rows] = total


def block_copies(source, target, semaphores, order, first):
    rows = target.shape[0] // len(order)
    copies = {}
    for position, k in enumerate(order):
        part = pl.ds(k * rows, rows)
        copies[k] = pltpu.make_async_copy(
            source.at[part], target.at[part], semaphores.at[first + position]
        )
        copies[k].start()
    return copies


def pair_sums_kernel(
    core_ref, mine_hbm, sibling_hbm, early_ref, sums_ref, mine, sibling, per_lane, per_column, semaphores
):
    core = core_ref[0]
    blocks, wide = per_column.shape[0], per_column.shape[2]
    half = blocks // 2
    mine_copies = block_copies(mine_hbm, mine, semaphores, (3, 0, 1, 2), 0)
    sibling_copies = block_copies(sibling_hbm, sibling, semaphores, (2, 3, 0, 1), blocks)
    per_lane[...] = jnp.zeros_like(per_lane)
    per_column[...] = jnp.zeros_like(per_column)

    def block(ref, k):
        return ref[k * wide : (k + 1) * wide, :]

    mine_copies[blocks - 1].wait()
    last = block(mine, blocks - 1)
    column = over_rows(without_self(exponentials(last, last)))
    same = []
    for i in range(blocks - 1):
        mine_copies[i].wait()
        values = exponentials(block(mine, i), last)
        column += over_rows(values)
        same.append(early_ref[i] + row_totals(over_lane_groups(values)))
    same.append(column.sum(0, keepdims=True))

    def pairs(left_ref, first, right_ref, columns):
        for i in range(half):
            left = block(left_ref, first + i)
            for j in columns:
                values = exponentials(left, block(right_ref, j))
                per_column[j] += over_rows(values)
                per_lane[i] += over_lane_groups(values)

    sibling_copies[2].wait()
    sibling_copies[3].wait()

    @pl.when(core == 0)
    def _():
        pairs(mine, 0, sibling, (2, 3))

    @pl.when(core == 1)
    def _():
        pairs(sibling, half, mine, (0, 1))

    sibling_copies[0].wait()
    sibling_copies[1].wait()

    @pl.when(core == 0)
    def _():
        pairs(mine, 0, sibling, (0, 1))

    @pl.when(core == 1)
    def _():
        pairs(sibling, half, mine, (2, 3))

    for k in range(blocks):
        sums_ref[k] = jnp.zeros_like(sums_ref[k])
        sums_ref[blocks + k] = per_column[k].sum(0, keepdims=True)
    for i in range(half):
        sums_ref[half * core + i] = row_totals(per_lane[i])
    for k in range(blocks):
        sums_ref[blocks * core + k] += same[k]


def weight_kernel(
    core_ref,
    start_ref,
    side_ref,
    sums_ref,
    mine_hbm,
    sibling_hbm,
    keep_ref,
    send_ref,
    mine_ref,
    sibling_ref,
    weights,
    semaphores,
):
    core = core_ref[0]
    wide = sums_ref.shape[2]
    blocks = sums_ref.shape[0] // 2
    rows = side_ref.shape[0]
    copies = (
        block_copies(mine_hbm, mine_ref, semaphores, (0,), 0)[0],
        block_copies(sibling_hbm, sibling_ref, semaphores, (0,), 1)[0],
    )
    copies[0].wait()
    own = mine_ref[:rows, :]
    mine_sums = sums_ref[blocks * core][:, :rows]
    inverse_own = 1.0 / jnp.broadcast_to(mine_sums, (128, rows)).T[:, :1]
    partner = side_ref[:, 0:1].astype(jnp.int32)
    lanes = lax.broadcasted_iota(jnp.int32, (1, wide), 1)
    for part, ref in enumerate((mine_ref, sibling_ref)):
        if part > 0:
            copies[part].wait()
        for k in range(blocks):
            which = core if part == 0 else 1 - core
            right = ref[k * wide : (k + 1) * wide, :]
            inverse = 1.0 / sums_ref[blocks * which + k]
            values = exponentials(own, right)
            if part == 0 and k == 0:
                values = without_self(values)
            first = start_ref[part * blocks * 2 + 2 * k]
            second = start_ref[part * blocks * 2 + 2 * k + 1]
            columns = lanes + jnp.where(lanes < rows, first, second - rows)
            target = jnp.where(columns == partner, 1.0, 0.0)
            place_here = slice(k * wide, (k + 1) * wide)
            weights[part, :rows, place_here] = (values * inverse_own - target).astype(jnp.bfloat16)
            weights[part, rows:, place_here] = (values * inverse - target).astype(jnp.bfloat16)
    total = jnp.dot(weights[0], mine_ref[...], preferred_element_type=jnp.float32)
    total += jnp.dot(weights[1], sibling_ref[...], preferred_element_type=jnp.float32)
    grad_unit = (total[:rows] + total[rows:]) * (1.0 / softness_factor)
    unit = own.astype(jnp.float32)
    along = jnp.sum(unit * grad_unit, axis=1, keepdims=True)
    grad_hidden = ((grad_unit - unit * along) * side_ref[:, 1:2]).astype(jnp.bfloat16)
    middle = grad_hidden.shape[1] // 2
    first, second = grad_hidden[:, :middle], grad_hidden[:, middle:]
    keep_ref[...] = jnp.where(core == 0, first, second)
    send_ref[...] = jnp.where(core == 0, second, first)


def squares_kernel(spread_ref, squares_ref):
    values = spread_ref[...].astype(jnp.float32)
    squares_ref[...] = jnp.full(squares_ref.shape, jnp.sum(values * values), jnp.float32)


def scale_kernel(spread_ref, squares_ref, update_ref):
    total = jnp.sum(squares_ref[...], axis=0, keepdims=True)
    entries = 16 * update_ref.shape[0] * update_ref.shape[1]
    scale = 1.0 / jnp.sqrt(total * (1.0 / entries) + 1e-06)
    scale = jnp.concatenate([scale, scale], axis=1)
    for core in range(2):
        for row in range(16):
            tile = spread_ref[16 * core + row].astype(jnp.float32)
            update_ref[8 * row : 8 * row + 8, 256 * core : 256 * core + 256] = tile * scale


VMEM = pl.BlockSpec(memory_space=pltpu.VMEM)
SMEM = pl.BlockSpec(memory_space=pltpu.SMEM)
ANYWHERE = pl.BlockSpec(memory_space=pl.ANY)


def kernel_call(body, outputs, in_specs, scratch, flops, name):
    return pl.pallas_call(
        body,
        out_shape=outputs,
        in_specs=in_specs,
        out_specs=jax.tree.map(lambda unused: VMEM, outputs),
        scratch_shapes=scratch,
        compiler_params=pltpu.CompilerParams(vmem_limit_bytes=24 * 1024 * 1024),
        cost_estimate=pl.CostEstimate(
            flops=flops, bytes_accessed=2_000_000, transcendentals=100_000
        ),
        name=name,
    )


def on_device(features, head_weight, partner):
    rows = features.shape[0]
    channels, width = head_weight.shape
    y = lax.axis_index("y2") * 4 + lax.axis_index("y1") * 2 + lax.axis_index("y0")
    core = lax.axis_index("c")
    core_scalar = core.reshape(1).astype(jnp.int32)

    hidden = jnp.dot(features, head_weight, preferred_element_type=jnp.float32)
    row_norm = jnp.sqrt(jnp.sum(hidden * hidden, axis=1, keepdims=True) + 1e-05)
    unit = (hidden / row_norm).astype(jnp.bfloat16)
    side = jnp.stack([partner.astype(jnp.float32), 1.0 / row_norm[:, 0]])

    sign = jnp.where(core == 0, -1, 1)
    same_core = lax.ppermute(unit, BITS, TO_NEXT_SAME)
    other_core = lax.ppermute(unit, BITS, TO_NEXT_OTHER)
    own = lax.ppermute(unit, BITS, TO_HOST)
    side_here = lax.ppermute(side, BITS, TO_HOST)
    pieces, places = [own], [y * 2 + core]
    for distance in range(1, 5):
        place_there = (y + sign * distance) % Y * 2
        if distance > 1:
            same_core = lax.ppermute(same_core, (*YBITS, "c"), ROUND)
        if distance == 4:
            early = kernel_call(
                early_sums_kernel,
                jax.ShapeDtypeStruct((3, 1, 512), jnp.float32),
                [VMEM] * 6,
                [pltpu.VMEM((6, rows, 128), jnp.float32), pltpu.VMEM((6, 8, rows), jnp.float32)],
                2_000_000_000,
                "early_sums",
            )(*pieces[:6])
            same_core, side_here, early = lax.optimization_barrier((same_core, side_here, early))
        pieces.append(same_core)
        places.append(place_there + core)
        if distance == 4:
            break
        if distance == 3:
            later, unused = lax.optimization_barrier((features, same_core))
            rows_here = lax.ppermute(later, BITS, TO_HOST)
            rows_beside = lax.ppermute(later, BITS, TO_SIBLING)
        if distance > 1:
            other_core = lax.ppermute(other_core, (*YBITS, "c"), ROUND)
        pieces.append(other_core)
        places.append(place_there + 1 - core)
    sign, core_there = -sign, 1 - core
    places.append(y * 2 + core_there)
    for distance in range(1, 5):
        place_there = (y + sign * distance) % Y * 2
        there = [place_there + core_there, place_there + 1 - core_there]
        places += there[: 1 if distance == 4 else 2]
    mine = jnp.concatenate(pieces)
    starts = jnp.stack(places).astype(jnp.int32) * rows

    sibling = lax.ppermute(mine, "c", OTHER_CORE)
    held = [pltpu.VMEM(mine.shape, jnp.bfloat16)] * 2
    semaphores = pltpu.SemaphoreType.DMA((8,))
    sums = kernel_call(
        pair_sums_kernel,
        jax.ShapeDtypeStruct((8, 1, 512), jnp.float32),
        [SMEM, ANYWHERE, ANYWHERE, VMEM],
        held
        + [
            pltpu.VMEM((2, 512, 128), jnp.float32),
            pltpu.VMEM((4, 8, 512), jnp.float32),
            semaphores,
        ],
        3_000_000_000,
        "pair_sums",
    )(core_scalar, mine, sibling, early)
    sums = lax.psum(sums, "c")
    piece = jax.ShapeDtypeStruct((rows, width // 2), jnp.bfloat16)
    kept, sent = kernel_call(
        weight_kernel,
        (piece, piece),
        [SMEM, SMEM, VMEM, VMEM, ANYWHERE, ANYWHERE],
        held + [pltpu.VMEM((2, 2 * rows, 8 * rows), jnp.bfloat16), pltpu.SemaphoreType.DMA((2,))],
        2_000_000_000,
        "weights",
    )(core_scalar, starts, side_here.T, sums, mine, sibling)
    beside = lax.ppermute(sent, "c", OTHER_CORE)

    def contract(left, right):
        return lax.dot_general(
            left, right, (((0,), (0,)), ((), ())), preferred_element_type=jnp.float32
        )

    partial = (contract(rows_here, kept) + contract(rows_beside, beside)).astype(jnp.bfloat16)
    tiles = partial.reshape(4, 2, 2, 2, 4, 2, 8, 256)
    tiles = tiles.transpose(5, 3, 1, 2, 0, 4, 6, 7).reshape(16, 16 * 8, 256)
    received = lax.all_to_all(tiles, ("z0", "xl", "y0", "xh"), 0, 0)
    near_sum = received.astype(jnp.float32).sum(0).astype(jnp.bfloat16).reshape(16, 8, 256)
    received = lax.all_to_all(near_sum, ("y2", "y1", "z2", "z1"), 0, 0)
    fragment = received.astype(jnp.float32).sum(0).astype(jnp.bfloat16)
    spread = lax.all_to_all(
        jnp.broadcast_to(fragment[None], (32, 8, 256)), ("c", "xl", "z2", "z1", "z0"), 0, 0
    )
    squares = kernel_call(
        squares_kernel, jax.ShapeDtypeStruct((16, 128), jnp.float32), [VMEM], [], 100_000, "squares"
    )(spread)
    squares = lax.all_to_all(squares, ("y2", "y1", "y0", "xh"), 0, 0)
    return kernel_call(
        scale_kernel,
        jax.ShapeDtypeStruct((channels // 16, width), jnp.float32),
        [VMEM, VMEM],
        [],
        100_000,
        "scale",
    )(spread, squares)


def solution(mesh):
    bits = Mesh(mesh.devices.reshape((2,) * len(BITS)), BITS)
    images = P(("xl", "z2", "z1", "z0", "c", "y2", "y1", "y0", "xh"))
    return jax.shard_map(
        on_device,
        mesh=bits,
        in_specs=(P(*images, None), P(), images),
        out_specs=P(("y2", "y1", "y0", "xh"), None),
        check_vma=False,
    )
```

```python
import itertools

import jax
import jax.numpy as jnp
from jax import lax
from jax.experimental import pallas as pl
from jax.experimental.pallas import tpu as pltpu
from jax.sharding import Mesh
from jax.sharding import PartitionSpec as P

softness_factor = 0.05
EXP2_SCALE = 1.4426950408889634 / softness_factor
Y = 8
BITS = ("y2", "y1", "y0", "xh", "xl", "z2", "z1", "z0", "c")
YBITS = BITS[:3]
OTHER_CORE = [(0, 1), (1, 0)]


def moves(other_core, step):
    pairs = []
    for y, xh, xl, z, core in itertools.product(range(Y), range(2), range(2), range(8), range(2)):
        there = xh ^ other_core
        y_there = (y + step * (1, -1)[there]) % Y
        pairs.append((place(y, xh, xl, z, core), place(y_there, core ^ xl, 1 - xl, z, there)))
    return pairs


def place(y, xh, xl, z, core):
    return (((y * 2 + xh) * 2 + xl) * 8 + z) * 2 + core


TO_HOST = moves(0, 0)
TO_NEXT_SAME, TO_NEXT_OTHER = moves(0, 1), moves(1, 1)
ROUND = [(2 * y + c, 2 * ((y + (1, -1)[c]) % Y) + c) for y in range(Y) for c in range(2)]


def exponentials(left, right):
    scores = lax.dot_general(
        left, right, (((1,), (1,)), ((), ())), preferred_element_type=jnp.float32
    )
    return jnp.exp2(scores * EXP2_SCALE)


def over_rows(values):
    return values.reshape(values.shape[0] // 8, 8, values.shape[1]).sum(0)


def over_lane_groups(values):
    return sum(values[:, k : k + 128] for k in range(0, values.shape[1], 128))


def row_totals(per_lane):
    ones = jnp.ones((8, per_lane.shape[1]), jnp.float32)
    totals = lax.dot_general(
        ones,
        per_lane,
        (((1,), (1,)), ((), ())),
        precision=lax.Precision.HIGHEST,
        preferred_element_type=jnp.float32,
    )
    return totals[0:1, :]


def without_self(values):
    rows = lax.broadcasted_iota(jnp.int32, values.shape, 0)
    columns = lax.broadcasted_iota(jnp.int32, values.shape, 1)
    return jnp.where(rows == columns, 0.0, values)


def early_sums_kernel(*refs):
    pieces, (sums_ref, per_lane, per_column) = refs[:-3], refs[-3:]
    rows = per_lane.shape[1]
    per_lane[...] = jnp.zeros_like(per_lane)
    for i, piece in enumerate(pieces):
        left = piece[...]
        own = over_rows(without_self(exponentials(left, left)))
        per_column[i] = own if i == 0 else per_column[i] + own
        for j in range(i + 1, len(pieces)):
            values = exponentials(left, pieces[j][...])
            column = over_rows(values)
            per_column[j] = column if i == 0 else per_column[j] + column
            per_lane[i] += over_lane_groups(values)
    for i in range(len(pieces)):
        total = per_column[i].sum(0, keepdims=True) + row_totals(per_lane[i])
        sums_ref[i // 2, :, i % 2 * rows : (i % 2 + 1) * rows] = total


def block_copies(source, target, semaphores, order, first):
    rows = target.shape[0] // len(order)
    copies = {}
    for position, k in enumerate(order):
        part = pl.ds(k * rows, rows)
        copies[k] = pltpu.make_async_copy(
            source.at[part], target.at[part], semaphores.at[first + position]
        )
        copies[k].start()
    return copies


def pair_sums_kernel(
    core_ref, mine_hbm, sibling_hbm, early_ref, sums_ref, mine, sibling, per_lane, per_column, semaphores
):
    core = core_ref[0]
    blocks, wide = per_column.shape[0], per_column.shape[2]
    half = blocks // 2
    mine_copies = block_copies(mine_hbm, mine, semaphores, (3, 0, 1, 2), 0)
    sibling_copies = block_copies(sibling_hbm, sibling, semaphores, (2, 3, 0, 1), blocks)
    per_lane[...] = jnp.zeros_like(per_lane)
    per_column[...] = jnp.zeros_like(per_column)

    def block(ref, k):
        return ref[k * wide : (k + 1) * wide, :]

    mine_copies[blocks - 1].wait()
    last = block(mine, blocks - 1)
    column = over_rows(without_self(exponentials(last, last)))
    same = []
    for i in range(blocks - 1):
        mine_copies[i].wait()
        values = exponentials(block(mine, i), last)
        column += over_rows(values)
        same.append(early_ref[i] + row_totals(over_lane_groups(values)))
    same.append(column.sum(0, keepdims=True))

    def pairs(left_ref, first, right_ref, columns):
        for i in range(half):
            left = block(left_ref, first + i)
            for j in columns:
                values = exponentials(left, block(right_ref, j))
                per_column[j] += over_rows(values)
                per_lane[i] += over_lane_groups(values)

    sibling_copies[2].wait()
    sibling_copies[3].wait()

    @pl.when(core == 0)
    def _():
        pairs(mine, 0, sibling, (2, 3))

    @pl.when(core == 1)
    def _():
        pairs(sibling, half, mine, (0, 1))

    sibling_copies[0].wait()
    sibling_copies[1].wait()

    @pl.when(core == 0)
    def _():
        pairs(mine, 0, sibling, (0, 1))

    @pl.when(core == 1)
    def _():
        pairs(sibling, half, mine, (2, 3))

    for k in range(blocks):
        sums_ref[k] = jnp.zeros_like(sums_ref[k])
        sums_ref[blocks + k] = per_column[k].sum(0, keepdims=True)
    for i in range(half):
        sums_ref[half * core + i] = row_totals(per_lane[i])
    for k in range(blocks):
        sums_ref[blocks * core + k] += same[k]


def weight_kernel(
    core_ref,
    start_ref,
    side_ref,
    sums_ref,
    mine_ref,
    sibling_ref,
    keep_ref,
    send_ref,
    weights,
):
    core = core_ref[0]
    wide = sums_ref.shape[2]
    blocks = sums_ref.shape[0] // 2
    rows = side_ref.shape[0]
    own = mine_ref[:rows, :]
    mine_sums = sums_ref[blocks * core][:, :rows]
    inverse_own = 1.0 / jnp.broadcast_to(mine_sums, (128, rows)).T[:, :1]
    partner = side_ref[:, 0:1].astype(jnp.int32)
    lanes = lax.broadcasted_iota(jnp.int32, (1, wide), 1)
    for part, ref in enumerate((mine_ref, sibling_ref)):
        for k in range(blocks):
            which = core if part == 0 else 1 - core
            right = ref[k * wide : (k + 1) * wide, :]
            inverse = 1.0 / sums_ref[blocks * which + k]
            values = exponentials(own, right)
            if part == 0 and k == 0:
                values = without_self(values)
            first = start_ref[part * blocks * 2 + 2 * k]
            second = start_ref[part * blocks * 2 + 2 * k + 1]
            columns = lanes + jnp.where(lanes < rows, first, second - rows)
            target = jnp.where(columns == partner, 1.0, 0.0)
            place_here = slice(k * wide, (k + 1) * wide)
            weights[part, :rows, place_here] = (values * inverse_own - target).astype(jnp.bfloat16)
            weights[part, rows:, place_here] = (values * inverse - target).astype(jnp.bfloat16)
    total = jnp.dot(weights[0], mine_ref[...], preferred_element_type=jnp.float32)
    total += jnp.dot(weights[1], sibling_ref[...], preferred_element_type=jnp.float32)
    grad_unit = (total[:rows] + total[rows:]) * (1.0 / softness_factor)
    unit = own.astype(jnp.float32)
    along = jnp.sum(unit * grad_unit, axis=1, keepdims=True)
    grad_hidden = ((grad_unit - unit * along) * side_ref[:, 1:2]).astype(jnp.bfloat16)
    middle = grad_hidden.shape[1] // 2
    first, second = grad_hidden[:, :middle], grad_hidden[:, middle:]
    keep_ref[...] = jnp.where(core == 0, first, second)
    send_ref[...] = jnp.where(core == 0, second, first)


def squares_kernel(spread_ref, squares_ref):
    values = spread_ref[...].astype(jnp.float32)
    squares_ref[...] = jnp.full(squares_ref.shape, jnp.sum(values * values), jnp.float32)


def scale_kernel(spread_ref, squares_ref, update_ref):
    total = jnp.sum(squares_ref[...], axis=0, keepdims=True)
    entries = 16 * update_ref.shape[0] * update_ref.shape[1]
    scale = 1.0 / jnp.sqrt(total * (1.0 / entries) + 1e-06)
    scale = jnp.concatenate([scale, scale], axis=1)
    for core in range(2):
        for row in range(16):
            tile = spread_ref[16 * core + row].astype(jnp.float32)
            update_ref[8 * row : 8 * row + 8, 256 * core : 256 * core + 256] = tile * scale


VMEM = pl.BlockSpec(memory_space=pltpu.VMEM)
SMEM = pl.BlockSpec(memory_space=pltpu.SMEM)
ANYWHERE = pl.BlockSpec(memory_space=pl.ANY)


def kernel_call(body, outputs, in_specs, scratch, flops, name):
    return pl.pallas_call(
        body,
        out_shape=outputs,
        in_specs=in_specs,
        out_specs=jax.tree.map(lambda unused: VMEM, outputs),
        scratch_shapes=scratch,
        compiler_params=pltpu.CompilerParams(vmem_limit_bytes=24 * 1024 * 1024),
        cost_estimate=pl.CostEstimate(
            flops=flops, bytes_accessed=2_000_000, transcendentals=100_000
        ),
        name=name,
    )


def on_device(features, head_weight, partner):
    rows = features.shape[0]
    channels, width = head_weight.shape
    y = lax.axis_index("y2") * 4 + lax.axis_index("y1") * 2 + lax.axis_index("y0")
    core = lax.axis_index("c")
    core_scalar = core.reshape(1).astype(jnp.int32)

    hidden = jnp.dot(features, head_weight, preferred_element_type=jnp.float32)
    row_norm = jnp.sqrt(jnp.sum(hidden * hidden, axis=1, keepdims=True) + 1e-05)
    unit = (hidden / row_norm).astype(jnp.bfloat16)
    side = jnp.stack([partner.astype(jnp.float32), 1.0 / row_norm[:, 0]])

    sign = jnp.where(core == 0, -1, 1)
    same_core = lax.ppermute(unit, BITS, TO_NEXT_SAME)
    other_core = lax.ppermute(unit, BITS, TO_NEXT_OTHER)
    own = lax.ppermute(unit, BITS, TO_HOST)
    side_here = lax.ppermute(side, BITS, TO_HOST)
    pieces, places = [own], [y * 2 + core]
    for distance in range(1, 5):
        place_there = (y + sign * distance) % Y * 2
        if distance > 1:
            same_core = lax.ppermute(same_core, (*YBITS, "c"), ROUND)
        if distance == 4:
            early = kernel_call(
                early_sums_kernel,
                jax.ShapeDtypeStruct((3, 1, 512), jnp.float32),
                [VMEM] * 6,
                [pltpu.VMEM((6, rows, 128), jnp.float32), pltpu.VMEM((6, 8, rows), jnp.float32)],
                2_000_000_000,
                "early_sums",
            )(*pieces[:6])
            same_core, side_here, early = lax.optimization_barrier((same_core, side_here, early))
        pieces.append(same_core)
        places.append(place_there + core)
        if distance == 4:
            break
        if distance == 3:
            later, unused = lax.optimization_barrier((features, same_core))
            rows_here = lax.ppermute(later, BITS, TO_HOST)
        if distance > 1:
            other_core = lax.ppermute(other_core, (*YBITS, "c"), ROUND)
        pieces.append(other_core)
        places.append(place_there + 1 - core)
    sign, core_there = -sign, 1 - core
    places.append(y * 2 + core_there)
    for distance in range(1, 5):
        place_there = (y + sign * distance) % Y * 2
        there = [place_there + core_there, place_there + 1 - core_there]
        places += there[: 1 if distance == 4 else 2]
    mine = jnp.concatenate(pieces)
    starts = jnp.stack(places).astype(jnp.int32) * rows

    sibling = lax.ppermute(mine, "c", OTHER_CORE)
    held = [pltpu.VMEM(mine.shape, jnp.bfloat16)] * 2
    semaphores = pltpu.SemaphoreType.DMA((8,))
    sums = kernel_call(
        pair_sums_kernel,
        jax.ShapeDtypeStruct((8, 1, 512), jnp.float32),
        [SMEM, ANYWHERE, ANYWHERE, VMEM],
        held
        + [
            pltpu.VMEM((2, 512, 128), jnp.float32),
            pltpu.VMEM((4, 8, 512), jnp.float32),
            semaphores,
        ],
        3_000_000_000,
        "pair_sums",
    )(core_scalar, mine, sibling, early)
    sums = lax.psum(sums, "c")
    piece = jax.ShapeDtypeStruct((rows, width // 2), jnp.bfloat16)
    kept, sent = kernel_call(
        weight_kernel,
        (piece, piece),
        [SMEM, SMEM, VMEM, VMEM, VMEM, VMEM],
        [pltpu.VMEM((2, 2 * rows, 8 * rows), jnp.bfloat16)],
        2_000_000_000,
        "weights",
    )(core_scalar, starts, side_here.T, sums, mine, sibling)
    def contract(left, right):
        return lax.dot_general(
            left, right, (((0,), (0,)), ((), ())), preferred_element_type=jnp.float32
        )

    theirs = contract(rows_here, sent).astype(jnp.bfloat16)
    arrived = lax.ppermute(theirs, "c", OTHER_CORE)
    partial = (contract(rows_here, kept) + arrived.astype(jnp.float32)).astype(jnp.bfloat16)
    tiles = partial.reshape(4, 2, 2, 2, 4, 2, 8, 256)
    tiles = tiles.transpose(5, 3, 1, 2, 0, 4, 6, 7).reshape(16, 16 * 8, 256)
    received = lax.all_to_all(tiles, ("z0", "xl", "y0", "xh"), 0, 0)
    near_sum = received.astype(jnp.float32).sum(0).astype(jnp.bfloat16).reshape(16, 8, 256)
    received = lax.all_to_all(near_sum, ("y2", "y1", "z2", "z1"), 0, 0)
    fragment = received.astype(jnp.float32).sum(0).astype(jnp.bfloat16)
    spread = lax.all_to_all(
        jnp.broadcast_to(fragment[None], (32, 8, 256)), ("c", "xl", "z2", "z1", "z0"), 0, 0
    )
    squares = kernel_call(
        squares_kernel, jax.ShapeDtypeStruct((16, 128), jnp.float32), [VMEM], [], 100_000, "squares"
    )(spread)
    squares = lax.all_to_all(squares, ("y2", "y1", "y0", "xh"), 0, 0)
    return kernel_call(
        scale_kernel,
        jax.ShapeDtypeStruct((channels // 16, width), jnp.float32),
        [VMEM, VMEM],
        [],
        100_000,
        "scale",
    )(spread, squares)


def solution(mesh):
    bits = Mesh(mesh.devices.reshape((2,) * len(BITS)), BITS)
    images = P(("xl", "z2", "z1", "z0", "c", "y2", "y1", "y0", "xh"))
    return jax.shard_map(
        on_device,
        mesh=bits,
        in_specs=(P(*images, None), P(), images),
        out_specs=P(("y2", "y1", "y0", "xh"), None),
        check_vma=False,
    )
```

```python
import itertools

import jax
import jax.numpy as jnp
from jax import lax
from jax.experimental import pallas as pl
from jax.experimental.pallas import tpu as pltpu
from jax.sharding import Mesh
from jax.sharding import PartitionSpec as P

softness_factor = 0.05
EXP2_SCALE = 1.4426950408889634 / softness_factor
Y = 8
BITS = ("y2", "y1", "y0", "xh", "xl", "z2", "z1", "z0", "c")
YBITS = BITS[:3]
OTHER_CORE = [(0, 1), (1, 0)]


def moves(other_core, step):
    pairs = []
    for y, xh, xl, z, core in itertools.product(range(Y), range(2), range(2), range(8), range(2)):
        there = xh ^ other_core
        y_there = (y + step * (1, -1)[there]) % Y
        pairs.append((place(y, xh, xl, z, core), place(y_there, core ^ xl, 1 - xl, z, there)))
    return pairs


def place(y, xh, xl, z, core):
    return (((y * 2 + xh) * 2 + xl) * 8 + z) * 2 + core


TO_HOST = moves(0, 0)
TO_NEXT_SAME, TO_NEXT_OTHER = moves(0, 1), moves(1, 1)
ROUND = [(2 * y + c, 2 * ((y + (1, -1)[c]) % Y) + c) for y in range(Y) for c in range(2)]


def exponentials(left, right):
    scores = lax.dot_general(
        left, right, (((1,), (1,)), ((), ())), preferred_element_type=jnp.float32
    )
    return jnp.exp2(scores * EXP2_SCALE)


def over_rows(values):
    return values.reshape(values.shape[0] // 8, 8, values.shape[1]).sum(0)


def over_lane_groups(values):
    return sum(values[:, k : k + 128] for k in range(0, values.shape[1], 128))


def row_totals(per_lane):
    ones = jnp.ones((8, per_lane.shape[1]), jnp.float32)
    totals = lax.dot_general(
        ones,
        per_lane,
        (((1,), (1,)), ((), ())),
        precision=lax.Precision.HIGHEST,
        preferred_element_type=jnp.float32,
    )
    return totals[0:1, :]


def without_self(values):
    rows = lax.broadcasted_iota(jnp.int32, values.shape, 0)
    columns = lax.broadcasted_iota(jnp.int32, values.shape, 1)
    return jnp.where(rows == columns, 0.0, values)


def early_sums_kernel(*refs):
    pieces, (sums_ref, per_lane, per_column) = refs[:-3], refs[-3:]
    rows = per_lane.shape[1]
    per_lane[...] = jnp.zeros_like(per_lane)
    for i, piece in enumerate(pieces):
        left = piece[...]
        own = over_rows(without_self(exponentials(left, left)))
        per_column[i] = own if i == 0 else per_column[i] + own
        for j in range(i + 1, len(pieces)):
            values = exponentials(left, pieces[j][...])
            column = over_rows(values)
            per_column[j] = column if i == 0 else per_column[j] + column
            per_lane[i] += over_lane_groups(values)
    for i in range(len(pieces)):
        total = per_column[i].sum(0, keepdims=True) + row_totals(per_lane[i])
        sums_ref[i // 2, :, i % 2 * rows : (i % 2 + 1) * rows] = total


def block_copies(source, target, semaphores, order, first):
    rows = target.shape[0] // len(order)
    copies = {}
    for position, k in enumerate(order):
        part = pl.ds(k * rows, rows)
        copies[k] = pltpu.make_async_copy(
            source.at[part], target.at[part], semaphores.at[first + position]
        )
        copies[k].start()
    return copies


def pair_sums_kernel(
    core_ref, mine_hbm, sibling_hbm, early_ref, sums_ref, mine, sibling, per_lane, per_column, semaphores
):
    core = core_ref[0]
    blocks, wide = per_column.shape[0], per_column.shape[2]
    half = blocks // 2
    mine_copies = block_copies(mine_hbm, mine, semaphores, (3, 0, 1, 2), 0)
    sibling_copies = block_copies(sibling_hbm, sibling, semaphores, (2, 3, 0, 1), blocks)
    per_lane[...] = jnp.zeros_like(per_lane)
    per_column[...] = jnp.zeros_like(per_column)

    def block(ref, k):
        return ref[k * wide : (k + 1) * wide, :]

    mine_copies[blocks - 1].wait()
    last = block(mine, blocks - 1)
    column = over_rows(without_self(exponentials(last, last)))
    same = []
    for i in range(blocks - 1):
        mine_copies[i].wait()
        values = exponentials(block(mine, i), last)
        column += over_rows(values)
        same.append(early_ref[i] + row_totals(over_lane_groups(values)))
    same.append(column.sum(0, keepdims=True))

    def pairs(left_ref, first, right_ref, columns):
        for i in range(half):
            left = block(left_ref, first + i)
            for j in columns:
                values = exponentials(left, block(right_ref, j))
                per_column[j] += over_rows(values)
                per_lane[i] += over_lane_groups(values)

    sibling_copies[2].wait()
    sibling_copies[3].wait()

    @pl.when(core == 0)
    def _():
        pairs(mine, 0, sibling, (2, 3))

    @pl.when(core == 1)
    def _():
        pairs(sibling, half, mine, (0, 1))

    sibling_copies[0].wait()
    sibling_copies[1].wait()

    @pl.when(core == 0)
    def _():
        pairs(mine, 0, sibling, (0, 1))

    @pl.when(core == 1)
    def _():
        pairs(sibling, half, mine, (2, 3))

    for k in range(blocks):
        sums_ref[k] = jnp.zeros_like(sums_ref[k])
        sums_ref[blocks + k] = per_column[k].sum(0, keepdims=True)
    for i in range(half):
        sums_ref[half * core + i] = row_totals(per_lane[i])
    for k in range(blocks):
        sums_ref[blocks * core + k] += same[k]


def weight_kernel(
    core_ref,
    start_ref,
    side_ref,
    sums_ref,
    mine_ref,
    sibling_ref,
    keep_ref,
    send_ref,
    weights,
):
    core = core_ref[0]
    wide = sums_ref.shape[2]
    blocks = sums_ref.shape[0] // 2
    rows = side_ref.shape[0]
    own = mine_ref[:rows, :]
    mine_sums = sums_ref[blocks * core][:, :rows]
    inverse_own = 1.0 / jnp.broadcast_to(mine_sums, (128, rows)).T[:, :1]
    partner = side_ref[:, 0:1].astype(jnp.int32)
    lanes = lax.broadcasted_iota(jnp.int32, (1, wide), 1)
    for part, ref in enumerate((mine_ref, sibling_ref)):
        for k in range(blocks):
            which = core if part == 0 else 1 - core
            right = ref[k * wide : (k + 1) * wide, :]
            inverse = 1.0 / sums_ref[blocks * which + k]
            values = exponentials(own, right)
            if part == 0 and k == 0:
                values = without_self(values)
            first = start_ref[part * blocks * 2 + 2 * k]
            second = start_ref[part * blocks * 2 + 2 * k + 1]
            columns = lanes + jnp.where(lanes < rows, first, second - rows)
            target = jnp.where(columns == partner, 1.0, 0.0)
            place_here = slice(k * wide, (k + 1) * wide)
            weights[part, :rows, place_here] = (values * inverse_own - target).astype(jnp.bfloat16)
            weights[part, rows:, place_here] = (values * inverse - target).astype(jnp.bfloat16)
    total = jnp.dot(weights[0], mine_ref[...], preferred_element_type=jnp.float32)
    total += jnp.dot(weights[1], sibling_ref[...], preferred_element_type=jnp.float32)
    grad_unit = (total[:rows] + total[rows:]) * (1.0 / softness_factor)
    unit = own.astype(jnp.float32)
    along = jnp.sum(unit * grad_unit, axis=1, keepdims=True)
    grad_hidden = ((grad_unit - unit * along) * side_ref[:, 1:2]).astype(jnp.bfloat16)
    middle = grad_hidden.shape[1] // 2
    first, second = grad_hidden[:, :middle], grad_hidden[:, middle:]
    keep_ref[...] = jnp.where(core == 0, first, second)
    send_ref[...] = jnp.where(core == 0, second, first)


def unit_kernel(features_ref, weight_ref, unit_ref, inverse_ref, hidden):
    step = pl.program_id(0)
    product = jnp.dot(features_ref[...], weight_ref[...], preferred_element_type=jnp.float32)

    @pl.when(step == 0)
    def _():
        hidden[...] = product

    @pl.when(step > 0)
    def _():
        hidden[...] += product

    @pl.when(step == pl.num_programs(0) - 1)
    def _():
        squares = hidden[...] * hidden[...]
        inverse = 1.0 / jnp.sqrt(jnp.sum(squares, axis=1, keepdims=True) + 1e-05)
        unit_ref[...] = (hidden[...] * inverse).astype(jnp.bfloat16)
        inverse_ref[...] = jnp.broadcast_to(inverse, (inverse.shape[0], 128)).T[0:1, :]


def units(features, head_weight):
    rows, channels = features.shape
    width = head_weight.shape[1]
    deep = channels // 4
    return pl.pallas_call(
        unit_kernel,
        grid=(4,),
        out_shape=(
            jax.ShapeDtypeStruct((rows, width), jnp.bfloat16),
            jax.ShapeDtypeStruct((1, rows), jnp.float32),
        ),
        in_specs=[
            pl.BlockSpec((rows, deep), lambda k: (0, k)),
            pl.BlockSpec((deep, width), lambda k: (k, 0)),
        ],
        out_specs=(
            pl.BlockSpec((rows, width), lambda k: (0, 0)),
            pl.BlockSpec((1, rows), lambda k: (0, 0)),
        ),
        scratch_shapes=[pltpu.VMEM((rows, width), jnp.float32)],
        compiler_params=pltpu.CompilerParams(vmem_limit_bytes=60 * 1024 * 1024),
        cost_estimate=pl.CostEstimate(
            flops=2 * rows * channels * width, bytes_accessed=3_000_000, transcendentals=0
        ),
        name="units",
    )(features, head_weight)


def squares_kernel(spread_ref, squares_ref):
    values = spread_ref[...].astype(jnp.float32)
    squares_ref[...] = jnp.full(squares_ref.shape, jnp.sum(values * values), jnp.float32)


def scale_kernel(spread_ref, squares_ref, update_ref):
    total = jnp.sum(squares_ref[...], axis=0, keepdims=True)
    entries = 16 * update_ref.shape[0] * update_ref.shape[1]
    scale = 1.0 / jnp.sqrt(total * (1.0 / entries) + 1e-06)
    scale = jnp.concatenate([scale, scale], axis=1)
    for core in range(2):
        for row in range(16):
            tile = spread_ref[16 * core + row].astype(jnp.float32)
            update_ref[8 * row : 8 * row + 8, 256 * core : 256 * core + 256] = tile * scale


VMEM = pl.BlockSpec(memory_space=pltpu.VMEM)
SMEM = pl.BlockSpec(memory_space=pltpu.SMEM)
ANYWHERE = pl.BlockSpec(memory_space=pl.ANY)


def kernel_call(body, outputs, in_specs, scratch, flops, name):
    return pl.pallas_call(
        body,
        out_shape=outputs,
        in_specs=in_specs,
        out_specs=jax.tree.map(lambda unused: VMEM, outputs),
        scratch_shapes=scratch,
        compiler_params=pltpu.CompilerParams(vmem_limit_bytes=24 * 1024 * 1024),
        cost_estimate=pl.CostEstimate(
            flops=flops, bytes_accessed=2_000_000, transcendentals=100_000
        ),
        name=name,
    )


def on_device(features, head_weight, partner):
    rows = features.shape[0]
    channels, width = head_weight.shape
    y = lax.axis_index("y2") * 4 + lax.axis_index("y1") * 2 + lax.axis_index("y0")
    core = lax.axis_index("c")
    core_scalar = core.reshape(1).astype(jnp.int32)

    unit, inverse_norm = units(features, head_weight)
    side = jnp.concatenate([partner.astype(jnp.float32)[None], inverse_norm])

    sign = jnp.where(core == 0, -1, 1)
    same_core = lax.ppermute(unit, BITS, TO_NEXT_SAME)
    other_core = lax.ppermute(unit, BITS, TO_NEXT_OTHER)
    own = lax.ppermute(unit, BITS, TO_HOST)
    side_here = lax.ppermute(side, BITS, TO_HOST)
    pieces, places = [own], [y * 2 + core]
    for distance in range(1, 5):
        place_there = (y + sign * distance) % Y * 2
        if distance > 1:
            same_core = lax.ppermute(same_core, (*YBITS, "c"), ROUND)
        if distance == 4:
            early = kernel_call(
                early_sums_kernel,
                jax.ShapeDtypeStruct((3, 1, 512), jnp.float32),
                [VMEM] * 6,
                [pltpu.VMEM((6, rows, 128), jnp.float32), pltpu.VMEM((6, 8, rows), jnp.float32)],
                2_000_000_000,
                "early_sums",
            )(*pieces[:6])
            same_core, side_here, early = lax.optimization_barrier((same_core, side_here, early))
        pieces.append(same_core)
        places.append(place_there + core)
        if distance == 4:
            break
        if distance == 3:
            later, unused = lax.optimization_barrier((features, same_core))
            rows_here = lax.ppermute(later, BITS, TO_HOST)
        if distance > 1:
            other_core = lax.ppermute(other_core, (*YBITS, "c"), ROUND)
        pieces.append(other_core)
        places.append(place_there + 1 - core)
    sign, core_there = -sign, 1 - core
    places.append(y * 2 + core_there)
    for distance in range(1, 5):
        place_there = (y + sign * distance) % Y * 2
        there = [place_there + core_there, place_there + 1 - core_there]
        places += there[: 1 if distance == 4 else 2]
    mine = jnp.concatenate(pieces)
    starts = jnp.stack(places).astype(jnp.int32) * rows

    sibling = lax.ppermute(mine, "c", OTHER_CORE)
    held = [pltpu.VMEM(mine.shape, jnp.bfloat16)] * 2
    semaphores = pltpu.SemaphoreType.DMA((8,))
    sums = kernel_call(
        pair_sums_kernel,
        jax.ShapeDtypeStruct((8, 1, 512), jnp.float32),
        [SMEM, ANYWHERE, ANYWHERE, VMEM],
        held
        + [
            pltpu.VMEM((2, 512, 128), jnp.float32),
            pltpu.VMEM((4, 8, 512), jnp.float32),
            semaphores,
        ],
        3_000_000_000,
        "pair_sums",
    )(core_scalar, mine, sibling, early)
    sums = lax.psum(sums, "c")
    piece = jax.ShapeDtypeStruct((rows, width // 2), jnp.bfloat16)
    kept, sent = kernel_call(
        weight_kernel,
        (piece, piece),
        [SMEM, SMEM, VMEM, VMEM, VMEM, VMEM],
        [pltpu.VMEM((2, 2 * rows, 8 * rows), jnp.bfloat16)],
        2_000_000_000,
        "weights",
    )(core_scalar, starts, side_here.T, sums, mine, sibling)
    def contract(left, right):
        return lax.dot_general(
            left, right, (((0,), (0,)), ((), ())), preferred_element_type=jnp.float32
        )

    theirs = contract(rows_here, sent).astype(jnp.bfloat16)
    arrived = lax.ppermute(theirs, "c", OTHER_CORE)
    ours, arrived = lax.optimization_barrier((contract(rows_here, kept), arrived))
    partial = (ours + arrived.astype(jnp.float32)).astype(jnp.bfloat16)
    tiles = partial.reshape(4, 2, 2, 2, 4, 2, 8, 256)
    tiles = tiles.transpose(5, 3, 1, 2, 0, 4, 6, 7).reshape(16, 16 * 8, 256)
    received = lax.all_to_all(tiles, ("z0", "xl", "y0", "xh"), 0, 0)
    near_sum = received.astype(jnp.float32).sum(0).astype(jnp.bfloat16).reshape(16, 8, 256)
    received = lax.all_to_all(near_sum, ("y2", "y1", "z2", "z1"), 0, 0)
    fragment = received.astype(jnp.float32).sum(0).astype(jnp.bfloat16)
    spread = lax.all_to_all(
        jnp.broadcast_to(fragment[None], (32, 8, 256)), ("c", "xl", "z2", "z1", "z0"), 0, 0
    )
    squares = kernel_call(
        squares_kernel, jax.ShapeDtypeStruct((16, 128), jnp.float32), [VMEM], [], 100_000, "squares"
    )(spread)
    squares = lax.all_to_all(squares, ("y2", "y1", "y0", "xh"), 0, 0)
    return kernel_call(
        scale_kernel,
        jax.ShapeDtypeStruct((channels // 16, width), jnp.float32),
        [VMEM, VMEM],
        [],
        100_000,
        "scale",
    )(spread, squares)


def solution(mesh):
    bits = Mesh(mesh.devices.reshape((2,) * len(BITS)), BITS)
    images = P(("xl", "z2", "z1", "z0", "c", "y2", "y1", "y0", "xh"))
    return jax.shard_map(
        on_device,
        mesh=bits,
        in_specs=(P(*images, None), P(), images),
        out_specs=P(("y2", "y1", "y0", "xh"), None),
        check_vma=False,
    )
```

```python
import itertools

import jax
import jax.numpy as jnp
from jax import lax
from jax.experimental import pallas as pl
from jax.experimental.pallas import tpu as pltpu
from jax.sharding import Mesh
from jax.sharding import PartitionSpec as P

softness_factor = 0.05
EXP2_SCALE = 1.4426950408889634 / softness_factor
Y = 8
BITS = ("y2", "y1", "y0", "xh", "xl", "z2", "z1", "z0", "c")
YBITS = BITS[:3]
OTHER_CORE = [(0, 1), (1, 0)]


def moves(other_core, step):
    pairs = []
    for y, xh, xl, z, core in itertools.product(range(Y), range(2), range(2), range(8), range(2)):
        there = xh ^ other_core
        y_there = (y + step * (1, -1)[there]) % Y
        pairs.append((place(y, xh, xl, z, core), place(y_there, core ^ xl, 1 - xl, z, there)))
    return pairs


def place(y, xh, xl, z, core):
    return (((y * 2 + xh) * 2 + xl) * 8 + z) * 2 + core


TO_HOST = moves(0, 0)
TO_NEXT_SAME, TO_NEXT_OTHER = moves(0, 1), moves(1, 1)
ROUND = [(2 * y + c, 2 * ((y + (1, -1)[c]) % Y) + c) for y in range(Y) for c in range(2)]


def exponentials(left, right):
    scores = lax.dot_general(
        left, right, (((1,), (1,)), ((), ())), preferred_element_type=jnp.float32
    )
    return jnp.exp2(scores * EXP2_SCALE)


def over_rows(values):
    return values.reshape(values.shape[0] // 8, 8, values.shape[1]).sum(0)


def over_lane_groups(values):
    return sum(values[:, k : k + 128] for k in range(0, values.shape[1], 128))


def row_totals(per_lane):
    ones = jnp.ones((8, per_lane.shape[1]), jnp.float32)
    totals = lax.dot_general(
        ones,
        per_lane,
        (((1,), (1,)), ((), ())),
        precision=lax.Precision.HIGHEST,
        preferred_element_type=jnp.float32,
    )
    return totals[0:1, :]


def without_self(values):
    rows = lax.broadcasted_iota(jnp.int32, values.shape, 0)
    columns = lax.broadcasted_iota(jnp.int32, values.shape, 1)
    return jnp.where(rows == columns, 0.0, values)


def early_sums_kernel(*refs):
    pieces, (sums_ref, per_lane, per_column) = refs[:-3], refs[-3:]
    rows = per_lane.shape[1]
    per_lane[...] = jnp.zeros_like(per_lane)
    for i, piece in enumerate(pieces):
        left = piece[...]
        own = over_rows(without_self(exponentials(left, left)))
        per_column[i] = own if i == 0 else per_column[i] + own
        for j in range(i + 1, len(pieces)):
            values = exponentials(left, pieces[j][...])
            column = over_rows(values)
            per_column[j] = column if i == 0 else per_column[j] + column
            per_lane[i] += over_lane_groups(values)
    for i in range(len(pieces)):
        total = per_column[i].sum(0, keepdims=True) + row_totals(per_lane[i])
        sums_ref[i // 2, :, i % 2 * rows : (i % 2 + 1) * rows] = total


def block_copies(source, target, semaphores, order, first):
    rows = target.shape[0] // len(order)
    copies = {}
    for position, k in enumerate(order):
        part = pl.ds(k * rows, rows)
        copies[k] = pltpu.make_async_copy(
            source.at[part], target.at[part], semaphores.at[first + position]
        )
        copies[k].start()
    return copies


def pair_sums_kernel(
    core_ref, mine_hbm, sibling_hbm, early_ref, sums_ref, mine, sibling, per_lane, per_column, semaphores
):
    core = core_ref[0]
    blocks, wide = per_column.shape[0], per_column.shape[2]
    half = blocks // 2
    mine_copies = block_copies(mine_hbm, mine, semaphores, (3, 0, 1, 2), 0)
    sibling_copies = block_copies(sibling_hbm, sibling, semaphores, (2, 3, 0, 1), blocks)
    per_lane[...] = jnp.zeros_like(per_lane)
    per_column[...] = jnp.zeros_like(per_column)

    def block(ref, k):
        return ref[k * wide : (k + 1) * wide, :]

    mine_copies[blocks - 1].wait()
    last = block(mine, blocks - 1)
    column = over_rows(without_self(exponentials(last, last)))
    same = []
    for i in range(blocks - 1):
        mine_copies[i].wait()
        values = exponentials(block(mine, i), last)
        column += over_rows(values)
        same.append(early_ref[i] + row_totals(over_lane_groups(values)))
    same.append(column.sum(0, keepdims=True))

    def pairs(left_ref, first, right_ref, columns):
        for i in range(half):
            left = block(left_ref, first + i)
            for j in columns:
                values = exponentials(left, block(right_ref, j))
                per_column[j] += over_rows(values)
                per_lane[i] += over_lane_groups(values)

    sibling_copies[2].wait()
    sibling_copies[3].wait()

    @pl.when(core == 0)
    def _():
        pairs(mine, 0, sibling, (2, 3))

    @pl.when(core == 1)
    def _():
        pairs(sibling, half, mine, (0, 1))

    sibling_copies[0].wait()
    sibling_copies[1].wait()

    @pl.when(core == 0)
    def _():
        pairs(mine, 0, sibling, (0, 1))

    @pl.when(core == 1)
    def _():
        pairs(sibling, half, mine, (2, 3))

    for k in range(blocks):
        sums_ref[k] = jnp.zeros_like(sums_ref[k])
        sums_ref[blocks + k] = per_column[k].sum(0, keepdims=True)
    for i in range(half):
        sums_ref[half * core + i] = row_totals(per_lane[i])
    for k in range(blocks):
        sums_ref[blocks * core + k] += same[k]


def weight_kernel(
    core_ref,
    start_ref,
    side_ref,
    sums_ref,
    mine_ref,
    sibling_ref,
    keep_ref,
    send_ref,
    weights,
):
    core = core_ref[0]
    wide = sums_ref.shape[2]
    blocks = sums_ref.shape[0] // 2
    rows = side_ref.shape[0]
    own = mine_ref[:rows, :]
    mine_sums = sums_ref[blocks * core][:, :rows]
    inverse_own = 1.0 / jnp.broadcast_to(mine_sums, (128, rows)).T[:, :1]
    partner = side_ref[:, 0:1].astype(jnp.int32)
    lanes = lax.broadcasted_iota(jnp.int32, (1, wide), 1)
    for part, ref in enumerate((mine_ref, sibling_ref)):
        for k in range(blocks):
            which = core if part == 0 else 1 - core
            right = ref[k * wide : (k + 1) * wide, :]
            inverse = 1.0 / sums_ref[blocks * which + k]
            values = exponentials(own, right)
            if part == 0 and k == 0:
                values = without_self(values)
            first = start_ref[part * blocks * 2 + 2 * k]
            second = start_ref[part * blocks * 2 + 2 * k + 1]
            columns = lanes + jnp.where(lanes < rows, first, second - rows)
            target = jnp.where(columns == partner, 1.0, 0.0)
            place_here = slice(k * wide, (k + 1) * wide)
            weights[part, :rows, place_here] = (values * inverse_own - target).astype(jnp.bfloat16)
            weights[part, rows:, place_here] = (values * inverse - target).astype(jnp.bfloat16)
    total = jnp.dot(weights[0], mine_ref[...], preferred_element_type=jnp.float32)
    total += jnp.dot(weights[1], sibling_ref[...], preferred_element_type=jnp.float32)
    grad_unit = (total[:rows] + total[rows:]) * (1.0 / softness_factor)
    unit = own.astype(jnp.float32)
    along = jnp.sum(unit * grad_unit, axis=1, keepdims=True)
    grad_hidden = ((grad_unit - unit * along) * side_ref[:, 1:2]).astype(jnp.bfloat16)
    middle = grad_hidden.shape[1] // 2
    first, second = grad_hidden[:, :middle], grad_hidden[:, middle:]
    keep_ref[...] = jnp.where(core == 0, first, second)
    send_ref[...] = jnp.where(core == 0, second, first)


def unit_kernel(features_ref, weight_ref, unit_ref, inverse_ref, hidden):
    step = pl.program_id(0)
    product = jnp.dot(features_ref[...], weight_ref[...], preferred_element_type=jnp.float32)

    @pl.when(step == 0)
    def _():
        hidden[...] = product

    @pl.when(step > 0)
    def _():
        hidden[...] += product

    @pl.when(step == pl.num_programs(0) - 1)
    def _():
        squares = hidden[...] * hidden[...]
        inverse = 1.0 / jnp.sqrt(jnp.sum(squares, axis=1, keepdims=True) + 1e-05)
        unit_ref[...] = (hidden[...] * inverse).astype(jnp.bfloat16)
        inverse_ref[...] = jnp.broadcast_to(inverse, (inverse.shape[0], 128)).T[0:1, :]


def units(features, head_weight):
    rows, channels = features.shape
    width = head_weight.shape[1]
    deep = channels // 4
    return pl.pallas_call(
        unit_kernel,
        grid=(4,),
        out_shape=(
            jax.ShapeDtypeStruct((rows, width), jnp.bfloat16),
            jax.ShapeDtypeStruct((1, rows), jnp.float32),
        ),
        in_specs=[
            pl.BlockSpec((rows, deep), lambda k: (0, k)),
            pl.BlockSpec((deep, width), lambda k: (k, 0)),
        ],
        out_specs=(
            pl.BlockSpec((rows, width), lambda k: (0, 0)),
            pl.BlockSpec((1, rows), lambda k: (0, 0)),
        ),
        scratch_shapes=[pltpu.VMEM((rows, width), jnp.float32)],
        compiler_params=pltpu.CompilerParams(vmem_limit_bytes=60 * 1024 * 1024),
        cost_estimate=pl.CostEstimate(
            flops=2 * rows * channels * width, bytes_accessed=3_000_000, transcendentals=0
        ),
        name="units",
    )(features, head_weight)


def squares_kernel(spread_ref, squares_ref):
    values = spread_ref[...].astype(jnp.float32)
    squares_ref[...] = jnp.full(squares_ref.shape, jnp.sum(values * values), jnp.float32)


def scale_kernel(spread_ref, squares_ref, update_ref):
    total = jnp.sum(squares_ref[...], axis=0, keepdims=True)
    entries = 16 * update_ref.shape[0] * update_ref.shape[1]
    scale = 1.0 / jnp.sqrt(total * (1.0 / entries) + 1e-06)
    scale = jnp.concatenate([scale, scale], axis=1)
    for core in range(2):
        for row in range(16):
            tile = spread_ref[16 * core + row].astype(jnp.float32)
            update_ref[8 * row : 8 * row + 8, 256 * core : 256 * core + 256] = tile * scale


VMEM = pl.BlockSpec(memory_space=pltpu.VMEM)
SMEM = pl.BlockSpec(memory_space=pltpu.SMEM)
ANYWHERE = pl.BlockSpec(memory_space=pl.ANY)


def kernel_call(body, outputs, in_specs, scratch, flops, name):
    return pl.pallas_call(
        body,
        out_shape=outputs,
        in_specs=in_specs,
        out_specs=jax.tree.map(lambda unused: VMEM, outputs),
        scratch_shapes=scratch,
        compiler_params=pltpu.CompilerParams(vmem_limit_bytes=16 * 1024 * 1024),
        cost_estimate=pl.CostEstimate(
            flops=flops, bytes_accessed=2_000_000, transcendentals=100_000
        ),
        name=name,
    )


def on_device(features, head_weight, partner):
    rows = features.shape[0]
    channels, width = head_weight.shape
    y = lax.axis_index("y2") * 4 + lax.axis_index("y1") * 2 + lax.axis_index("y0")
    core = lax.axis_index("c")
    core_scalar = core.reshape(1).astype(jnp.int32)

    unit, inverse_norm = units(features, head_weight)
    side = jnp.concatenate([partner.astype(jnp.float32)[None], inverse_norm])

    sign = jnp.where(core == 0, -1, 1)
    same_core = lax.ppermute(unit, BITS, TO_NEXT_SAME)
    other_core = lax.ppermute(unit, BITS, TO_NEXT_OTHER)
    own = lax.ppermute(unit, BITS, TO_HOST)
    side_here = lax.ppermute(side, BITS, TO_HOST)
    pieces, places = [own], [y * 2 + core]
    for distance in range(1, 5):
        place_there = (y + sign * distance) % Y * 2
        if distance > 1:
            same_core = lax.ppermute(same_core, (*YBITS, "c"), ROUND)
        if distance == 4:
            early = kernel_call(
                early_sums_kernel,
                jax.ShapeDtypeStruct((3, 1, 512), jnp.float32),
                [VMEM] * 6,
                [pltpu.VMEM((6, rows, 128), jnp.float32), pltpu.VMEM((6, 8, rows), jnp.float32)],
                2_000_000_000,
                "early_sums",
            )(*pieces[:6])
            same_core, side_here, early = lax.optimization_barrier((same_core, side_here, early))
        pieces.append(same_core)
        places.append(place_there + core)
        if distance == 4:
            break
        if distance == 3:
            later, unused = lax.optimization_barrier((features, same_core))
            rows_here = lax.ppermute(later, BITS, TO_HOST)
        if distance > 1:
            other_core = lax.ppermute(other_core, (*YBITS, "c"), ROUND)
        pieces.append(other_core)
        places.append(place_there + 1 - core)
    sign, core_there = -sign, 1 - core
    places.append(y * 2 + core_there)
    for distance in range(1, 5):
        place_there = (y + sign * distance) % Y * 2
        there = [place_there + core_there, place_there + 1 - core_there]
        places += there[: 1 if distance == 4 else 2]
    mine = jnp.concatenate(pieces)
    starts = jnp.stack(places).astype(jnp.int32) * rows

    sibling = lax.ppermute(mine, "c", OTHER_CORE)
    held = [pltpu.VMEM(mine.shape, jnp.bfloat16)] * 2
    semaphores = pltpu.SemaphoreType.DMA((8,))
    sums = kernel_call(
        pair_sums_kernel,
        jax.ShapeDtypeStruct((8, 1, 512), jnp.float32),
        [SMEM, ANYWHERE, ANYWHERE, VMEM],
        held
        + [
            pltpu.VMEM((2, 512, 128), jnp.float32),
            pltpu.VMEM((4, 8, 512), jnp.float32),
            semaphores,
        ],
        3_000_000_000,
        "pair_sums",
    )(core_scalar, mine, sibling, early)
    sums = lax.psum(sums, "c")
    piece = jax.ShapeDtypeStruct((rows, width // 2), jnp.bfloat16)
    kept, sent = kernel_call(
        weight_kernel,
        (piece, piece),
        [SMEM, SMEM, VMEM, VMEM, VMEM, VMEM],
        [pltpu.VMEM((2, 2 * rows, 8 * rows), jnp.bfloat16)],
        2_000_000_000,
        "weights",
    )(core_scalar, starts, side_here.T, sums, mine, sibling)
    def contract(left, right):
        return lax.dot_general(
            left, right, (((0,), (0,)), ((), ())), preferred_element_type=jnp.float32
        )

    theirs = contract(rows_here, sent).astype(jnp.bfloat16)
    arrived = lax.ppermute(theirs, "c", OTHER_CORE)
    ours, arrived = lax.optimization_barrier((contract(rows_here, kept), arrived))
    partial = (ours + arrived.astype(jnp.float32)).astype(jnp.bfloat16)
    tiles = partial.reshape(4, 2, 2, 2, 4, 2, 8, 256)
    tiles = tiles.transpose(5, 3, 1, 2, 0, 4, 6, 7).reshape(16, 16 * 8, 256)
    received = lax.all_to_all(tiles, ("z0", "xl", "y0", "xh"), 0, 0)
    near_sum = received.astype(jnp.float32).sum(0).astype(jnp.bfloat16).reshape(16, 8, 256)
    received = lax.all_to_all(near_sum, ("y2", "y1", "z2", "z1"), 0, 0)
    fragment = received.astype(jnp.float32).sum(0).astype(jnp.bfloat16)
    spread = lax.all_to_all(
        jnp.broadcast_to(fragment[None], (32, 8, 256)), ("c", "xl", "z2", "z1", "z0"), 0, 0
    )
    squares = kernel_call(
        squares_kernel, jax.ShapeDtypeStruct((16, 128), jnp.float32), [VMEM], [], 100_000, "squares"
    )(spread)
    squares = lax.all_to_all(squares, ("y2", "y1", "y0", "xh"), 0, 0)
    return kernel_call(
        scale_kernel,
        jax.ShapeDtypeStruct((channels // 16, width), jnp.float32),
        [VMEM, VMEM],
        [],
        100_000,
        "scale",
    )(spread, squares)


def solution(mesh):
    bits = Mesh(mesh.devices.reshape((2,) * len(BITS)), BITS)
    images = P(("xl", "z2", "z1", "z0", "c", "y2", "y1", "y0", "xh"))
    return jax.shard_map(
        on_device,
        mesh=bits,
        in_specs=(P(*images, None), P(), images),
        out_specs=P(("y2", "y1", "y0", "xh"), None),
        check_vma=False,
    )
```
